32 devices in a mesh: rep: 8 (over z, core), shard: 4 (over y, x).
Axes of the slice: x: 2, y: 2, z: 4, core: 2. Of those that a mesh axis runs over, the one named last changes fastest.
Arguments:
- tokens: bfloat16 [32, 256, 1024], P(('rep', 'shard')), may hold values from -6 to 6
- cotangent: bfloat16 [32, 256, 1024], P(('rep', 'shard')), may hold values from -6 to 6
- lengths: int32 [8, 4], P('rep'), may hold values from 1 to 256, 768 in all within a row
- sequence_deal: int32 [8, 4], P('rep'), may hold values from 0 to 3, each once within a row
- routes: int32 [32, 256, 2], P(('rep', 'shard')), may hold values from 0 to 3, all different within a row
- fill_order: int32 [32, 256], P(('rep', 'shard')), may hold values from 0 to 255, each once within a row
- norm_attn: bfloat16 [1024], P('shard'), may hold values from 0.5 to 1.5
- w_query: bfloat16 [1024, 1024], P('shard'), may hold values from -0.1875 to 0.1875
- w_key: bfloat16 [1024, 1024], P('shard'), may hold values from -0.1875 to 0.1875
- w_value: bfloat16 [1024, 1024], P('shard'), may hold values from -0.1875 to 0.1875
- w_out: bfloat16 [1024, 1024], P('shard'), may hold values from -0.75 to 0.75
- rel_bias: bfloat16 [32, 16], P('shard'), may hold values from -3 to 3
- norm_ffn: bfloat16 [1024], P('shard'), may hold values from 0.5 to 1.5
- w_router: bfloat16 [1024, 4], P('shard'), may hold values from -0.1875 to 0.1875
- w_gate: bfloat16 [4, 1024, 2816], P(None, None, 'shard'), may hold values from -0.1875 to 0.1875
- w_up: bfloat16 [4, 1024, 2816], P(None, None, 'shard'), may hold values from -0.1875 to 0.1875
- w_down: bfloat16 [4, 2816, 1024], P(None, 'shard'), may hold values from -0.4375 to 0.4375
Outputs:
- output: bfloat16 [32, 256, 1024], P(('rep', 'shard'))
- grad_tokens: bfloat16 [32, 256, 1024], P(('rep', 'shard'))
- grad_norm_attn: float32 [1024], P('shard')
- grad_query: float32 [1024, 1024], P('shard')
- grad_key: float32 [1024, 1024], P('shard')
- grad_value: float32 [1024, 1024], P('shard')
- grad_out: float32 [1024, 1024], P('shard')
- grad_bias: float32 [32, 16], P('shard')
- grad_norm_ffn: float32 [1024], P('shard')
- grad_router: float32 [1024, 4], P('shard')
- grad_gate: float32 [4, 1024, 2816], P(None, None, 'shard')
- grad_up: float32 [4, 1024, 2816], P(None, None, 'shard')
- grad_down: float32 [4, 2816, 1024], P(None, 'shard')
The draws below stay inside these ranges and needn't reach their ends.
Inputs may be any that keep to these rules, and one draw needn't show every extreme that they name: Each row holds the lengths of the 4 sequences of a replica group; they sum to 768 and the largest is 256; positions at or past a length are padding. `sequence_deal`: each row is a permutation of 0 to 3. `routes`: a token's two experts differ; every expert is named somewhere. `fill_order`: each row is a permutation of 0 to 255.
All inputs are finite; a program needn't handle non-finite values.
Results may differ from the reference program's by a relative error of at most 0.022.
Values may be sent and summed in bfloat16 or wider, within the bound.
No kernel may reach another device: no remote copies, remote signals or barrier semaphores. Data moves between devices by JAX's collectives and lax.ppermute only.
A program may use at most 448 MiB of HBM per device.

```python
import math
import jax
import jax.numpy as jnp
import numpy as np
from jax import lax

D = 1024
HEADS = 16
HEAD_DIM = 64
FF = 2816
EXPERTS = 4
BUCKETS = 32
SLOT = 256
CAP = 144
SEQS = 32
N_REP = 8
N_SHARD = 4


def level_of(key, dims, split, low, top_value):
    def one(dim, blocks):
        draws = jax.random.uniform(jax.random.fold_in(jax.random.fold_in(key, 6), dim), (blocks,), jnp.float32, low / len(split), top_value / len(split))
        return jnp.repeat(jnp.exp(draws), dims[dim] // blocks).reshape((-1,) + (1,) * (len(dims) - dim - 1))

    gain = one(*split[0])
    for cut in split[1:]:
        gain = gain * one(*cut)
    return gain


def different_ones(stream_key, rows, amount, top, lift):
    ranking = jax.random.permutation(jax.random.fold_in(stream_key, 1), amount)
    pull = ranking
    for power in range(3):
        pull = pull * pull // amount
    pull = pull * lift // amount
    tickets = jax.random.randint(jax.random.fold_in(stream_key, 2), (rows, amount), 0, 4096) + pull
    sure = jax.random.permutation(jax.random.fold_in(stream_key, 3), rows)[jnp.arange(amount) % rows]
    tickets = jnp.where(jnp.arange(rows)[:, None] == sure[None, :], 1 << 14, tickets)
    merit = tickets * amount + jnp.arange(amount)
    return lax.top_k(merit.astype(jnp.int32), top)[1].astype(jnp.int32)


def profile(count, total, most, skew):
    loads = [(1 << 20) // math.isqrt(standing ** skew) + 1 for standing in range(2, count + 1)]
    rest, given = total - most - (count - 1), [1] * (count - 1)
    while rest > 0:
        candidates = [i for i in range(count - 1) if given[i] < most]
        mass, left = sum([loads[i] for i in candidates]), rest
        for i in candidates:
            addition = min(most - given[i], max(1, left * loads[i] // mass), rest)
            given[i] = given[i] + addition
            rest = rest - addition
    return np.array([most] + given)


def ragged_sizes(rng, number_of, total, limit, slope):
    if number_of == 2:
        one = jax.random.randint(rng, (), max(1, total - limit), min(limit, total - 1) + 1)
        return jnp.stack([one, total - one])
    sizes = jnp.asarray(profile(number_of, total, limit, slope), jnp.int32)
    twos = (number_of - 1) // 2
    donor, receiver = sizes[1:1 + 2 * twos:2], sizes[2:2 + 2 * twos:2]
    margin = jnp.minimum(donor - 1, limit - receiver)
    passed = jax.random.randint(jax.random.fold_in(rng, 1), (twos,), 0, 1 << 20) % (margin + 1)
    sizes = sizes.at[1:1 + 2 * twos:2].set(donor - passed).at[2:2 + 2 * twos:2].set(receiver + passed)
    return sizes[jax.random.permutation(jax.random.fold_in(rng, 2), number_of)]


def gaussian(rng, extent, deviation, reach, split=(), kind=jnp.bfloat16):
    array = jax.random.normal(rng, extent, jnp.float32) * deviation
    if len(split) > 0:
        array = level_of(rng, extent, split, -0.22, 0.18) * array
    return jnp.clip(array, min=-reach, max=reach).astype(kind)


def setup_inputs(seed: int = 0) -> dict:
    key_list = jax.random.split(jax.random.key(seed), 18)
    tokens = gaussian(key_list[0], (SEQS, SLOT, D), 1.0, 6.0, ((0, 32),))
    cotangent = gaussian(key_list[1], (SEQS, SLOT, D), 1.0, 6.0, ((0, 32),))
    lengths = jax.vmap(lambda own: ragged_sizes(own, N_SHARD, N_SHARD * SLOT * 3 // 4, SLOT, 2))(jax.random.split(key_list[2], N_REP)).reshape((N_REP, N_SHARD)).astype(jnp.int32)
    sequence_deal = jax.vmap(lambda own: jax.random.permutation(own, N_SHARD))(jax.random.split(key_list[3], N_REP)).reshape((N_REP, N_SHARD)).astype(jnp.int32)
    routes = different_ones(key_list[4], SEQS * SLOT, EXPERTS, 2, 4096).reshape((SEQS, SLOT, 2))
    fill_order = jax.vmap(lambda own: jax.random.permutation(own, SLOT))(jax.random.split(key_list[5], SEQS)).reshape((SEQS, SLOT)).astype(jnp.int32)
    norm_attn = jnp.clip(1.0 + 0.1 * jax.random.normal(key_list[6], (D,), jnp.float32), 0.5, 1.5).astype(jnp.bfloat16)
    w_query = gaussian(key_list[7], (D, D), D ** -0.5, 0.1875, ((0, 4),))
    w_key = gaussian(key_list[8], (D, D), D ** -0.5, 0.1875, ((0, 4),))
    w_value = gaussian(key_list[9], (D, D), D ** -0.5, 0.1875, ((0, 4),))
    w_out = gaussian(key_list[10], (D, D), (D // 16) ** -0.5, 0.75, ((0, 4),))
    rel_bias = gaussian(key_list[11], (BUCKETS, HEADS), 0.5, 3.0, ((0, 4),))
    norm_ffn = jnp.clip(1.0 + 0.1 * jax.random.normal(key_list[12], (D,), jnp.float32), 0.5, 1.5).astype(jnp.bfloat16)
    w_router = gaussian(key_list[13], (D, EXPERTS), D ** -0.5, 0.1875, ((0, 4),))
    w_gate = gaussian(key_list[14], (EXPERTS, D, FF), D ** -0.5, 0.1875, ((2, 4),))
    w_up = gaussian(key_list[15], (EXPERTS, D, FF), D ** -0.5, 0.1875, ((2, 4),))
    w_down = gaussian(key_list[16], (EXPERTS, FF, D), (FF // 16) ** -0.5, 0.4375, ((1, 4),))
    return {"tokens": tokens, "cotangent": cotangent, "lengths": lengths, "sequence_deal": sequence_deal, "routes": routes, "fill_order": fill_order, "norm_attn": norm_attn, "w_query": w_query, "w_key": w_key, "w_value": w_value, "w_out": w_out, "rel_bias": rel_bias, "norm_ffn": norm_ffn, "w_router": w_router, "w_gate": w_gate, "w_up": w_up, "w_down": w_down}


@jax.custom_vjp
def low(v):
    return lax.optimization_barrier(v.astype(jnp.bfloat16)).astype(jnp.float32)

@jax.custom_vjp
def low_back(v):
    return v

def low_keep(v):
    return (low(v), None)

def low_pass(kept, grad):
    return (grad,)

def back_keep(v):
    return (v, None)

def back_low(kept, grad):
    return (low(grad),)
low.defvjp(low_keep, low_pass)
low_back.defvjp(back_keep, back_low)
eps = 1e-06
bucket_edges = [int(math.ceil(16.0 * 8.0 ** (level / 16.0))) for level in range(1, 16)]

def product(left_side, right_side):
    return jnp.dot(left_side, right_side, precision=lax.Precision.HIGHEST, preferred_element_type=jnp.float32)

def rms_norm(values, gain_row):
    return values * lax.rsqrt(lax.optimization_barrier(jnp.mean(values * values, axis=-1, keepdims=True)) + eps) * gain_row

def bucket_ids(slot_count):
    query_pos = lax.broadcasted_iota(jnp.int32, (slot_count, slot_count), 0)
    key_pos = lax.broadcasted_iota(jnp.int32, (slot_count, slot_count), 1)
    distance = jnp.maximum(query_pos - key_pos, 0)
    bucket = jnp.minimum(distance, 16)
    for border in bucket_edges:
        bucket = bucket + (distance >= border).astype(jnp.int32)
    return (bucket, query_pos, key_pos)

def slot_plan(seq_routes, seq_order, length):
    slot_count = seq_order.shape[0]
    positions = jnp.arange(slot_count, dtype=jnp.int32)
    valid_rows = positions < length
    ranked_token = jnp.zeros((slot_count,), jnp.int32).at[seq_order].set(positions)
    ranked_routes = seq_routes[ranked_token]
    ranked_valid = valid_rows[ranked_token]
    picked = jnp.concatenate([ranked_routes[:, 0], ranked_routes[:, 1]])
    picked_valid = jnp.concatenate([ranked_valid, ranked_valid])
    expert_ids = jnp.arange(EXPERTS, dtype=jnp.int32)
    expert_hits = ((picked[:, None] == expert_ids[None, :]) & picked_valid[:, None]).astype(jnp.int32)
    running = jnp.cumsum(expert_hits, axis=0)
    place_rank = lax.optimization_barrier(jnp.sum(running * expert_hits, axis=1)) - 1
    kept_pair = picked_valid & (place_rank < CAP)
    flat_slot = jnp.where(kept_pair, picked * CAP + place_rank, EXPERTS * CAP).astype(jnp.int32)
    owner_token = jnp.concatenate([ranked_token, ranked_token])
    branch = jnp.concatenate([jnp.zeros((slot_count,), jnp.int32), jnp.ones((slot_count,), jnp.int32)])
    slot_token = jnp.full((EXPERTS * CAP + 1,), slot_count, jnp.int32).at[flat_slot].set(owner_token)[:EXPERTS * CAP]
    slot_choice = jnp.zeros((EXPERTS * CAP + 1,), jnp.int32).at[flat_slot].set(branch)[:EXPERTS * CAP]
    token_slot = jnp.zeros((slot_count, 2), jnp.int32).at[owner_token, branch].set(flat_slot)
    return (slot_token, slot_choice, token_slot)

def layer(weights, seq_x, length, seq_routes, seq_order):
    norm_attn, w_query, w_key, w_value, w_out, rel_bias, norm_ffn, w_router, w_gate, w_up, w_down = weights
    slot_count = seq_x.shape[0]
    width = seq_x.shape[1]
    normed = low(rms_norm(seq_x, norm_attn))
    queries = low(low_back(product(normed, w_query))).reshape(slot_count, HEADS, HEAD_DIM)
    keys_in = low(low_back(product(normed, w_key))).reshape(slot_count, HEADS, HEAD_DIM)
    values_in = low(low_back(product(normed, w_value))).reshape(slot_count, HEADS, HEAD_DIM)
    bucket, query_pos, key_pos = bucket_ids(slot_count)
    allowed = (key_pos <= query_pos) & (key_pos < length)
    bias_full = jnp.transpose(jnp.take(rel_bias, bucket, axis=0), (2, 0, 1))
    scores = jnp.einsum('qhd,khd->hqk', queries, keys_in, precision=lax.Precision.HIGHEST) * 0.125 + bias_full
    scores = low_back(jnp.where(allowed[None], scores, -1000000000.0))
    row_max = lax.optimization_barrier(jnp.max(scores, axis=-1, keepdims=True))
    log_total = row_max + jnp.log(lax.optimization_barrier(jnp.sum(jnp.exp(scores - row_max), axis=-1, keepdims=True)))
    attention = low(jnp.exp(scores - log_total))
    context = jnp.einsum('hqk,khd->qhd', attention, values_in, precision=lax.Precision.HIGHEST)
    context = low(low_back(context)).reshape(slot_count, width)
    middle = seq_x + low_back(product(context, w_out))
    ffn_in = low(rms_norm(middle, norm_ffn))
    router = jax.nn.softmax(product(ffn_in, w_router), axis=-1)
    slot_token, slot_choice, token_slot = slot_plan(seq_routes, seq_order, length)
    padded = jnp.concatenate([ffn_in, jnp.zeros((1, width), jnp.float32)])
    buffers = jnp.take(padded, slot_token, axis=0).reshape(EXPERTS, CAP, width)
    gate_act = low_back(jnp.einsum('ecd,edf->ecf', buffers, w_gate, precision=lax.Precision.HIGHEST))
    up_act = low_back(jnp.einsum('ecd,edf->ecf', buffers, w_up, precision=lax.Precision.HIGHEST))
    hidden = low(jax.nn.gelu(gate_act, approximate=True) * up_act)
    expert_out = jnp.einsum('ecf,efd->ecd', hidden, w_down, precision=lax.Precision.HIGHEST)
    expert_out = low(low_back(expert_out)).reshape(EXPERTS * CAP, width)
    padded_out = jnp.concatenate([expert_out, jnp.zeros((1, width), jnp.float32)])
    gathered = jnp.take(padded_out, token_slot, axis=0)
    kept_pair = (token_slot < EXPERTS * CAP).astype(jnp.float32)
    route_hits = (seq_routes[:, :, None] == jnp.arange(EXPERTS, dtype=jnp.int32)[None, None, :]).astype(jnp.float32)
    gates = lax.optimization_barrier(jnp.sum(router[:, None, :] * route_hits, axis=-1)) * kept_pair
    return middle + lax.optimization_barrier(jnp.sum(gates[:, :, None] * gathered, axis=1))

def reference(tokens, cotangent, lengths, sequence_deal, routes, fill_order, norm_attn, w_query, w_key, w_value, w_out, rel_bias, norm_ffn, w_router, w_gate, w_up, w_down):
    weights = tuple((item.astype(jnp.float32) for item in (norm_attn, w_query, w_key, w_value, w_out, rel_bias, norm_ffn, w_router, w_gate, w_up, w_down)))
    group_size = sequence_deal.shape[1]
    group_ids = jnp.arange(sequence_deal.shape[0], dtype=jnp.int32)
    source_index = (group_ids[:, None] * group_size + sequence_deal).reshape(-1).astype(jnp.int32)
    seq_inputs = tokens[source_index].astype(jnp.float32)
    seq_grads = cotangent[source_index].astype(jnp.float32)
    seq_lengths = lengths.reshape(-1)[source_index]

    def one_step(totals, items):
        seq_x, seq_up, length, seq_routes, seq_order = items
        result, pullback = jax.vjp(lambda params, values: layer(params, values, length, seq_routes, seq_order), weights, seq_x)
        grad_params, grad_x = pullback(seq_up)
        totals = jax.tree.map(lambda total, addend: total + addend, totals, grad_params)
        return (totals, (result, grad_x))
    initial = jax.tree.map(jnp.zeros_like, weights)
    totals, (results, grad_rows) = lax.scan(one_step, initial, (seq_inputs, seq_grads, seq_lengths, routes, fill_order))
    output = jnp.zeros_like(results).at[source_index].set(results).astype(jnp.bfloat16)
    grad_tokens = jnp.zeros_like(grad_rows).at[source_index].set(grad_rows).astype(jnp.bfloat16)
    return (output, grad_tokens, totals[0], totals[1], totals[2], totals[3], totals[4], totals[5], totals[6], totals[7], totals[8], totals[9], totals[10])
```

```python
import functools
import math

import jax
import jax.numpy as jnp
from jax import lax
from jax.experimental import pallas as pl
from jax.experimental.pallas import tpu as pltpu
from jax.sharding import PartitionSpec as P

HEADS = 16
HEAD_DIM = 64
EXPERTS = 4
BUCKETS = 32
CAP = 144
LANES = 128

eps = 1e-06
bucket_edges = [int(math.ceil(16.0 * 8.0 ** (level / 16.0))) for level in range(1, 16)]
bf16 = jnp.bfloat16
f32 = jnp.float32


def dot_nn(a, b):
    return lax.dot_general(a, b, (((1,), (0,)), ((), ())), preferred_element_type=f32)


def dot_nt(a, b):
    return lax.dot_general(a, b, (((1,), (1,)), ((), ())), preferred_element_type=f32)


def dot_tn(a, b):
    return lax.dot_general(a, b, (((0,), (0,)), ((), ())), preferred_element_type=f32)


def params(mib):
    return pltpu.CompilerParams(vmem_limit_bytes=mib * 1024 * 1024)


def vmem():
    return pl.BlockSpec(memory_space=pltpu.VMEM)


def anywhere():
    return pl.BlockSpec(memory_space=pl.ANY)


def smem():
    return pl.BlockSpec(memory_space=pltpu.SMEM)


def bias_kernel(len_ref, base_ref, out_ref):
    n = base_ref.shape[2]
    rows = lax.broadcasted_iota(jnp.int32, (n, n), 0)
    cols = lax.broadcasted_iota(jnp.int32, (n, n), 1)
    allowed = (cols <= rows) & (cols < len_ref[0])
    for h in range(2):
        row = jnp.broadcast_to(base_ref[0, h : h + 1, :], (n, n))
        bias = pltpu.roll(row, 0, 1, stride=1, stride_axis=0)
        out_ref[h] = jnp.where(allowed, bias, -1000000000.0).astype(bf16)


def bias_of(length, base):
    pairs, _, n = base.shape
    return pl.pallas_call(
        bias_kernel,
        grid_spec=pltpu.PrefetchScalarGridSpec(
            num_scalar_prefetch=1,
            grid=(pairs,),
            in_specs=[pl.BlockSpec((1, 2, n), lambda i, l: (i, 0, 0))],
            out_specs=pl.BlockSpec((2, n, n), lambda i, l: (i, 0, 0)),
        ),
        out_shape=jax.ShapeDtypeStruct((2 * pairs, n, n), bf16),
        compiler_params=params(16),
        name="bias",
    )(length, base)


def softmax_of(q, k, bias):
    s = dot_nt(q, k) * 0.125 + bias.astype(f32)
    e = jnp.exp(s - jnp.max(s, axis=-1, keepdims=True))
    return e * (1.0 / jnp.sum(e, axis=-1, keepdims=True))


def gather_rows(off_ref, pieces, dest, sems):
    rows = pieces[0].shape[0]
    copies = []
    for p, piece in enumerate(pieces):
        start = pl.multiple_of(off_ref[p] * rows, rows)
        copies.append(pltpu.make_async_copy(piece, dest.at[pl.ds(start, rows)], sems.at[p]))
        copies[-1].start()
    return copies


def attn_fwd_kernel(N, *refs):
    off_ref, x_ref, gain_ref, bias_ref = refs[:4]
    pieces = refs[4 : 4 + N]
    h_ref, qkv_ref, c_ref, wout_ref, w_s, sems = refs[4 + N :]
    width = x_ref.shape[1]
    copies = gather_rows(off_ref, pieces, w_s, sems)
    x = x_ref[...].astype(f32)
    scale = lax.rsqrt(jnp.mean(x * x, axis=-1, keepdims=True) + eps)
    h_ref[...] = (x * scale * gain_ref[...]).astype(bf16)
    for copy in copies:
        copy.wait()
    out = pltpu.make_async_copy(w_s, wout_ref, sems.at[N])
    out.start()
    step = width // 2

    def project(i, carry):
        cut = pl.ds(pl.multiple_of(i * step, step), step)
        qkv_ref[:, cut] = dot_nn(h_ref[...], w_s[:, cut]).astype(bf16)
        return carry

    lax.fori_loop(0, 3 * width // step, project, 0)

    def pair(i, carry):
        def at(j):
            return pl.ds(pl.multiple_of(j * width + i * LANES, LANES), LANES)

        q2, k2, v2 = qkv_ref[:, at(0)], qkv_ref[:, at(1)], qkv_ref[:, at(2)]
        heads = []
        for h in range(2):
            cut = slice(h * HEAD_DIM, (h + 1) * HEAD_DIM)
            p = softmax_of(q2[:, cut], k2[:, cut], bias_ref[2 * i + h]).astype(bf16)
            heads.append(dot_nn(p, v2[:, cut]).astype(bf16))
        c_ref[:, at(0)] = jnp.concatenate(heads, axis=1)
        return carry

    lax.fori_loop(0, HEADS // 2, pair, 0)
    out.wait()


def attn_fwd(offsets, x, gain, bias, pieces):
    n, width = x.shape
    N = len(pieces)
    full = jax.ShapeDtypeStruct((n, width), bf16)
    return pl.pallas_call(
        functools.partial(attn_fwd_kernel, N),
        in_specs=[smem(), vmem(), vmem(), vmem()] + [anywhere()] * N,
        out_specs=[vmem(), vmem(), vmem(), anywhere()],
        out_shape=[
            full,
            jax.ShapeDtypeStruct((n, 3 * width), bf16),
            full,
            jax.ShapeDtypeStruct((width, 3 * width), bf16),
        ],
        scratch_shapes=[pltpu.VMEM((width, 3 * width), bf16), pltpu.SemaphoreType.DMA((N + 1,))],
        compiler_params=params(24),
        name="attn_fwd",
    )(offsets, x, gain, bias, *pieces)


def mid_kernel(N, *refs):
    off_ref, x_ref, gain_ref, c_ref = refs[:4]
    pieces = refs[4 : 4 + N]
    mid_ref, h_ref, wout_ref, w_s, sems = refs[4 + N :]
    for copy in gather_rows(off_ref, pieces, w_s, sems):
        copy.wait()
    out = pltpu.make_async_copy(w_s, wout_ref, sems.at[N])
    out.start()
    mid = x_ref[...].astype(f32) + dot_nn(c_ref[...], w_s[...])
    scale = lax.rsqrt(jnp.mean(mid * mid, axis=-1, keepdims=True) + eps)
    mid_ref[...] = mid
    h_ref[...] = (mid * scale * gain_ref[...]).astype(bf16)
    out.wait()


def mid_of(offsets, x, gain, context, pieces):
    n, width = x.shape
    N = len(pieces)
    return pl.pallas_call(
        functools.partial(mid_kernel, N),
        in_specs=[smem(), vmem(), vmem(), vmem()] + [anywhere()] * N,
        out_specs=[vmem(), vmem(), anywhere()],
        out_shape=[
            jax.ShapeDtypeStruct((n, width), f32),
            jax.ShapeDtypeStruct((n, width), bf16),
            jax.ShapeDtypeStruct((width, width), bf16),
        ],
        scratch_shapes=[pltpu.VMEM((width, width), bf16), pltpu.SemaphoreType.DMA((N + 1,))],
        compiler_params=params(16),
        name="middle",
    )(offsets, x, gain, context, *pieces)


def attn_bwd_kernel(q_ref, k_ref, v_ref, bias_ref, dc_ref, dq_ref, dk_ref, dv_ref, diag_ref):
    n = q_ref.shape[0]
    rows = lax.broadcasted_iota(jnp.int32, (n, n), 0)
    cols = lax.broadcasted_iota(jnp.int32, (n, n), 1)
    reverse = (rows + cols == n - 1).astype(bf16)
    for h in range(2):
        cut = slice(h * HEAD_DIM, (h + 1) * HEAD_DIM)
        q, k, v, dc = q_ref[:, cut], k_ref[:, cut], v_ref[:, cut], dc_ref[:, cut]
        p = softmax_of(q, k, bias_ref[h])
        dp = dot_nt(dc, v)
        ds = p * (dp - jnp.sum(p * dp, axis=-1, keepdims=True))
        low = ds.astype(bf16)
        dq_ref[:, cut] = (dot_nn(low, k) * 0.125).astype(bf16)
        dk_ref[:, cut] = (dot_tn(low, q) * 0.125).astype(bf16)
        dv_ref[:, cut] = dot_tn(p.astype(bf16), dc).astype(bf16)
        turned = pltpu.roll(dot_nn(reverse, low), 1, 1, stride=1, stride_axis=0)
        diag_ref[0, h : h + 1, :] = jnp.sum(turned, axis=0, keepdims=True)


def attn_bwd(qkv, bias, dc):
    n = qkv.shape[0]
    pairs = HEADS // 2
    blk = pl.BlockSpec((n, LANES), lambda i: (0, i))
    row = pl.BlockSpec((1, 2, n), lambda i: (i, 0, 0))
    full = jax.ShapeDtypeStruct((n, HEADS * HEAD_DIM), bf16)
    return pl.pallas_call(
        attn_bwd_kernel,
        grid=(pairs,),
        in_specs=[
            blk,
            pl.BlockSpec((n, LANES), lambda i: (0, pairs + i)),
            pl.BlockSpec((n, LANES), lambda i: (0, 2 * pairs + i)),
            pl.BlockSpec((2, n, n), lambda i: (i, 0, 0)),
            blk,
        ],
        out_specs=[blk, blk, blk, row],
        out_shape=[full, full, full, jax.ShapeDtypeStruct((pairs, 2, n), f32)],
        compiler_params=params(16),
        name="attn_bwd",
    )(qkv, qkv, qkv, bias, dc)


def ffn_kernel(S, e, *refs):
    core_ref, pos_ref, aux_ref = refs[:3]
    h2 = refs[3 : 3 + S]
    ct = refs[3 + S : 3 + 2 * S]
    wg_hbm, wu_hbm, wd_hbm = refs[3 + 2 * S : 6 + 2 * S]
    refs = refs[6 + 2 * S + (1 if e else 0) :]
    gk, gs, uk, us, dk, ds, eodx, dr = refs[:8]
    refs = refs[8:]
    if e == 0:
        prob_ref, refs = refs[0], refs[1:]
    else:
        prob_ref = aux_ref
    wg, wu, wd, x_s, c_s, gate_s, a_s, u_s, d_s, hid_s, da_s, du_s, g_o, u_o, d_o, ed_o, sems = refs
    n, width = h2[0].shape
    loads = []
    for i, (src, dst) in enumerate(((wg_hbm, wg), (wu_hbm, wu), (wd_hbm, wd))):
        loads.append(pltpu.make_async_copy(src.at[e], dst, sems.at[i]))
        loads[-1].start()
    lanes = lax.broadcasted_iota(jnp.int32, (n, LANES), 1)
    slots = lax.broadcasted_iota(jnp.int32, (CAP, n), 0)
    if e == 0:
        for s in range(S):
            logits = jnp.where(lanes < EXPERTS, dot_nn(h2[s][...], aux_ref[...]), -1e30)
            ex = jnp.exp(logits - jnp.max(logits, axis=-1, keepdims=True))
            prob = ex / jnp.sum(ex, axis=-1, keepdims=True)
            high = prob.astype(bf16).astype(f32)
            rest = pltpu.roll(prob - high, EXPERTS, 1)
            prob_ref[s] = jnp.where(lanes < EXPERTS, high, rest).astype(bf16)
    for s in range(S):
        rows = slice(s * CAP, (s + 1) * CAP)
        hot = (slots == pos_ref[s, e : e + 1, :]).astype(bf16)
        x_s[rows, :] = dot_nn(hot, h2[s][...]).astype(bf16)
        c_s[rows, :] = dot_nn(hot, ct[s][...]).astype(bf16)
        picked = dot_nn(hot, prob_ref[s])
        gate_s[rows, :] = jnp.broadcast_to(
            picked[:, e : e + 1] + picked[:, EXPERTS + e : EXPERTS + e + 1], (CAP, LANES)
        )
    loads[0].wait()
    a_s[...] = dot_nt(x_s[...], wg[...])
    loads[1].wait()
    u_s[...] = dot_nt(x_s[...], wu[...])
    loads[2].wait()
    d_s[...] = dot_nt(c_s[...], wd[...])
    const = math.sqrt(2.0 / math.pi)
    for s in range(S):
        rows = slice(s * CAP, (s + 1) * CAP)
        a, u, d0, gate = a_s[rows, :], u_s[rows, :], d_s[rows, :], gate_s[rows, 0:1]
        t = jnp.tanh(const * (a + 0.044715 * a * a * a))
        half = 0.5 * (1.0 + t)
        act = a * half
        slope = half + 0.5 * a * (1.0 - t * t) * (const * (1.0 + 3 * 0.044715 * a * a))
        hid = act * u
        dg = jnp.sum(hid * d0, axis=-1, keepdims=True)
        hid_s[rows, :] = (gate * hid).astype(bf16)
        dh = gate * d0
        da_s[rows, :] = (dh * u * slope).astype(bf16)
        du_s[rows, :] = (dh * act).astype(bf16)
        hot = (slots == pos_ref[s, e : e + 1, :]).astype(f32)
        dr[s : s + 1, :] = jnp.sum(hot * dg, axis=0, keepdims=True)
    half_w = width // 2
    core = core_ref[0]
    mine = pl.ds(pl.multiple_of(core * half_w, half_w), half_w)
    other = pl.ds(pl.multiple_of((1 - core) * half_w, half_w), half_w)
    stores = []

    def store(src, dst):
        stores.append(pltpu.make_async_copy(src, dst, sems.at[3 + len(stores)]))
        stores[-1].start()

    for left, right, buf, keep, send in (
        (hid_s, c_s, d_o, dk, ds),
        (da_s, x_s, g_o, gk, gs),
        (du_s, x_s, u_o, uk, us),
    ):
        buf[...] = dot_tn(left[...], right[...]).astype(bf16)
        store(buf.at[:, other], send)
        store(buf.at[:, mine], keep)
    ed_o[:, :width] = dot_nn(hid_s[...], wd[...]).astype(bf16)
    ed_o[:, width:] = (dot_nn(da_s[...], wg[...]) + dot_nn(du_s[...], wu[...])).astype(bf16)
    for s in range(S):
        store(ed_o.at[pl.ds(s * CAP, CAP)], eodx.at[s, pl.ds(e * CAP, CAP)])
    for copy in stores:
        copy.wait()


def ffn(e, core, pos, aux, h2, ct, w_gate, w_up, w_down, chain):
    S = len(h2)
    n, width = h2[0].shape
    cols = w_gate.shape[1]
    rows = S * CAP
    half = jax.ShapeDtypeStruct((cols, width // 2), bf16)
    shapes = [half] * 6 + [
        jax.ShapeDtypeStruct((S, EXPERTS * CAP, 2 * width), bf16),
        jax.ShapeDtypeStruct((S, n), f32),
    ]
    specs = [anywhere()] * 7 + [vmem()]
    if e == 0:
        shapes.append(jax.ShapeDtypeStruct((S, n, LANES), bf16))
        specs.append(vmem())
    return pl.pallas_call(
        functools.partial(ffn_kernel, S, e),
        in_specs=[smem()] + [vmem()] * (2 + 2 * S) + [anywhere()] * (4 if e else 3),
        out_specs=specs,
        out_shape=shapes,
        input_output_aliases={6 + 2 * S: 6} if e else {},
        scratch_shapes=[pltpu.VMEM((cols, width), bf16)] * 3
        + [pltpu.VMEM((rows, width), bf16)] * 2
        + [pltpu.VMEM((rows, LANES), f32)]
        + [pltpu.VMEM((rows, cols), f32)] * 3
        + [pltpu.VMEM((rows, cols), bf16)] * 3
        + [pltpu.VMEM((cols, width), bf16)] * 3
        + [pltpu.VMEM((rows, 2 * width), bf16), pltpu.SemaphoreType.DMA((9 + S,))],
        compiler_params=params(44),
        cost_estimate=pl.CostEstimate(
            flops=18 * rows * width * cols, bytes_accessed=20_000_000, transcendentals=0
        ),
        name=f"ffn{e}",
    )(core, pos, aux, *h2, *ct, w_gate, w_up, w_down, *([chain] if e else []))


def combine_kernel(S, pos_ref, src_ref, *outs):
    n, width = outs[0].shape
    lanes = lax.broadcasted_iota(jnp.int32, (n, EXPERTS * CAP), 1)
    s = pl.program_id(0)
    hot = lanes == pos_ref[:, 0:1]
    for e in range(1, EXPERTS):
        hot = hot | (lanes == pos_ref[:, e : e + 1])
    total = dot_nn(hot.astype(bf16), src_ref[...]).astype(bf16)
    for i in range(S):

        @pl.when(s == i)
        def _(i=i):
            outs[i][...] = total


def combine(pos_col, eodx):
    S, n = pos_col.shape[:2]
    width = eodx.shape[2]
    return pl.pallas_call(
        functools.partial(combine_kernel, S),
        grid=(S,),
        in_specs=[
            pl.BlockSpec((None, n, LANES), lambda s: (s, 0, 0)),
            pl.BlockSpec((None, EXPERTS * CAP, width), lambda s: (s, 0, 0)),
        ],
        out_specs=[pl.BlockSpec((n, width), lambda s: (0, 0))] * S,
        out_shape=[jax.ShapeDtypeStruct((n, width), bf16)] * S,
        compiler_params=params(40),
        name="combine",
    )(pos_col, eodx)


def stages_of(size):
    n = size // 2
    h = n // 2
    swap = [(i, i ^ 1) for i in range(size)]
    plan = [(swap, "add")]
    for k in range(h - 1):
        plan.append((line_perm([(k, k + 1), (n - 1 - k, n - 2 - k)]), "add"))
    plan.append((line_perm([(h - 1, h), (h, h - 1)]), "add"))
    for k in reversed(range(h - 1)):
        plan.append((line_perm([(k + 1, k), (n - 2 - k, n - 1 - k)]), k))
    plan.append((swap, "final"))
    return plan


def wave_kernel(size, kinds, *refs):
    place_ref = refs[0]
    line, core = place_ref[0], place_ref[1]
    n_in = 2 * len(kinds)
    ins = refs[1 : 1 + n_in]
    outs = refs[-len(kinds) :]
    last = size // 2 - 1
    for i, kind in enumerate(kinds):
        have, got, out = ins[2 * i], ins[2 * i + 1], outs[i]
        half = have.shape[1]
        if kind == "add":
            out[...] = (have[...].astype(f32) + got[...].astype(f32)).astype(bf16)
        elif kind == "final":
            a, b = have[...].astype(f32), got[...].astype(f32)
            out[:, :half] = jnp.where(core == 0, a, b)
            out[:, half:] = jnp.where(core == 0, b, a)
        else:
            take = (line == kind) | (line == last - kind)
            out[...] = jnp.where(take, got[...], have[...])


def row_block(rows):
    return max(b for b in range(16, min(rows, 256) + 1, 16) if rows % b == 0)


def wave(size, place, entries):
    kinds = tuple(e[0] for e in entries)
    rows, half = entries[0][1].shape
    blk = row_block(rows)
    spec = pl.BlockSpec((blk, half), lambda r: (r, 0))
    ins, outs, shapes, extra, aliases = [], [], [], [], {}
    for kind, have, got, final in entries:
        ins += [have, got]
    for i, (kind, have, got, final) in enumerate(entries):
        if kind == "final":
            expert, target = final
            outs.append(pl.BlockSpec((None, blk, 2 * half), lambda r, e=expert: (e, r, 0)))
            shapes.append(jax.ShapeDtypeStruct((EXPERTS, rows, 2 * half), f32))
            if target is not None:
                aliases[1 + len(ins) + len(extra)] = i
                extra.append(target)
        else:
            outs.append(spec)
            shapes.append(jax.ShapeDtypeStruct((rows, half), bf16))
    return pl.pallas_call(
        functools.partial(wave_kernel, size, kinds),
        grid=(rows // blk,),
        in_specs=[smem()] + [spec] * len(ins) + [anywhere()] * len(extra),
        out_specs=outs,
        out_shape=shapes,
        input_output_aliases=aliases,
        compiler_params=params(24),
        name="wave",
    )(place, *ins, *extra)


def pipelined_sums(size, place, chunks):
    plan = stages_of(size)
    targets = {}
    state = {}
    for w in range(len(chunks) + len(plan) - 1):
        entries, where = [], []
        for k in range(max(0, w - len(plan) + 1), min(w + 1, len(chunks))):
            pairs, kind = plan[w - k]
            keep, send, out, expert = chunks[k]
            have = keep if w == k else state[k]
            got = lax.ppermute(send if w == k else have, "rep", pairs)
            entries.append((kind, have, got, (expert, targets.get(out))))
            where.append((k, out, kind))
        for (k, out, kind), value in zip(where, wave(size, place, entries)):
            if kind == "final":
                targets[out] = value
            else:
                state[k] = value
    return targets


def swap_core(x, size):
    return lax.ppermute(x, "rep", [(i, i ^ 1) for i in range(size)])


def swap_shard(x, size, mask):
    return lax.ppermute(x, "shard", [(i, i ^ mask) for i in range(size)])


def line_perm(pairs):
    return [(2 * a + c, 2 * b + c) for a, b in pairs for c in range(2)]


def line_sum(x, size, line):
    n = size // 2
    h = n // 2
    for k in range(h - 1):
        x = x + lax.ppermute(x, "rep", line_perm([(k, k + 1), (n - 1 - k, n - 2 - k)]))
    x = x + lax.ppermute(x, "rep", line_perm([(h - 1, h), (h, h - 1)]))
    for k in reversed(range(h - 1)):
        got = lax.ppermute(x, "rep", line_perm([(k + 1, k), (n - 2 - k, n - 1 - k)]))
        x = jnp.where((line == k) | (line == n - 1 - k), got, x)
    return x


def rms_backward(values, scale, gain_row, upward):
    grad_gain = jnp.sum(upward * values * scale, axis=0)
    weighted = upward * gain_row
    grad_values = scale * weighted - values * scale * scale * scale * jnp.mean(
        values * weighted, axis=-1, keepdims=True
    )
    return (grad_values, grad_gain)


def bucket_of(distance):
    bucket = jnp.minimum(distance, 16)
    for border in bucket_edges:
        bucket = bucket + (distance >= border).astype(jnp.int32)
    return bucket


def slot_positions(routes, order, lengths):
    n = order.shape[1]
    valid = jnp.arange(n, dtype=jnp.int32)[None, :] < lengths[:, None]
    experts = jnp.arange(EXPERTS, dtype=jnp.int32)
    hits = (routes[:, :, :, None] == experts) & valid[:, :, None, None]
    hits = hits.reshape(routes.shape[0], n, 2 * EXPERTS)
    before = (order[:, None, :] < order[:, :, None]).astype(bf16)
    count = jnp.einsum("stk,sut->sku", hits.astype(bf16), before, preferred_element_type=f32)
    total = jnp.sum(hits[:, :, :EXPERTS].astype(f32), axis=1)
    hits = jnp.swapaxes(hits, 1, 2)
    first, second = count[:, :EXPERTS], count[:, EXPERTS:] + total[:, :, None]
    slot = jnp.where(
        hits[:, :EXPERTS], first, jnp.where(hits[:, EXPERTS:], second, float(2 * CAP + n))
    )
    return jnp.where(slot < CAP, slot, -1.0).astype(jnp.int32)


def shards(
    R,
    S,
    tokens,
    cotangent,
    lengths,
    sequence_deal,
    routes,
    fill_order,
    norm_attn,
    w_query,
    w_key,
    w_value,
    w_out,
    rel_bias,
    norm_ffn,
    w_router,
    w_gate,
    w_up,
    w_down,
):
    me = lax.axis_index("shard")
    rep = lax.axis_index("rep")
    core = rep % 2
    line = rep // 2
    x_low, ct_low = tokens[0], cotangent[0]
    n, width = x_low.shape
    part = width // S
    half = part // 2
    group = jnp.arange(S, dtype=jnp.int32)

    bias_flat = jnp.pad(rel_bias.reshape(-1), (0, part - rel_bias.size))
    small = jnp.concatenate(
        [norm_attn[:, None], norm_ffn[:, None], w_router, bias_flat[:, None]], axis=1
    )
    plan = jnp.concatenate([routes[0], fill_order[0][:, None]], axis=1)
    small_all = jnp.zeros((S,) + small.shape, bf16)
    plan_all = jnp.zeros((S,) + plan.shape, jnp.int32)
    for m in range(S):
        got_s = small if m == 0 else swap_shard(small, S, m)
        got_p = plan if m == 0 else swap_shard(plan, S, m)
        small_all = lax.dynamic_update_slice(small_all, got_s[None], (me ^ m, 0, 0))
        plan_all = lax.dynamic_update_slice(plan_all, got_p[None], (me ^ m, 0, 0))
    gain_one = small_all[:, :, 0].reshape(-1).astype(f32)
    gain_two = small_all[:, :, 1].reshape(-1).astype(f32)
    router_w = small_all[:, :, 2 : 2 + EXPERTS].reshape(width, EXPERTS)
    bias_table = small_all[:, : rel_bias.size, 2 + EXPERTS].reshape(BUCKETS, HEADS)

    low_half = [
        lax.dynamic_slice_in_dim(w, core * half, half, 0) for w in (w_query, w_key, w_value, w_out)
    ]
    stack_qkv = jnp.concatenate(low_half[:3], axis=1)
    qkv_pieces, out_pieces, offsets = [], [], []
    for stack, pieces in ((stack_qkv, qkv_pieces), (low_half[3], out_pieces)):
        for m in range(S):
            got = stack if m == 0 else swap_shard(stack, S, m)
            pieces += [got, swap_core(got, R)]
    for m in range(S):
        offsets += [2 * (me ^ m) + core, 2 * (me ^ m) + 1 - core]
    offsets = jnp.stack(offsets).astype(jnp.int32)
    ct_all = [ct_low] + [swap_shard(ct_low, S, m) for m in range(1, S)]

    deal = sequence_deal[0]
    row_of = jnp.sum(group[:, None] * (deal[:, None] == group[None, :]).astype(jnp.int32), axis=0)
    homes = me ^ group
    rows = jnp.take(row_of, homes)
    plans = jnp.take(plan_all, rows, axis=0)
    pos = slot_positions(plans[:, :, :2], plans[:, :, 2], jnp.take(lengths[0], homes))
    length = lax.dynamic_slice_in_dim(lengths[0], me, 1, 0)

    turned = jnp.arange(n, dtype=jnp.int32)
    hot = (bucket_of((n - turned) % n)[None, :] == jnp.arange(BUCKETS)[:, None]).astype(bf16)
    base = dot_tn(bias_table, hot).reshape(HEADS // 2, 2, n)

    bias = bias_of(length, base)
    normed_low, qkv, context, qkv_w = attn_fwd(offsets, x_low, gain_one[None], bias, qkv_pieces)
    middle, ffn_in, out_w = mid_of(offsets, x_low, gain_two[None], context, out_pieces)

    h2_all = [ffn_in] + [swap_shard(ffn_in, S, m) for m in range(1, S)]
    router_pad = jnp.pad(router_w, ((0, 0), (0, LANES - EXPERTS)))
    core_one = core.reshape(1).astype(jnp.int32)
    place = jnp.stack([line, core]).astype(jnp.int32)
    gate_t, up_t = jnp.swapaxes(w_gate, 1, 2), jnp.swapaxes(w_up, 1, 2)
    eodx, aux, drs, chunks = None, router_pad, [], []
    for e in range(EXPERTS):
        got = ffn(e, core_one, pos, aux, h2_all, ct_all, gate_t, up_t, w_down, eodx)
        gk, gs, uk, us, dk, ds, eodx, dr = got[:8]
        if e == 0:
            aux = got[8]
        drs.append(dr)
        chunks += [(dk, ds, 2, e), (gk, gs, 0, e), (uk, us, 1, e)]
    flat = jnp.arange(EXPERTS, dtype=jnp.int32) * CAP
    pos_col = jnp.swapaxes(jnp.where(pos < 0, -1, pos + flat[None, :, None]), 1, 2)
    pos_col = jnp.pad(pos_col, ((0, 0), (0, 0), (0, LANES - EXPERTS)))
    parts = combine(pos_col, eodx)
    dr_all = jnp.stack(drs, axis=1)
    total = parts[0].astype(f32)
    drouter = dr_all[0]
    for m in range(1, S):
        total = total + swap_shard(parts[m], S, m).astype(f32)
        drouter = drouter + swap_shard(dr_all[m], S, m)

    sums = pipelined_sums(R, place, chunks)
    gate_total, up_total, down_total = jnp.swapaxes(sums[0], 1, 2), jnp.swapaxes(sums[1], 1, 2), sums[2]

    result = middle + total[:, :width]
    upstream = ct_low.astype(f32)
    inputs = x_low.astype(f32)
    scale_one = lax.rsqrt(jnp.mean(inputs * inputs, axis=-1, keepdims=True) + eps)
    scale_two = lax.rsqrt(jnp.mean(middle * middle, axis=-1, keepdims=True) + eps)
    probs = jax.nn.softmax(dot_nn(ffn_in, router_w), axis=-1)
    drouter = drouter.T
    dlogit = probs * (drouter - jnp.sum(probs * drouter, axis=-1, keepdims=True))
    grad_ffn_in = total[:, width:] + lax.dot_general(
        dlogit,
        router_w.astype(f32),
        (((1,), (1,)), ((), ())),
        precision=lax.Precision.HIGHEST,
        preferred_element_type=f32,
    )
    grad_router_w = lax.dot_general(
        ffn_in.astype(f32),
        dlogit,
        (((0,), (0,)), ((), ())),
        precision=lax.Precision.HIGHEST,
        preferred_element_type=f32,
    )
    grad_middle, grad_gain_two = rms_backward(middle, scale_two, gain_two, grad_ffn_in)
    grad_middle = grad_middle + upstream
    grad_attn_low = grad_middle.astype(bf16)
    grad_out_w = dot_tn(context, grad_attn_low).astype(bf16)
    grad_context = dot_nt(grad_attn_low, out_w).astype(bf16)
    dq, dk, dv, diag = attn_bwd(qkv, bias, grad_context)
    grad_table = dot_nt(hot.astype(f32), diag.reshape(HEADS, n))
    dqkv = jnp.concatenate([dq, dk, dv], axis=1)
    grad_normed = dot_nt(dqkv, qkv_w)
    grad_qkv_w = dot_tn(normed_low, dqkv).astype(bf16)
    grad_inputs, grad_gain_one = rms_backward(inputs, scale_one, gain_one, grad_normed)
    grad_inputs = grad_inputs + grad_middle

    table = jnp.pad(grad_table.reshape(S, -1), ((0, 0), (0, part - rel_bias.size)))
    extra = jnp.concatenate(
        [grad_gain_one[:, None], grad_gain_two[:, None], grad_router_w, table.reshape(-1, 1)],
        axis=1,
    ).astype(bf16)
    extra = jnp.pad(extra, ((0, 0), (0, LANES - extra.shape[1])))
    dense = jnp.concatenate([grad_qkv_w, grad_out_w, extra], axis=1)
    dense = dense.reshape(S, 2, half, -1)
    keep = lax.dynamic_index_in_dim(dense, core, 1, keepdims=False)
    send = lax.dynamic_index_in_dim(dense, 1 - core, 1, keepdims=False)
    keep = keep + swap_core(send, R)
    owned = lax.dynamic_index_in_dim(keep, me, 0, keepdims=False).astype(f32)
    for m in range(1, S):
        block = lax.dynamic_index_in_dim(keep, me ^ m, 0, keepdims=False)
        owned = owned + swap_shard(block, S, m).astype(f32)
    mine = line_sum(owned.astype(bf16), R, line)
    other = swap_core(mine, R)
    dense = jnp.concatenate(
        [jnp.where(core == 0, mine, other), jnp.where(core == 0, other, mine)], axis=0
    ).astype(f32)
    extra = dense[:, 4 * width :]
    return (
        result.astype(bf16)[None],
        grad_inputs.astype(bf16)[None],
        extra[:, 0],
        dense[:, :width],
        dense[:, width : 2 * width],
        dense[:, 2 * width : 3 * width],
        dense[:, 3 * width : 4 * width],
        extra[: rel_bias.size, 2 + EXPERTS].reshape(rel_bias.shape),
        extra[:, 1],
        extra[:, 2 : 2 + EXPERTS],
        gate_total,
        up_total,
        down_total,
    )


def solution(mesh):
    R, S = mesh.shape["rep"], mesh.shape["shard"]
    rows = P(("rep", "shard"), None, None)
    mat = P("shard", None)
    return jax.shard_map(
        functools.partial(shards, R, S),
        mesh=mesh,
        in_specs=(rows, rows, P("rep", None), P("rep", None), rows, P(("rep", "shard"), None))
        + (P("shard"), mat, mat, mat, mat, mat, P("shard"), mat)
        + (P(None, None, "shard"), P(None, None, "shard"), P(None, "shard", None)),
        out_specs=(rows, rows, P("shard"), mat, mat, mat, mat, mat, P("shard"), mat)
        + (P(None, None, "shard"), P(None, None, "shard"), P(None, "shard", None)),
        check_vma=False,
    )
```

```python
import functools
import math

import jax
import jax.numpy as jnp
from jax import lax
from jax.experimental import pallas as pl
from jax.experimental.pallas import tpu as pltpu
from jax.sharding import PartitionSpec as P

HEADS = 16
HEAD_DIM = 64
EXPERTS = 4
BUCKETS = 32
CAP = 144
LANES = 128

eps = 1e-06
bucket_edges = [int(math.ceil(16.0 * 8.0 ** (level / 16.0))) for level in range(1, 16)]
bf16 = jnp.bfloat16
f32 = jnp.float32


def dot_nn(a, b):
    return lax.dot_general(a, b, (((1,), (0,)), ((), ())), preferred_element_type=f32)


def dot_nt(a, b):
    return lax.dot_general(a, b, (((1,), (1,)), ((), ())), preferred_element_type=f32)


def dot_tn(a, b):
    return lax.dot_general(a, b, (((0,), (0,)), ((), ())), preferred_element_type=f32)


def params(mib):
    return pltpu.CompilerParams(vmem_limit_bytes=mib * 1024 * 1024)


def vmem():
    return pl.BlockSpec(memory_space=pltpu.VMEM)


def anywhere():
    return pl.BlockSpec(memory_space=pl.ANY)


TOKEN = jax.ShapeDtypeStruct((8, LANES), f32)


def token_spec():
    return pl.BlockSpec((8, LANES), lambda *i: (0, 0))


def give(token):
    token[...] = jnp.zeros(token.shape, token.dtype)


def short():
    return pl.CostEstimate(flops=1, bytes_accessed=1, transcendentals=0)


def hbm():
    return pl.BlockSpec(memory_space=pltpu.HBM)


def pin(x):
    return pltpu.with_memory_space_constraint(x, pltpu.HBM)


def smem():
    return pl.BlockSpec(memory_space=pltpu.SMEM)


def bias_kernel(len_ref, base_ref, out_ref):
    n = base_ref.shape[2]
    rows = lax.broadcasted_iota(jnp.int32, (n, n), 0)
    cols = lax.broadcasted_iota(jnp.int32, (n, n), 1)
    allowed = (cols <= rows) & (cols < len_ref[0])
    for h in range(2):
        row = jnp.broadcast_to(base_ref[0, h : h + 1, :], (n, n))
        bias = pltpu.roll(row, 0, 1, stride=1, stride_axis=0)
        out_ref[h] = jnp.where(allowed, bias, -1000000000.0).astype(bf16)


def bias_of(length, base):
    pairs, _, n = base.shape
    return pl.pallas_call(
        bias_kernel,
        grid_spec=pltpu.PrefetchScalarGridSpec(
            num_scalar_prefetch=1,
            grid=(pairs,),
            in_specs=[pl.BlockSpec((1, 2, n), lambda i, l: (i, 0, 0))],
            out_specs=pl.BlockSpec((2, n, n), lambda i, l: (i, 0, 0)),
        ),
        out_shape=jax.ShapeDtypeStruct((2 * pairs, n, n), bf16),
        compiler_params=params(60),
        name="bias",
    )(length, base)


def softmax_of(q, k, bias):
    s = dot_nt(q, k) * 0.125 + bias.astype(f32)
    e = jnp.exp(s - jnp.max(s, axis=-1, keepdims=True))
    return e * (1.0 / jnp.sum(e, axis=-1, keepdims=True))


def attn_fwd_kernel(N, *refs):
    off_ref, x_ref, gain_ref, bias_ref = refs[:4]
    own, pieces = refs[4:8], refs[8 : 8 + N]
    h_ref, qkv_ref, c_ref, wout_ref, w_s, sem = refs[8 + N :]
    width = x_ref.shape[1]
    unit = min(piece.shape[0] for piece in pieces)
    first = pl.multiple_of(off_ref[N] * unit, unit)
    for j in range(4):
        w_s[pl.ds(first, own[j].shape[0]), j * width : (j + 1) * width] = own[j][...]
    for p, piece in enumerate(pieces):
        start = pl.multiple_of(off_ref[p] * unit, unit)
        w_s[pl.ds(start, piece.shape[0]), :] = piece[...]
    out = pltpu.make_async_copy(w_s, wout_ref, sem)
    out.start()
    x = x_ref[...].astype(f32)
    scale = lax.rsqrt(jnp.mean(x * x, axis=-1, keepdims=True) + eps)
    h_ref[...] = (x * scale * gain_ref[...]).astype(bf16)
    step = width // 2

    def project(i, carry):
        cut = pl.ds(pl.multiple_of(i * step, step), step)
        qkv_ref[:, cut] = dot_nn(h_ref[...], w_s[:, cut]).astype(bf16)
        return carry

    lax.fori_loop(0, 3 * width // step, project, 0)

    def pair(i, carry):
        def at(j):
            return pl.ds(pl.multiple_of(j * width + i * LANES, LANES), LANES)

        q2, k2, v2 = qkv_ref[:, at(0)], qkv_ref[:, at(1)], qkv_ref[:, at(2)]
        heads = []
        for h in range(2):
            cut = slice(h * HEAD_DIM, (h + 1) * HEAD_DIM)
            p = softmax_of(q2[:, cut], k2[:, cut], bias_ref[2 * i + h]).astype(bf16)
            heads.append(dot_nn(p, v2[:, cut]).astype(bf16))
        c_ref[:, at(0)] = jnp.concatenate(heads, axis=1)
        return carry

    lax.fori_loop(0, HEADS // 2, pair, 0)
    out.wait()


def attn_fwd(offsets, x, gain, bias, own, pieces):
    n, width = x.shape
    N = len(pieces)
    full = jax.ShapeDtypeStruct((n, width), bf16)
    return pl.pallas_call(
        functools.partial(attn_fwd_kernel, N),
        in_specs=[smem(), vmem(), vmem(), vmem()] + [vmem()] * (4 + N),
        out_specs=[vmem(), vmem(), vmem(), hbm()],
        out_shape=[
            full,
            jax.ShapeDtypeStruct((n, 3 * width), bf16),
            full,
            pltpu.HBM((width, 4 * width), bf16),
        ],
        scratch_shapes=[pltpu.VMEM((width, 4 * width), bf16), pltpu.SemaphoreType.DMA],
        compiler_params=params(60),
        cost_estimate=short(),
        name="attn_fwd",
    )(offsets, x, gain, bias, *own, *pieces)


def mid_kernel(x_ref, gain_ref, c_ref, w_hbm, *refs):
    mid_ref, h_ref, w_s, sem = refs[-4:]
    width = x_ref.shape[1]
    load = pltpu.make_async_copy(w_hbm.at[:, pl.ds(3 * width, width)], w_s, sem)
    load.start()
    load.wait()
    mid = x_ref[...].astype(f32) + dot_nn(c_ref[...], w_s[...])
    scale = lax.rsqrt(jnp.mean(mid * mid, axis=-1, keepdims=True) + eps)
    mid_ref[...] = mid
    h_ref[...] = (mid * scale * gain_ref[...]).astype(bf16)


def mid_of(x, gain, context, weights, tokens):
    n, width = x.shape
    return pl.pallas_call(
        mid_kernel,
        in_specs=[vmem(), vmem(), vmem(), hbm()] + [anywhere()] * len(tokens),
        out_specs=[vmem(), vmem()],
        out_shape=[
            jax.ShapeDtypeStruct((n, width), f32),
            jax.ShapeDtypeStruct((n, width), bf16),
        ],
        scratch_shapes=[pltpu.VMEM((width, width), bf16), pltpu.SemaphoreType.DMA],
        compiler_params=params(60),
        cost_estimate=short(),
        name="middle",
    )(x, gain, context, weights, *tokens)


def attn_bwd_kernel(q_ref, k_ref, v_ref, bias_ref, dc_ref, *refs):
    dq_ref, dk_ref, dv_ref, diag_ref, token = refs[-5:]
    give(token)
    n = q_ref.shape[0]
    rows = lax.broadcasted_iota(jnp.int32, (n, n), 0)
    cols = lax.broadcasted_iota(jnp.int32, (n, n), 1)
    reverse = (rows + cols == n - 1).astype(bf16)
    for h in range(2):
        cut = slice(h * HEAD_DIM, (h + 1) * HEAD_DIM)
        q, k, v, dc = q_ref[:, cut], k_ref[:, cut], v_ref[:, cut], dc_ref[:, cut]
        p = softmax_of(q, k, bias_ref[h])
        dp = dot_nt(dc, v)
        ds = p * (dp - jnp.sum(p * dp, axis=-1, keepdims=True))
        low = ds.astype(bf16)
        dq_ref[:, cut] = (dot_nn(low, k) * 0.125).astype(bf16)
        dk_ref[:, cut] = (dot_tn(low, q) * 0.125).astype(bf16)
        dv_ref[:, cut] = dot_tn(p.astype(bf16), dc).astype(bf16)
        turned = pltpu.roll(dot_nn(reverse, low), 1, 1, stride=1, stride_axis=0)
        diag_ref[0, h : h + 1, :] = jnp.sum(turned, axis=0, keepdims=True)


def attn_bwd(qkv, bias, dc, tokens):
    n = qkv.shape[0]
    pairs = HEADS // 2
    blk = pl.BlockSpec((n, LANES), lambda i: (0, i))
    row = pl.BlockSpec((1, 2, n), lambda i: (i, 0, 0))
    full = jax.ShapeDtypeStruct((n, HEADS * HEAD_DIM), bf16)
    return pl.pallas_call(
        attn_bwd_kernel,
        grid=(pairs,),
        in_specs=[
            blk,
            pl.BlockSpec((n, LANES), lambda i: (0, pairs + i)),
            pl.BlockSpec((n, LANES), lambda i: (0, 2 * pairs + i)),
            pl.BlockSpec((2, n, n), lambda i: (i, 0, 0)),
            blk,
        ]
        + [anywhere()] * len(tokens),
        out_specs=[blk, blk, blk, row, token_spec()],
        out_shape=[full, full, full, jax.ShapeDtypeStruct((pairs, 2, n), f32), TOKEN],
        compiler_params=params(60),
        cost_estimate=short(),
        name="attn_bwd",
    )(qkv, qkv, qkv, bias, dc, *tokens)


def rows_of(refs):
    return refs[0][...] if len(refs) == 1 else jnp.concatenate([r[...] for r in refs], axis=0)


def ffn_kernel(shape, experts, groups, n_after, *refs):
    S, n_seq, first = len(shape), sum(shape), experts[0] == 0
    where_ref, pos_ref, aux_ref = refs[:3]
    refs = refs[3:]

    def sequences(parts):
        out, at = [], 0
        for count in shape:
            out.append(parts[at : at + count])
            at += count
        return out

    h2, ct = sequences(refs[:n_seq]), sequences(refs[n_seq : 2 * n_seq])
    refs = refs[2 * n_seq :]
    w_hbm = refs[:3]
    refs = refs[3 + n_after + (0 if first else 2) :]
    keeps, sends, (e_all, d_all, token) = refs[0], refs[1 : 1 + len(groups)], refs[1 + len(groups) : 4 + len(groups)]
    give(token)
    refs = refs[4 + len(groups) :]
    where_to = [(g, k) for g, size in enumerate(groups) for k in range(size)]
    if first:
        prob_ref, refs = refs[0], refs[1:]
    else:
        prob_ref = aux_ref
    w_v, x_s, c_s, gate_s, a_s, u_s, d_s, hid_s, da_s, du_s, o_s, eo_s, dx_s, sem_l, sem_s = refs
    n, width = pos_ref.shape[2], x_s.shape[1]
    loads = [[] for _ in experts]
    for i, e in enumerate(experts):
        for j in range(3):
            copy = pltpu.make_async_copy(w_hbm[j].at[e], w_v.at[i, j], sem_l.at[i, j])
            copy.start()
            loads[i].append(copy)
    lanes = lax.broadcasted_iota(jnp.int32, (n, LANES), 1)
    slot_lanes = lax.broadcasted_iota(jnp.int32, (CAP, LANES), 1)
    slots = lax.broadcasted_iota(jnp.int32, (CAP, n), 0)
    if first:
        for s in range(S):
            logits = jnp.where(lanes < EXPERTS, dot_nn(rows_of(h2[s]), aux_ref[...]), -1e30)
            ex = jnp.exp(logits - jnp.max(logits, axis=-1, keepdims=True))
            prob = ex / jnp.sum(ex, axis=-1, keepdims=True)
            high = prob.astype(bf16).astype(f32)
            rest = pltpu.roll(prob - high, EXPERTS, 1)
            prob_ref[s] = jnp.where(lanes < EXPERTS, high, rest).astype(bf16)
    half_w = width // 2
    core = where_ref[1]
    mine = pl.ds(pl.multiple_of(core * half_w, half_w), half_w)
    other = pl.ds(pl.multiple_of((1 - core) * half_w, half_w), half_w)
    const = math.sqrt(2.0 / math.pi)
    pending = {}

    def store(key, i, j, src, dst):
        copy = pltpu.make_async_copy(src, dst, sem_s.at[i, j])
        copy.start()
        pending.setdefault(key, []).append(copy)

    def settle(key):
        for copy in pending.pop(key, []):
            copy.wait()

    for i, e in enumerate(experts):
        wg, wu, wd = w_v.at[i, 0], w_v.at[i, 1], w_v.at[i, 2]
        for s in range(S):
            rows = slice(s * CAP, (s + 1) * CAP)
            hot = (slots == pos_ref[s, e : e + 1, :]).astype(bf16)
            x_s[rows, :] = dot_nn(hot, rows_of(h2[s])).astype(bf16)
            c_s[rows, :] = dot_nn(hot, rows_of(ct[s])).astype(bf16)
            picked = dot_nn(hot, prob_ref[s])
            gate_s[rows, :] = jnp.broadcast_to(
                picked[:, e : e + 1] + picked[:, EXPERTS + e : EXPERTS + e + 1], (CAP, LANES)
            )
        loads[i][0].wait()
        a_s[...] = dot_nt(x_s[...], wg[...])
        loads[i][1].wait()
        u_s[...] = dot_nt(x_s[...], wu[...])
        loads[i][2].wait()
        d_s[...] = dot_nt(c_s[...], wd[...])
        settle("dx")
        for s in range(S):
            rows = slice(s * CAP, (s + 1) * CAP)
            a, u, d0, gate = a_s[rows, :], u_s[rows, :], d_s[rows, :], gate_s[rows, 0:1]
            t = jnp.tanh(const * (a + 0.044715 * a * a * a))
            half = 0.5 * (1.0 + t)
            act = a * half
            slope = half + 0.5 * a * (1.0 - t * t) * (const * (1.0 + 3 * 0.044715 * a * a))
            hid = act * u
            dg = jnp.sum(hid * d0, axis=-1, keepdims=True)
            hid_s[rows, :] = (gate * hid).astype(bf16)
            dh = gate * d0
            da_s[rows, :] = (dh * u * slope).astype(bf16)
            du_s[rows, :] = (dh * act).astype(bf16)
            dx_s[rows, width:] = jnp.where(slot_lanes == e, dg, 0.0).astype(bf16)
        for j, (left, right) in enumerate(((hid_s, c_s), (da_s, x_s), (du_s, x_s))):
            settle(j)
            o_s[j] = dot_tn(left[...], right[...]).astype(bf16)
            g, k = where_to[3 * i + j]
            store(j, i, 2 * j, o_s.at[j, :, other], sends[g].at[k])
            store(j, i, 2 * j + 1, o_s.at[j, :, mine], keeps.at[3 * i + j])
        settle("eo")
        eo_s[...] = dot_nn(hid_s[...], wd[...]).astype(bf16)
        for s in range(S):
            rows = pl.ds(s * CAP, CAP)
            store("eo", i, 6 + s, eo_s.at[rows], e_all.at[s, pl.ds(e * CAP, CAP)])
        dx_s[:, :width] = (dot_nn(da_s[...], wg[...]) + dot_nn(du_s[...], wu[...])).astype(bf16)
        for s in range(S):
            rows = pl.ds(s * CAP, CAP)
            store("dx", i, 6 + S + s, dx_s.at[rows], d_all.at[s, pl.ds(e * CAP, CAP)])
    for key in list(pending):
        settle(key)


def ffn(experts, groups, core, pos, aux, h2, ct, weights, chain, after):
    shape = tuple(len(blocks) for blocks in h2)
    S, n_seq, N = len(shape), sum(shape), len(experts)
    n = pos.shape[2]
    cols, width = weights[0].shape[1:]
    rows = S * CAP
    first = experts[0] == 0
    shapes = [pltpu.HBM((k, cols, width // 2), bf16) for k in (3 * N,) + groups] + [
        pltpu.HBM((S, EXPERTS * CAP, width), bf16),
        pltpu.HBM((S, EXPERTS * CAP, width + LANES), bf16),
        TOKEN,
    ]
    M = 1 + len(groups)
    specs = [hbm()] * (M + 2) + [vmem()]
    if first:
        shapes.append(jax.ShapeDtypeStruct((S, n, LANES), bf16))
        specs.append(vmem())
    at = 6 + 2 * n_seq + len(after)
    return pl.pallas_call(
        functools.partial(ffn_kernel, shape, experts, groups, len(after)),
        in_specs=[smem()]
        + [vmem()] * (2 + 2 * n_seq)
        + [hbm()] * 3
        + [anywhere()] * len(after)
        + [hbm()] * (0 if first else 2),
        out_specs=specs,
        out_shape=shapes,
        input_output_aliases={} if first else {at: M, at + 1: M + 1},
        scratch_shapes=[pltpu.VMEM((N, 3, cols, width), bf16)]
        + [pltpu.VMEM((rows, width), bf16)] * 2
        + [pltpu.VMEM((rows, LANES), f32)]
        + [pltpu.VMEM((rows, cols), f32)] * 3
        + [pltpu.VMEM((rows, cols), bf16)] * 3
        + [pltpu.VMEM((3, cols, width), bf16)]
        + [pltpu.VMEM((rows, width), bf16), pltpu.VMEM((rows, width + LANES), bf16)]
        + [pltpu.SemaphoreType.DMA((N, 3)), pltpu.SemaphoreType.DMA((N, 6 + 2 * S))],
        compiler_params=params(60),
        cost_estimate=short(),
        name=f"ffn{experts[0]}",
    )(
        core,
        pos,
        aux,
        *[b for blocks in h2 for b in blocks],
        *[b for blocks in ct for b in blocks],
        *weights,
        *after,
        *([] if first else [pin(x) for x in chain]),
    )


def combine_kernel(me_ref, pos_ref, src_ref, *refs):
    out, token = refs[-2:]
    give(token)
    n = pos_ref.shape[0]
    lanes = lax.broadcasted_iota(jnp.int32, (n, EXPERTS * CAP), 1)
    hot = lanes == pos_ref[:, 0:1]
    for e in range(1, EXPERTS):
        hot = hot | (lanes == pos_ref[:, e : e + 1])
    out[...] = dot_nn(hot.astype(bf16), src_ref[...]).astype(bf16)


def combine(me, pos_col, src, tokens):
    S, n = pos_col.shape[:2]
    width = src.shape[2]
    out, token = pl.pallas_call(
        combine_kernel,
        grid_spec=pltpu.PrefetchScalarGridSpec(
            num_scalar_prefetch=1,
            grid=(S,),
            in_specs=[
                pl.BlockSpec((None, n, LANES), lambda s, me: (s, 0, 0)),
                pl.BlockSpec((None, EXPERTS * CAP, width), lambda s, me: (s, 0, 0)),
            ]
            + [anywhere()] * len(tokens),
            out_specs=[
                pl.BlockSpec((None, n, width), lambda s, me: (jnp.bitwise_xor(me[0], s), 0, 0)),
                token_spec(),
            ],
        ),
        out_shape=[jax.ShapeDtypeStruct((S, n, width), bf16), TOKEN],
        compiler_params=params(60),
        cost_estimate=short(),
        name="combine",
    )(me, pos_col, src, *tokens)
    return out, [token]


PANEL = 512


def split_rows(src, core, S, keep, send, sems):
    half, panels = src.shape[0] // (2 * S), src.shape[1] // PANEL
    copies = []
    for m in range(S):
        for c, dest in enumerate((keep, send)):
            who = core if c == 0 else 1 - core
            start = pl.multiple_of((2 * m + who) * half, half)
            for p in range(panels):
                copies.append(
                    pltpu.make_async_copy(
                        src.at[pl.ds(start, half), pl.ds(p * PANEL, PANEL)],
                        dest.at[m, pl.ds(p * half, half)],
                        sems.at[(2 * m + c) * panels + p],
                    )
                )
                copies[-1].start()
    return copies


def hi_lo(x):
    high = x.astype(bf16)
    return high, (x - high.astype(f32)).astype(bf16)


def sum_columns(x):
    ones = jnp.ones((x.shape[0], LANES), bf16)
    high, rest = hi_lo(x)
    return dot_tn(high, ones) + dot_tn(rest, ones)


def back_mid_kernel(S, *refs):
    core_ref, mid_ref, ct_ref, gain_ref, h2_ref, wr_ref, c_ref, wo_hbm = refs[:8]
    parts_ref = refs[8]
    dmid_ref, dc_ref, extra_ref, keep, send, token, wo, go_s, sem_w, sems = refs[-10:]
    give(token)
    n, width = mid_ref.shape
    load = pltpu.make_async_copy(wo_hbm.at[:, pl.ds(3 * width, width)], wo, sem_w)
    load.start()

    dh = parts_ref[0].astype(f32)
    for m in range(1, S):
        dh = dh + parts_ref[m].astype(f32)
    lanes = lax.broadcasted_iota(jnp.int32, (n, LANES), 1)
    logits = jnp.where(lanes < EXPERTS, dot_nn(h2_ref[...], wr_ref[...]), -1e30)
    ex = jnp.exp(logits - jnp.max(logits, axis=-1, keepdims=True))
    prob = ex / jnp.sum(ex, axis=-1, keepdims=True)
    drouter = dh[:, width:]
    dlogit = prob * (drouter - jnp.sum(prob * drouter, axis=-1, keepdims=True))
    high, rest = hi_lo(dlogit)
    dh2 = dh[:, :width] + dot_nt(high, wr_ref[...]) + dot_nt(rest, wr_ref[...])
    grad_router = dot_tn(h2_ref[...], high) + dot_tn(h2_ref[...], rest)
    mid = mid_ref[...]
    scale = lax.rsqrt(jnp.mean(mid * mid, axis=-1, keepdims=True) + eps)
    weighted = dh2 * gain_ref[...]
    dz = scale * weighted - mid * (scale * scale * scale) * jnp.mean(
        mid * weighted, axis=-1, keepdims=True
    )
    dmid = ct_ref[...].astype(f32) + dz
    dmid_ref[...] = dmid
    low = dmid.astype(bf16)
    go_s[...] = dot_tn(c_ref[...], low).astype(bf16)
    copies = split_rows(go_s, core_ref[0], S, keep, send, sems)
    load.wait()
    dc_ref[...] = dot_nt(low, wo[...]).astype(bf16)
    wide = lax.broadcasted_iota(jnp.int32, (width, LANES), 1)
    gain_column = sum_columns(dh2 * mid * scale)
    extra_ref[...] = jnp.where(wide == 1, gain_column, pltpu.roll(grad_router, 2, 1))
    for copy in copies:
        copy.wait()


def back_mid(core, S, mid, ct, gain, h2, router_w, context, out_w, parts, tokens):
    n, width = mid.shape
    panels = width // PANEL
    part = pltpu.HBM((S, panels * width // (2 * S), PANEL), bf16)
    return pl.pallas_call(
        functools.partial(back_mid_kernel, S),
        in_specs=[smem()]
        + [vmem()] * 6
        + [hbm()]
        + [vmem()]
        + [anywhere()] * len(tokens),
        out_specs=[vmem(), vmem(), vmem(), hbm(), hbm(), vmem()],
        out_shape=[
            jax.ShapeDtypeStruct((n, width), f32),
            jax.ShapeDtypeStruct((n, width), bf16),
            jax.ShapeDtypeStruct((width, LANES), f32),
            part,
            part,
            TOKEN,
        ],
        scratch_shapes=[
            pltpu.VMEM((width, width), bf16),
            pltpu.VMEM((width, width), bf16),
            pltpu.SemaphoreType.DMA,
            pltpu.SemaphoreType.DMA((2 * S * panels,)),
        ],
        compiler_params=params(60),
        cost_estimate=short(),
        name="back_mid",
    )(core, mid, ct, gain, h2, router_w, context, out_w, parts, *tokens)


def back_in_kernel(S, *refs):
    core_ref, x_ref, gain_ref, h_ref, dq_ref, dk_ref, dv_ref, diag_ref, hot_ref = refs[:9]
    extra_ref, dmid_ref, w_hbm = refs[9:12]
    dx_ref, keep, send, token, w_s, g_s, sem_w, sems = refs[-8:]
    give(token)
    n, width = x_ref.shape
    load = pltpu.make_async_copy(w_hbm.at[:, pl.ds(0, 3 * width)], w_s, sem_w)
    load.start()
    for j, d_ref in enumerate((dq_ref, dk_ref, dv_ref)):
        g_s[:, j * width : (j + 1) * width] = dot_tn(h_ref[...], d_ref[...]).astype(bf16)
    load.wait()
    dh = dot_nt(dq_ref[...], w_s[:, :width])
    dh = dh + dot_nt(dk_ref[...], w_s[:, width : 2 * width])
    dh = dh + dot_nt(dv_ref[...], w_s[:, 2 * width :])
    x = x_ref[...].astype(f32)
    scale = lax.rsqrt(jnp.mean(x * x, axis=-1, keepdims=True) + eps)
    wide = lax.broadcasted_iota(jnp.int32, (width, LANES), 1)
    extra = jnp.where(wide == 0, sum_columns(dh * x * scale), extra_ref[...])
    end = 3 * width + LANES
    g_s[:, 3 * width : end] = jnp.where(wide < 2 + EXPERTS, extra, 0.0).astype(bf16)
    g_s[:, end:] = jnp.zeros((width, PANEL - LANES), bf16)
    diag = jnp.concatenate(
        [jnp.zeros((8, n), f32), diag_ref[...], jnp.zeros((LANES - 8 - HEADS, n), f32)], axis=0
    )
    high, rest = hi_lo(diag)
    table = dot_nt(hot_ref[...], high) + dot_nt(hot_ref[...], rest)
    part, count = width // S, BUCKETS // S
    places = lax.broadcasted_iota(jnp.int32, (16, BUCKETS), 0)
    buckets = lax.broadcasted_iota(jnp.int32, (16, BUCKETS), 1)
    high, rest = hi_lo(table)
    for s in range(S):
        pick = ((places < count) & (buckets == places + s * count)).astype(bf16)
        rows = dot_nn(pick, high) + dot_nn(pick, rest)
        rows = rows + g_s[s * part : s * part + 16, 3 * width : end].astype(f32)
        g_s[s * part : s * part + 16, 3 * width : end] = rows.astype(bf16)
    copies = split_rows(g_s, core_ref[0], S, keep, send, sems)
    weighted = dh * gain_ref[...]
    dz = scale * weighted - x * (scale * scale * scale) * jnp.mean(
        x * weighted, axis=-1, keepdims=True
    )
    dx_ref[...] = (dz + dmid_ref[...]).astype(bf16)
    for copy in copies:
        copy.wait()


def back_in(core, S, x, gain, h1, dq, dk, dv, diag, hot, extra, dmid, qkv_w, tokens):
    n, width = x.shape
    cols = 3 * width + PANEL
    panels = cols // PANEL
    part = pltpu.HBM((S, panels * width // (2 * S), PANEL), bf16)
    return pl.pallas_call(
        functools.partial(back_in_kernel, S),
        in_specs=[smem()] + [vmem()] * 10 + [hbm()] + [anywhere()] * len(tokens),
        out_specs=[vmem(), hbm(), hbm(), vmem()],
        out_shape=[jax.ShapeDtypeStruct((n, width), bf16), part, part, TOKEN],
        scratch_shapes=[
            pltpu.VMEM((width, 3 * width), bf16),
            pltpu.VMEM((width, cols), bf16),
            pltpu.SemaphoreType.DMA,
            pltpu.SemaphoreType.DMA((2 * S * panels,)),
        ],
        compiler_params=params(60),
        cost_estimate=short(),
        name="back_in",
    )(core, x, gain, h1, dq, dk, dv, diag, hot, extra, dmid, qkv_w, *tokens)


def wave_kernel(shapes_in, shapes_out, *refs):
    place_ref = refs[0]
    line, core = place_ref[0], place_ref[1]
    inner = (line == 1) | (line == 2)
    get = dict(zip(shapes_in, refs[1:]))
    put = dict(zip(shapes_out, refs[len(refs) - len(shapes_out) :]))
    give(put["token"])

    def add(a, b):
        return (get[a][...].astype(f32) + get[b][...].astype(f32)).astype(bf16)

    if "mid" in put:
        put["mid"][...] = add("s0", "got_pair")
    if "core" in put:
        put["core"][...] = jnp.where(inner, get["pair"][...], get["got_pair"][...])
    new = None
    if "keep" in get:
        new = add("keep", "recv") if "recv" in get else get["keep"][...]
    full = add("mid", "got_mid") if "mid" in get else None
    if new is not None:
        put["s0"][...] = new
    if "pair" in put:
        if new is None or full is None:
            put["pair"][...] = full if new is None else new
        else:
            put["pair"][...] = jnp.where(inner, full, new)
    if "final" in put:
        a, b = get["core"][...].astype(f32), get["got_core"][...].astype(f32)
        half = a.shape[1]
        put["final"][:, :half] = jnp.where(core == 0, a, b)
        put["final"][:, half:] = jnp.where(core == 0, b, a)


class Sums:
    def __init__(self, size, place):
        self.size, self.place = size, place
        self.line = size // 2 == 4
        self.queues = [[], []]
        self.state = [{}, {}]
        self.ids = [{}, {}]
        self.turn = 0
        self.added = 0
        self.final = None
        self.targets = {}
        self.last = []

    def add(self, keep, k, recv, j, name, expert):
        if self.line:
            self.queues[self.added % 2].append((keep, k, recv, j, name, expert))
            self.added += 1
            return
        mine = line_sum((keep[k].astype(f32) + recv[j].astype(f32)).astype(bf16), self.size)
        other = swap_core(mine, self.size)
        first = self.place[1] == 0
        whole = jnp.concatenate([jnp.where(first, mine, other), jnp.where(first, other, mine)], 1)
        if name not in self.targets:
            self.targets[name] = jnp.zeros((EXPERTS,) + whole.shape, f32)
        self.targets[name] = self.targets[name].at[expert].set(whole.astype(f32))

    def busy(self):
        return any(self.queues) or any(self.state) or self.final is not None

    def step(self, more=()):
        self.last = self.last + list(more)
        stream = self.turn
        self.turn = 1 - stream
        queue, state, ids = self.queues[stream], self.state[stream], self.ids[stream]
        rep_axis = "rep"
        ins, outs = {}, []
        if "s0" in state or "pair" in state:
            pairs = line_perm([(0, 1), (1, 0), (2, 3), (3, 2)])
            ins["got_pair"] = lax.ppermute(state["pair"], rep_axis, pairs)
        if "mid" in state:
            ins["mid"] = state["mid"]
            ins["got_mid"] = lax.ppermute(state["mid"], rep_axis, line_perm([(1, 2), (2, 1)]))
        new_ids = {}
        if "in" in ids:
            ins["s0"] = state["s0"]
            outs.append("mid")
            new_ids["mid"] = ids["in"]
        if "out" in ids:
            ins["pair"] = state["pair"]
            outs.append("core")
        if "mid" in ids:
            new_ids["out"] = ids["mid"]
        if queue:
            keep, k, recv, j, name, expert = queue.pop(0)
            ins["keep"] = (keep, k)
            if recv is not None:
                ins["recv"] = (recv, j)
            outs.append("s0")
            new_ids["in"] = (name, expert)
        if "in" in new_ids or "out" in new_ids:
            outs.append("pair")
        if self.final is not None:
            value, (name, expert) = self.final
            ins["core"] = value
            ins["got_core"] = swap_core(value, self.size)
            outs.append("final")
        if not outs:
            self.state[stream] = {}
            return
        result = self.kernel(ins, outs, self.final[1] if self.final is not None else None)
        if self.final is not None:
            self.targets[self.final[1][0]] = result["final"]
        self.final = (result["core"], ids["out"]) if "core" in outs else None
        self.last = [result["token"]]
        self.state[stream] = {key: result[key] for key in ("s0", "mid", "pair") if key in outs}
        self.ids[stream] = new_ids

    def kernel(self, ins, outs, final):
        arrays, specs = [], []
        rows, cols = next(
            (x[0].shape[1:] if isinstance(x, tuple) else x.shape) for x in ins.values()
        )
        steps = max(g for g in (1, 2, 4) if rows % (16 * g) == 0)
        spec = pl.BlockSpec((rows // steps, cols), lambda r: (r, 0))
        for x in ins.values():
            if isinstance(x, tuple):
                arrays.append(pin(x[0]))
                specs.append(
                    pl.BlockSpec((None, rows // steps, cols), lambda r, k=x[1]: (k, r, 0))
                )
            else:
                arrays.append(pin(x))
                specs.append(spec)
        shape = pltpu.HBM((rows, cols), bf16)
        out_specs, out_shapes, extra, aliases = [], [], [], {}
        for i, key in enumerate(outs):
            if key == "final":
                name, expert = final
                out_specs.append(
                    pl.BlockSpec((None, rows // steps, 2 * cols), lambda r: (expert, r, 0))
                )
                count = EXPERTS if name in ("gate", "up", "down") else 1
                out_shapes.append(pltpu.HBM((count, rows, 2 * cols), f32))
                if name in self.targets:
                    extra.append(pin(self.targets[name]))
                    aliases[1 + len(arrays)] = i
            else:
                out_specs.append(spec)
                out_shapes.append(shape)
        values = pl.pallas_call(
            functools.partial(wave_kernel, tuple(ins), tuple(outs) + ("token",)),
            grid=(steps,),
            in_specs=[smem()] + specs + [anywhere()] * (len(extra) + len(self.last)),
            out_specs=out_specs + [token_spec()],
            out_shape=out_shapes + [TOKEN],
            input_output_aliases=aliases,
            compiler_params=params(60),
            cost_estimate=short(),
            name="wave",
        )(self.place, *arrays, *extra, *self.last)
        return dict(zip(tuple(outs) + ("token",), values))


def swap_core(x, size):
    return lax.ppermute(x, "rep", [(i, i ^ 1) for i in range(size)])


def swap_shard(x, size, mask):
    return lax.ppermute(x, "shard", [(i, i ^ mask) for i in range(size)])


def line_perm(pairs):
    return [(2 * a + c, 2 * b + c) for a, b in pairs for c in range(2)]


def after(x, *others):
    return lax.optimization_barrier((x,) + others)[0]


def relay_gather(x, S):
    if S != 4:
        return [[x]] + [[swap_shard(x, S, m)] for m in range(1, S)]
    cut = x.shape[0] // 2
    one, two = swap_shard(x, S, 1), swap_shard(x, S, 2)
    return [[x], [one], [two], [swap_shard(one[:cut], S, 2), swap_shard(two[cut:], S, 1)]]


def line_sum(x, size):
    n = size // 2
    h = n // 2
    line = lax.axis_index("rep") // 2
    for k in range(h - 1):
        x = x + lax.ppermute(x, "rep", line_perm([(k, k + 1), (n - 1 - k, n - 2 - k)]))
    x = x + lax.ppermute(x, "rep", line_perm([(h - 1, h), (h, h - 1)]))
    for k in reversed(range(h - 1)):
        got = lax.ppermute(x, "rep", line_perm([(k + 1, k), (n - 2 - k, n - 1 - k)]))
        x = jnp.where((line == k) | (line == n - 1 - k), got, x)
    return x


def deal_out(x):
    return lax.all_to_all(x, "shard", 0, 0, tiled=True)


def bucket_of(distance):
    bucket = jnp.minimum(distance, 16)
    for border in bucket_edges:
        bucket = bucket + (distance >= border).astype(jnp.int32)
    return bucket


def slot_positions(routes, order, lengths):
    n = order.shape[1]
    valid = jnp.arange(n, dtype=jnp.int32)[None, :] < lengths[:, None]
    experts = jnp.arange(EXPERTS, dtype=jnp.int32)
    hits = (routes[:, :, :, None] == experts) & valid[:, :, None, None]
    hits = hits.reshape(routes.shape[0], n, 2 * EXPERTS)
    before = (order[:, None, :] < order[:, :, None]).astype(bf16)
    count = jnp.einsum("stk,sut->sku", hits.astype(bf16), before, preferred_element_type=f32)
    total = jnp.sum(hits[:, :, :EXPERTS].astype(f32), axis=1)
    hits = jnp.swapaxes(hits, 1, 2)
    first, second = count[:, :EXPERTS], count[:, EXPERTS:] + total[:, :, None]
    slot = jnp.where(
        hits[:, :EXPERTS], first, jnp.where(hits[:, EXPERTS:], second, float(2 * CAP + n))
    )
    return jnp.where(slot < CAP, slot, -1.0).astype(jnp.int32)


def shards(
    R,
    S,
    tokens,
    cotangent,
    lengths,
    sequence_deal,
    routes,
    fill_order,
    norm_attn,
    w_query,
    w_key,
    w_value,
    w_out,
    rel_bias,
    norm_ffn,
    w_router,
    w_gate,
    w_up,
    w_down,
):
    me = lax.axis_index("shard")
    rep = lax.axis_index("rep")
    core = rep % 2
    line = rep // 2
    x_low, ct_low = tokens[0], cotangent[0]
    n, width = x_low.shape
    part = width // S
    half = part // 2
    group = jnp.arange(S, dtype=jnp.int32)

    dense = (w_query, w_key, w_value, w_out)
    stack = jnp.where(
        core == 0,
        jnp.concatenate([w[:half] for w in dense], axis=1),
        jnp.concatenate([w[half:] for w in dense], axis=1),
    )
    blocks = relay_gather(stack, S)
    count = len(blocks[-1])
    pieces, places = [], []
    for m in range(1, S):
        place = 2 * count * (me ^ m)
        each = count // len(blocks[m])
        pieces += blocks[m]
        places += [place + count * core + j * each for j in range(len(blocks[m]))]
        for j, block in enumerate(blocks[m]):
            pieces.append(swap_core(block, R))
            places.append(place + count * (1 - core) + j * each)
    offsets = jnp.stack(places + [2 * count * me]).astype(jnp.int32)
    ct_all = relay_gather(after(ct_low, *blocks[-1]), S)

    bias_flat = jnp.pad(rel_bias.reshape(-1), (0, part - rel_bias.size))
    small = jnp.concatenate(
        [norm_attn[:, None], norm_ffn[:, None], w_router, bias_flat[:, None]], axis=1
    )
    small = jnp.pad(small, ((0, n - part), (0, 0)))
    plan = jnp.concatenate([routes[0], fill_order[0][:, None]], axis=1).astype(bf16)
    small = jnp.concatenate([small, plan], axis=1)
    small = after(small, blocks[1][0])
    small_all = deal_out(jnp.broadcast_to(small[None], (S,) + small.shape))
    plan_all = small_all[:, :, 3 + EXPERTS :]
    small_all = small_all[:, :part]
    gain_one = small_all[:, :, 0].reshape(-1).astype(f32)
    gain_two = small_all[:, :, 1].reshape(-1).astype(f32)
    router_w = small_all[:, :, 2 : 2 + EXPERTS].reshape(width, EXPERTS)
    bias_table = small_all[:, : rel_bias.size, 2 + EXPERTS].reshape(BUCKETS, HEADS)

    length = lax.dynamic_slice_in_dim(lengths[0], me, 1, 0)

    turned = jnp.arange(n, dtype=jnp.int32)
    hot = (bucket_of((n - turned) % n)[None, :] == jnp.arange(BUCKETS)[:, None]).astype(bf16)
    base = dot_tn(bias_table, hot).reshape(HEADS // 2, 2, n)

    bias = bias_of(length, base)
    normed_low, qkv, context, dense_w = attn_fwd(offsets, x_low, gain_one[None], bias, dense, pieces)
    ct_tokens = [ct_all[m][0] for m in range(1, 3)]
    middle, ffn_in = mid_of(x_low, gain_two[None], context, dense_w, ct_tokens)

    plan_all = after(plan_all, ffn_in).astype(jnp.int32)
    deal = sequence_deal[0]
    row_of = jnp.sum(group[:, None] * (deal[:, None] == group[None, :]).astype(jnp.int32), axis=0)
    homes = me ^ group
    plans = jnp.take(plan_all, jnp.take(row_of, homes), axis=0)
    pos = slot_positions(plans[:, :, :2], plans[:, :, 2], jnp.take(lengths[0], homes))

    h2_all = relay_gather(ffn_in, S)
    router_pad = jnp.pad(router_w, ((0, 0), (0, LANES - EXPERTS)))
    core_one = core.reshape(1).astype(jnp.int32)
    place = jnp.stack([line, core]).astype(jnp.int32)
    me_one = me.reshape(1).astype(jnp.int32)
    where = jnp.stack([me, core]).astype(jnp.int32)
    weights = [pin(w) for w in (jnp.swapaxes(w_gate, 1, 2), jnp.swapaxes(w_up, 1, 2), w_down)]
    sums = Sums(R, place)
    chain, aux = (), router_pad
    for experts, groups in (((0, 1), (2, 2, 2)), ((2, 3), (2, 2, 2))):
        got = ffn(experts, groups, where, pos, aux, h2_all, ct_all, weights, chain, sums.last)
        M = 1 + len(groups)
        keep, sends, chain = got[0], got[1:M], got[M : M + 2]
        sums.last = [got[M + 2]]
        if experts[0] == 0:
            aux = got[-1]
        where_to = [(g, k) for g, size in enumerate(groups) for k in range(size)]
        recvs = [swap_core(x, R) for x in sends]
        for i, e in enumerate(experts):
            for j, name in enumerate(("down", "gate", "up")):
                g, k = where_to[3 * i + j]
                sums.add(keep, 3 * i + j, recvs[g], k, name, e)
        if experts[0] == 0 and sums.line:
            sums.step()
            sums.step()

    def run(steps, more=()):
        for _ in range(steps):
            if sums.line and sums.busy():
                sums.step(more)

    run(1)
    flat = jnp.arange(EXPERTS, dtype=jnp.int32) * CAP
    pos_col = jnp.swapaxes(jnp.where(pos < 0, -1, pos + flat[None, :, None]), 1, 2)
    pos_col = jnp.pad(pos_col, ((0, 0), (0, 0), (0, LANES - EXPERTS)))
    d_parts, sums.last = combine(me_one, pos_col, chain[1], sums.last)
    d_parts = deal_out(d_parts)
    run(3)

    dmid, dc, extra, keep, send, token = back_mid(
        core_one, S, middle, ct_low, gain_two[None], ffn_in, router_pad, context, dense_w, d_parts, sums.last
    )
    recv = swap_core(send, R)
    dq, dk, dv, diag, token = attn_bwd(qkv, bias, dc, [token])
    sums.last = [token]
    run(2)
    grad_x, keep_in, send, token = back_in(
        core_one, S, x_low, gain_one[None], normed_low, dq, dk, dv, diag.reshape(HEADS, n), hot, extra, dmid, dense_w, sums.last
    )
    sums.last = [token]

    recv_in = swap_core(send, R)
    run(1)
    halves = jnp.concatenate(
        [
            (keep_in.astype(f32) + recv_in.astype(f32)).astype(bf16),
            (keep.astype(f32) + recv.astype(f32)).astype(bf16),
        ],
        axis=1,
    )
    run(1, [halves])
    owned = jnp.sum(deal_out(halves).astype(f32), axis=0).astype(bf16)
    rows, cut = owned.shape[0], weights[0].shape[1]
    if sums.line:
        owned = jnp.pad(owned, ((0, 2 * cut - rows), (0, 0)))[None]
        run(1)
        sums.add(owned[:, :cut], 0, None, 0, "dense0", 0)
        sums.add(owned[:, cut:], 0, None, 0, "dense1", 0)
    else:
        owned = line_sum(owned, R)
        other = swap_core(owned, R)
        owned = jnp.concatenate(
            [jnp.where(core == 0, owned, other), jnp.where(core == 0, other, owned)], axis=1
        ).astype(f32)
    run(1)
    out_parts, sums.last = combine(me_one, pos_col, chain[0], sums.last)
    out_parts = deal_out(out_parts)
    run(4)
    result = (middle + jnp.sum(out_parts.astype(f32), axis=0)).astype(bf16)
    run(1, [result])
    run(100)
    if sums.line:
        owned = jnp.concatenate([sums.targets["dense0"][0], sums.targets["dense1"][0]], axis=0)

    def matrix(first, count):
        x = owned[first * half : (first + count) * half].reshape(count, half, 2, PANEL)
        return jnp.transpose(x, (2, 1, 0, 3)).reshape(part, count * PANEL)

    many = width // PANEL
    small = matrix(3 * many, 1)
    grad_in_w = [matrix(j * many, many) for j in range(3)]
    grad_out_w = matrix(3 * many + 1, many)
    return (
        result[None],
        grad_x[None],
        small[:, 0],
        *grad_in_w,
        grad_out_w,
        small[: BUCKETS // S, 8 : 8 + HEADS],
        small[:, 1],
        small[:, 2 : 2 + EXPERTS],
        jnp.swapaxes(sums.targets["gate"], 1, 2),
        jnp.swapaxes(sums.targets["up"], 1, 2),
        sums.targets["down"],
    )


def solution(mesh):
    R, S = mesh.shape["rep"], mesh.shape["shard"]
    rows = P(("rep", "shard"), None, None)
    mat = P("shard", None)
    return jax.shard_map(
        functools.partial(shards, R, S),
        mesh=mesh,
        in_specs=(rows, rows, P("rep", None), P("rep", None), rows, P(("rep", "shard"), None))
        + (P("shard"), mat, mat, mat, mat, mat, P("shard"), mat)
        + (P(None, None, "shard"), P(None, None, "shard"), P(None, "shard", None)),
        out_specs=(rows, rows, P("shard"), mat, mat, mat, mat, mat, P("shard"), mat)
        + (P(None, None, "shard"), P(None, None, "shard"), P(None, "shard", None)),
        check_vma=False,
    )
```

```python
import functools
import math

import jax
import jax.numpy as jnp
from jax import lax
from jax.experimental import pallas as pl
from jax.experimental.pallas import tpu as pltpu
from jax.sharding import PartitionSpec as P

HEADS = 16
HEAD_DIM = 64
EXPERTS = 4
BUCKETS = 32
CAP = 144
LANES = 128

eps = 1e-06
bucket_edges = [int(math.ceil(16.0 * 8.0 ** (level / 16.0))) for level in range(1, 16)]
bf16 = jnp.bfloat16
f32 = jnp.float32


def dot_nn(a, b):
    return lax.dot_general(a, b, (((1,), (0,)), ((), ())), preferred_element_type=f32)


def dot_nt(a, b):
    return lax.dot_general(a, b, (((1,), (1,)), ((), ())), preferred_element_type=f32)


def dot_tn(a, b):
    return lax.dot_general(a, b, (((0,), (0,)), ((), ())), preferred_element_type=f32)


def params(mib):
    return pltpu.CompilerParams(vmem_limit_bytes=mib * 1024 * 1024)


def vmem():
    return pl.BlockSpec(memory_space=pltpu.VMEM)


def anywhere():
    return pl.BlockSpec(memory_space=pl.ANY)


TOKEN = jax.ShapeDtypeStruct((8, LANES), f32)


def token_spec():
    return pl.BlockSpec((8, LANES), lambda *i: (0, 0))


def give(token):
    token[...] = jnp.zeros(token.shape, token.dtype)


def short():
    return pl.CostEstimate(flops=1, bytes_accessed=1, transcendentals=0)


def hbm():
    return pl.BlockSpec(memory_space=pltpu.HBM)


def pin(x):
    return pltpu.with_memory_space_constraint(x, pltpu.HBM)


def smem():
    return pl.BlockSpec(memory_space=pltpu.SMEM)


def softmax_of(q, k, bias):
    s = dot_nt(q, k) * 0.125 + bias.astype(f32)
    e = jnp.exp(s - jnp.max(s, axis=-1, keepdims=True))
    return e * (1.0 / jnp.sum(e, axis=-1, keepdims=True))


def attn_fwd_kernel(N, *refs):
    off_ref, len_ref, x_ref, gain_ref, gain2_ref, base_ref = refs[:6]
    own, pieces = refs[6:10], refs[10 : 10 + N]
    h_ref, qkv_ref, c_ref, mid_ref, h2_ref, wout_ref, bias_hbm, w_s, bias_ref, sem, sems = refs[10 + N :]
    n, width = x_ref.shape
    unit = min(piece.shape[0] for piece in pieces)
    copies = []
    first = pl.multiple_of(off_ref[N] * unit, unit)
    for j in range(4):
        dest = w_s.at[pl.ds(first, own[j].shape[0]), pl.ds(j * width, width)]
        copies.append(pltpu.make_async_copy(own[j], dest, sems.at[N + j]))
    for p, piece in enumerate(pieces):
        start = pl.multiple_of(off_ref[p] * unit, unit)
        copies.append(
            pltpu.make_async_copy(piece, w_s.at[pl.ds(start, piece.shape[0])], sems.at[p])
        )
    for copy in copies:
        copy.start()
    x = x_ref[...].astype(f32)
    scale = lax.rsqrt(jnp.mean(x * x, axis=-1, keepdims=True) + eps)
    h_ref[...] = (x * scale * gain_ref[...]).astype(bf16)
    rows = lax.broadcasted_iota(jnp.int32, (n, n), 0)
    cols = lax.broadcasted_iota(jnp.int32, (n, n), 1)
    allowed = (cols <= rows) & (cols < len_ref[0])
    for h in range(HEADS):
        row = jnp.broadcast_to(base_ref[h : h + 1, :], (n, n))
        turned = pltpu.roll(row, 0, 1, stride=1, stride_axis=0)
        bias_ref[h] = jnp.where(allowed, turned, -1000000000.0).astype(bf16)
    outs = [pltpu.make_async_copy(bias_ref, bias_hbm, sem.at[0])]
    outs.append(pltpu.make_async_copy(w_s, wout_ref, sem.at[1]))
    outs[0].start()
    for copy in copies:
        copy.wait()
    outs[1].start()
    step = width // 2

    def project(i, carry):
        cut = pl.ds(pl.multiple_of(i * step, step), step)
        qkv_ref[:, cut] = dot_nn(h_ref[...], w_s[:, cut]).astype(bf16)
        return carry

    lax.fori_loop(0, 3 * width // step, project, 0)

    def some_heads(i, carry):
        def at(j):
            return pl.ds(pl.multiple_of(j * width + i * 2 * LANES, LANES), 2 * LANES)

        q, k, v = qkv_ref[:, at(0)], qkv_ref[:, at(1)], qkv_ref[:, at(2)]
        heads = []
        for h in range(4):
            cut = slice(h * HEAD_DIM, (h + 1) * HEAD_DIM)
            p = softmax_of(q[:, cut], k[:, cut], bias_ref[4 * i + h]).astype(bf16)
            heads.append(dot_nn(p, v[:, cut]).astype(bf16))
        c_ref[:, at(0)] = jnp.concatenate(heads, axis=1)
        return carry

    lax.fori_loop(0, HEADS // 4, some_heads, 0)
    mid = x_ref[...].astype(f32) + dot_nn(c_ref[...], w_s[:, 3 * width :])
    scale = lax.rsqrt(jnp.mean(mid * mid, axis=-1, keepdims=True) + eps)
    mid_ref[...] = mid
    h2_ref[...] = (mid * scale * gain2_ref[...]).astype(bf16)
    for copy in outs:
        copy.wait()


def attn_fwd(offsets, length, x, gain, gain_two, base, own, pieces):
    n, width = x.shape
    N = len(pieces)
    full = jax.ShapeDtypeStruct((n, width), bf16)
    return pl.pallas_call(
        functools.partial(attn_fwd_kernel, N),
        in_specs=[smem(), smem(), vmem(), vmem(), vmem(), vmem()] + [anywhere()] * (4 + N),
        out_specs=[vmem()] * 5 + [hbm()] * 2,
        out_shape=[
            full,
            jax.ShapeDtypeStruct((n, 3 * width), bf16),
            full,
            jax.ShapeDtypeStruct((n, width), f32),
            full,
            pltpu.HBM((width, 4 * width), bf16),
            pltpu.HBM((HEADS, n, n), bf16),
        ],
        scratch_shapes=[
            pltpu.VMEM((width, 4 * width), bf16),
            pltpu.VMEM((HEADS, n, n), bf16),
            pltpu.SemaphoreType.DMA((2,)),
            pltpu.SemaphoreType.DMA((N + 4,)),
        ],
        compiler_params=params(60),
        cost_estimate=short(),
        name="attn_fwd",
    )(offsets, length, x, gain, gain_two, base, *own, *pieces)


def attn_bwd_kernel(q_ref, k_ref, v_ref, bias_ref, dc_ref, *refs):
    d_ref, diag_ref, token = refs[-3:]
    give(token)
    n = q_ref.shape[0]
    rows = lax.broadcasted_iota(jnp.int32, (n, n), 0)
    cols = lax.broadcasted_iota(jnp.int32, (n, n), 1)
    reverse = (rows + cols == n - 1).astype(bf16)
    for h in range(4):
        cut = slice(h * HEAD_DIM, (h + 1) * HEAD_DIM)
        q, k, v, dc = q_ref[:, cut], k_ref[:, cut], v_ref[:, cut], dc_ref[:, cut]
        p = softmax_of(q, k, bias_ref[h])
        dp = dot_nt(dc, v)
        ds = p * (dp - jnp.sum(p * dp, axis=-1, keepdims=True))
        low = ds.astype(bf16)
        d_ref[0, :, cut] = (dot_nn(low, k) * 0.125).astype(bf16)
        d_ref[1, :, cut] = (dot_tn(low, q) * 0.125).astype(bf16)
        d_ref[2, :, cut] = dot_tn(p.astype(bf16), dc).astype(bf16)
        turned = pltpu.roll(dot_nn(reverse, low), 1, 1, stride=1, stride_axis=0)
        diag_ref[0, h : h + 1, :] = jnp.sum(turned, axis=0, keepdims=True)


def attn_bwd(qkv, bias, dc, tokens):
    n = qkv.shape[0]
    steps = HEADS // 4
    blk = pl.BlockSpec((n, 2 * LANES), lambda i: (0, i))
    row = pl.BlockSpec((1, 4, n), lambda i: (i, 0, 0))
    return pl.pallas_call(
        attn_bwd_kernel,
        grid=(steps,),
        in_specs=[
            blk,
            pl.BlockSpec((n, 2 * LANES), lambda i: (0, steps + i)),
            pl.BlockSpec((n, 2 * LANES), lambda i: (0, 2 * steps + i)),
            pl.BlockSpec((4, n, n), lambda i: (i, 0, 0)),
            blk,
        ]
        + [anywhere()] * len(tokens),
        out_specs=[pl.BlockSpec((3, n, 2 * LANES), lambda i: (0, 0, i)), row, token_spec()],
        out_shape=[
            jax.ShapeDtypeStruct((3, n, HEADS * HEAD_DIM), bf16),
            jax.ShapeDtypeStruct((steps, 4, n), f32),
            TOKEN,
        ],
        compiler_params=params(60),
        cost_estimate=short(),
        name="attn_bwd",
    )(qkv, qkv, qkv, bias, dc, *tokens)


def rows_of(refs):
    return refs[0][...] if len(refs) == 1 else jnp.concatenate([r[...] for r in refs], axis=0)


def ffn_kernel(shape, experts, groups, n_after, *refs):
    S, n_seq, first = len(shape), sum(shape), experts[0] == 0
    where_ref, pos_ref, aux_ref = refs[:3]
    refs = refs[3:]

    def sequences(parts):
        out, at = [], 0
        for count in shape:
            out.append(parts[at : at + count])
            at += count
        return out

    h2, ct = sequences(refs[:n_seq]), sequences(refs[n_seq : 2 * n_seq])
    refs = refs[2 * n_seq :]
    w_hbm = refs[:3]
    refs = refs[3 + n_after + (0 if first else 2) :]
    keeps, sends, (e_all, d_all, token) = refs[0], refs[1 : 1 + len(groups)], refs[1 + len(groups) : 4 + len(groups)]
    give(token)
    refs = refs[4 + len(groups) :]
    where_to = [(g, k) for g, size in enumerate(groups) for k in range(size)]
    if first:
        prob_ref, refs = refs[0], refs[1:]
    else:
        prob_ref = aux_ref
    w_v, x_s, c_s, gate_s, hid_s, da_s, du_s, o_s, eo_s, dx_s, sem_l, sem_s = refs
    n, width = pos_ref.shape[2], x_s.shape[1]
    loads = [[] for _ in experts]
    for i, e in enumerate(experts):
        for j in range(3):
            copy = pltpu.make_async_copy(w_hbm[j].at[e], w_v.at[i, j], sem_l.at[i, j])
            copy.start()
            loads[i].append(copy)
    lanes = lax.broadcasted_iota(jnp.int32, (n, LANES), 1)
    slot_lanes = lax.broadcasted_iota(jnp.int32, (S * CAP, LANES), 1)
    slots = lax.broadcasted_iota(jnp.int32, (CAP, n), 0)
    if first:
        for s in range(S):
            logits = jnp.where(lanes < EXPERTS, dot_nn(rows_of(h2[s]), aux_ref[...]), -1e30)
            ex = jnp.exp(logits - jnp.max(logits, axis=-1, keepdims=True))
            prob = ex / jnp.sum(ex, axis=-1, keepdims=True)
            high = prob.astype(bf16).astype(f32)
            rest = pltpu.roll(prob - high, EXPERTS, 1)
            prob_ref[s] = jnp.where(lanes < EXPERTS, high, rest).astype(bf16)
    half_w = width // 2
    core = where_ref[1]
    mine = pl.ds(pl.multiple_of(core * half_w, half_w), half_w)
    other = pl.ds(pl.multiple_of((1 - core) * half_w, half_w), half_w)
    const = math.sqrt(2.0 / math.pi)
    pending = {}

    def store(key, i, j, src, dst):
        copy = pltpu.make_async_copy(src, dst, sem_s.at[i, j])
        copy.start()
        pending.setdefault(key, []).append(copy)

    def settle(key):
        for copy in pending.pop(key, []):
            copy.wait()

    for i, e in enumerate(experts):
        wg, wu, wd = w_v.at[i, 0], w_v.at[i, 1], w_v.at[i, 2]
        for s in range(S):
            rows = slice(s * CAP, (s + 1) * CAP)
            hot = (slots == pos_ref[s, e : e + 1, :]).astype(bf16)
            x_s[rows, :] = dot_nn(hot, rows_of(h2[s])).astype(bf16)
            c_s[rows, :] = dot_nn(hot, rows_of(ct[s])).astype(bf16)
            picked = dot_nn(hot, prob_ref[s])
            gate_s[rows, :] = jnp.broadcast_to(
                picked[:, e : e + 1] + picked[:, EXPERTS + e : EXPERTS + e + 1], (CAP, LANES)
            )
        for copy in loads[i]:
            copy.wait()
        settle("dx")
        cols, gate = hid_s.shape[1], gate_s[:, 0:1]
        dg = jnp.zeros(gate.shape, f32)
        for f in range(0, cols, 256):
            cut = slice(f, min(f + 256, cols))
            a = dot_nt(x_s[...], wg[cut, :])
            u = dot_nt(x_s[...], wu[cut, :])
            d0 = dot_nt(c_s[...], wd[cut, :])
            t = jnp.tanh(const * (a + 0.044715 * a * a * a))
            half = 0.5 * (1.0 + t)
            act = a * half
            slope = half + 0.5 * a * (1.0 - t * t) * (const * (1.0 + 3 * 0.044715 * a * a))
            hid = act * u
            dg = dg + jnp.sum(hid * d0, axis=-1, keepdims=True)
            hid_s[:, cut] = (gate * hid).astype(bf16)
            dh = gate * d0
            da_s[:, cut] = (dh * u * slope).astype(bf16)
            du_s[:, cut] = (dh * act).astype(bf16)
        dx_s[:, width:] = jnp.where(slot_lanes == e, dg, 0.0).astype(bf16)
        for j, (left, right) in enumerate(((hid_s, c_s), (da_s, x_s), (du_s, x_s))):
            settle(j)
            o_s[j] = dot_tn(left[...], right[...]).astype(bf16)
            g, k = where_to[3 * i + j]
            store(j, i, 2 * j, o_s.at[j, :, other], sends[g].at[k])
            store(j, i, 2 * j + 1, o_s.at[j, :, mine], keeps.at[3 * i + j])
        settle("eo")
        eo_s[...] = dot_nn(hid_s[...], wd[...]).astype(bf16)
        for s in range(S):
            rows = pl.ds(s * CAP, CAP)
            store("eo", i, 6 + s, eo_s.at[rows], e_all.at[s, pl.ds(e * CAP, CAP)])
        dx_s[:, :width] = (dot_nn(da_s[...], wg[...]) + dot_nn(du_s[...], wu[...])).astype(bf16)
        for s in range(S):
            rows = pl.ds(s * CAP, CAP)
            store("dx", i, 6 + S + s, dx_s.at[rows], d_all.at[s, pl.ds(e * CAP, CAP)])
    for key in list(pending):
        settle(key)


def ffn(experts, groups, core, pos, aux, h2, ct, weights, chain, after):
    shape = tuple(len(blocks) for blocks in h2)
    S, n_seq, N = len(shape), sum(shape), len(experts)
    n = pos.shape[2]
    cols, width = weights[0].shape[1:]
    rows = S * CAP
    first = experts[0] == 0
    shapes = [pltpu.HBM((k, cols, width // 2), bf16) for k in (3 * N,) + groups] + [
        pltpu.HBM((S, EXPERTS * CAP, width), bf16),
        pltpu.HBM((S, EXPERTS * CAP, width + LANES), bf16),
        TOKEN,
    ]
    M = 1 + len(groups)
    specs = [hbm()] * (M + 2) + [vmem()]
    if first:
        shapes.append(jax.ShapeDtypeStruct((S, n, LANES), bf16))
        specs.append(vmem())
    at = 6 + 2 * n_seq + len(after)
    return pl.pallas_call(
        functools.partial(ffn_kernel, shape, experts, groups, len(after)),
        in_specs=[smem()]
        + [vmem()] * (2 + 2 * n_seq)
        + [hbm()] * 3
        + [anywhere()] * len(after)
        + [hbm()] * (0 if first else 2),
        out_specs=specs,
        out_shape=shapes,
        input_output_aliases={} if first else {at: M, at + 1: M + 1},
        scratch_shapes=[pltpu.VMEM((N, 3, cols, width), bf16)]
        + [pltpu.VMEM((rows, width), bf16)] * 2
        + [pltpu.VMEM((rows, LANES), f32)]
        + [pltpu.VMEM((rows, cols), bf16)] * 3
        + [pltpu.VMEM((3, cols, width), bf16)]
        + [pltpu.VMEM((rows, width), bf16), pltpu.VMEM((rows, width + LANES), bf16)]
        + [pltpu.SemaphoreType.DMA((N, 3)), pltpu.SemaphoreType.DMA((N, 6 + 2 * S))],
        compiler_params=params(60),
        cost_estimate=short(),
        name=f"ffn{experts[0]}",
    )(
        core,
        pos,
        aux,
        *[b for blocks in h2 for b in blocks],
        *[b for blocks in ct for b in blocks],
        *weights,
        *after,
        *([] if first else [pin(x) for x in chain]),
    )


def combine_kernel(me_ref, pos_ref, src_ref, *refs):
    out, token = refs[-2:]
    give(token)
    n = pos_ref.shape[0]
    lanes = lax.broadcasted_iota(jnp.int32, (n, EXPERTS * CAP), 1)
    hot = lanes == pos_ref[:, 0:1]
    for e in range(1, EXPERTS):
        hot = hot | (lanes == pos_ref[:, e : e + 1])
    out[...] = dot_nn(hot.astype(bf16), src_ref[...]).astype(bf16)


def combine(me, pos_col, src, tokens):
    S, n = pos_col.shape[:2]
    width = src.shape[2]
    out, token = pl.pallas_call(
        combine_kernel,
        grid_spec=pltpu.PrefetchScalarGridSpec(
            num_scalar_prefetch=1,
            grid=(S,),
            in_specs=[
                pl.BlockSpec((None, n, LANES), lambda s, me: (s, 0, 0)),
                pl.BlockSpec((None, EXPERTS * CAP, width), lambda s, me: (s, 0, 0)),
            ]
            + [anywhere()] * len(tokens),
            out_specs=[
                pl.BlockSpec((None, n, width), lambda s, me: (jnp.bitwise_xor(me[0], s), 0, 0)),
                token_spec(),
            ],
        ),
        out_shape=[jax.ShapeDtypeStruct((S, n, width), bf16), TOKEN],
        compiler_params=params(60),
        cost_estimate=short(),
        name="combine",
    )(me, pos_col, src, *tokens)
    return out, [token]


PANEL = 512


def core_columns(ref, core, s, half):
    low = ref[:, 2 * s * half : (2 * s + 1) * half]
    return jnp.where(core == 0, low, ref[:, (2 * s + 1) * half : (2 * s + 2) * half])


def hi_lo(x):
    high = x.astype(bf16)
    return high, (x - high.astype(f32)).astype(bf16)


def sum_columns(x):
    ones = jnp.ones((x.shape[0], LANES), bf16)
    high, rest = hi_lo(x)
    return dot_tn(high, ones) + dot_tn(rest, ones)


def back_mid_kernel(S, *refs):
    mid_ref, ct_ref, gain_ref, h2_ref, wr_ref, wo_hbm = refs[:6]
    parts_ref = refs[6]
    dmid_ref, low_ref, dc_ref, extra_ref, token, wo, sem_w = refs[-7:]
    give(token)
    n, width = mid_ref.shape
    load = pltpu.make_async_copy(wo_hbm.at[:, pl.ds(3 * width, width)], wo, sem_w)
    load.start()

    dh = parts_ref[0].astype(f32)
    for m in range(1, S):
        dh = dh + parts_ref[m].astype(f32)
    lanes = lax.broadcasted_iota(jnp.int32, (n, LANES), 1)
    logits = jnp.where(lanes < EXPERTS, dot_nn(h2_ref[...], wr_ref[...]), -1e30)
    ex = jnp.exp(logits - jnp.max(logits, axis=-1, keepdims=True))
    prob = ex / jnp.sum(ex, axis=-1, keepdims=True)
    drouter = dh[:, width:]
    dlogit = prob * (drouter - jnp.sum(prob * drouter, axis=-1, keepdims=True))
    high, rest = hi_lo(dlogit)
    dh2 = dh[:, :width] + dot_nt(high, wr_ref[...]) + dot_nt(rest, wr_ref[...])
    grad_router = dot_tn(h2_ref[...], high) + dot_tn(h2_ref[...], rest)
    mid = mid_ref[...]
    scale = lax.rsqrt(jnp.mean(mid * mid, axis=-1, keepdims=True) + eps)
    weighted = dh2 * gain_ref[...]
    dz = scale * weighted - mid * (scale * scale * scale) * jnp.mean(
        mid * weighted, axis=-1, keepdims=True
    )
    dmid = ct_ref[...].astype(f32) + dz
    dmid_ref[...] = dmid
    low = dmid.astype(bf16)
    low_ref[...] = low
    load.wait()
    dc_ref[...] = dot_nt(low, wo[...]).astype(bf16)
    wide = lax.broadcasted_iota(jnp.int32, (width, LANES), 1)
    gain_column = sum_columns(dh2 * mid * scale)
    extra_ref[...] = jnp.where(wide == 1, gain_column, pltpu.roll(grad_router, 2, 1))


def back_mid(S, mid, ct, gain, h2, router_w, dense_w, parts, tokens):
    n, width = mid.shape
    low = jax.ShapeDtypeStruct((n, width), bf16)
    return pl.pallas_call(
        functools.partial(back_mid_kernel, S),
        in_specs=[vmem()] * 5 + [hbm(), vmem()] + [anywhere()] * len(tokens),
        out_specs=[vmem()] * 5,
        out_shape=[
            jax.ShapeDtypeStruct((n, width), f32),
            low,
            low,
            jax.ShapeDtypeStruct((width, LANES), f32),
            TOKEN,
        ],
        scratch_shapes=[pltpu.VMEM((width, width), bf16), pltpu.SemaphoreType.DMA],
        compiler_params=params(60),
        cost_estimate=short(),
        name="back_mid",
    )(mid, ct, gain, h2, router_w, dense_w, parts, *tokens)


def back_in_kernel(S, x_ref, gain_ref, d_ref, diag_ref, hot_ref, extra_ref, dmid_ref, w_hbm, *refs):
    dx_ref, small_ref, token, w_s, sem = refs[-5:]
    give(token)
    n, width = x_ref.shape
    load = pltpu.make_async_copy(w_hbm.at[:, pl.ds(0, 3 * width)], w_s, sem)
    load.start()
    diag = jnp.concatenate(
        [jnp.zeros((8, n), f32), diag_ref[...], jnp.zeros((LANES - 8 - HEADS, n), f32)], axis=0
    )
    high, rest = hi_lo(diag)
    table = dot_nt(hot_ref[...], high) + dot_nt(hot_ref[...], rest)
    part, count = width // S, BUCKETS // S
    places = lax.broadcasted_iota(jnp.int32, (16, BUCKETS), 0)
    buckets = lax.broadcasted_iota(jnp.int32, (16, BUCKETS), 1)
    high, rest = hi_lo(table)
    x = x_ref[...].astype(f32)
    scale = lax.rsqrt(jnp.mean(x * x, axis=-1, keepdims=True) + eps)
    load.wait()
    dh = dot_nt(d_ref[0], w_s[:, :width])
    dh = dh + dot_nt(d_ref[1], w_s[:, width : 2 * width])
    dh = dh + dot_nt(d_ref[2], w_s[:, 2 * width :])
    wide = lax.broadcasted_iota(jnp.int32, (width, LANES), 1)
    extra = jnp.where(wide == 0, sum_columns(dh * x * scale), extra_ref[...])
    small_ref[...] = jnp.where(wide < 2 + EXPERTS, extra, 0.0).astype(bf16)
    for s in range(S):
        pick = ((places < count) & (buckets == places + s * count)).astype(bf16)
        cut = slice(s * part, s * part + 16)
        rows = dot_nn(pick, high) + dot_nn(pick, rest) + small_ref[cut, :].astype(f32)
        small_ref[cut, :] = rows.astype(bf16)
    weighted = dh * gain_ref[...]
    dz = scale * weighted - x * (scale * scale * scale) * jnp.mean(
        x * weighted, axis=-1, keepdims=True
    )
    dx_ref[...] = (dz + dmid_ref[...]).astype(bf16)


def back_in(S, x, gain, d3, diag, hot, extra, dmid, dense_w, tokens):
    n, width = x.shape
    return pl.pallas_call(
        functools.partial(back_in_kernel, S),
        in_specs=[vmem()] * 7 + [hbm()] + [anywhere()] * len(tokens),
        out_specs=[vmem()] * 3,
        out_shape=[
            jax.ShapeDtypeStruct((n, width), bf16),
            jax.ShapeDtypeStruct((width, LANES), bf16),
            TOKEN,
        ],
        scratch_shapes=[pltpu.VMEM((width, 3 * width), bf16), pltpu.SemaphoreType.DMA],
        compiler_params=params(60),
        cost_estimate=short(),
        name="back_in",
    )(x, gain, d3, diag, hot, extra, dmid, dense_w, *tokens)


def dense_kernel(S, N, with_small, core_ref, *refs):
    left, left_o, *refs = refs
    right, refs = refs[: 2 * N], refs[2 * N :]
    out, token = refs[-2:]
    give(token)
    core = core_ref[0]
    width = left.shape[1]
    half, many = width // (2 * S), width // PANEL
    for s in range(S):
        a, b = core_columns(left, core, s, half), core_columns(left_o, core, s, half)
        for j in range(N):
            total = (dot_tn(a, right[j][...]) + dot_tn(b, right[N + j][...])).astype(bf16)
            for p in range(many):
                rows = slice((j * many + p) * half, (j * many + p + 1) * half)
                out[s, rows, :] = total[:, p * PANEL : (p + 1) * PANEL]
        if with_small:
            low, high = slice(2 * s * half, (2 * s + 1) * half), slice((2 * s + 1) * half, (2 * s + 2) * half)
            total = [
                jnp.where(core == 0, r[low, :], r[high, :]).astype(f32) for r in refs[:2]
            ]
            rows = slice(N * many * half, (N * many + 1) * half)
            out[s, rows, :LANES] = (total[0] + total[1]).astype(bf16)
            out[s, rows, LANES:] = jnp.zeros((half, PANEL - LANES), bf16)


def dense_grads_of(S, core, left, left_o, right, right_o, small, tokens):
    n, width = left.shape
    if isinstance(right, list):
        N, arrays = len(right), right + right_o
        specs = [vmem()] * (2 * N)
    else:
        N, arrays = 3, [right] * 3 + [right_o] * 3
        specs = [pl.BlockSpec((None, n, width), lambda i, j=j: (j, 0, 0)) for j in range(3)] * 2
    panels = N * (width // PANEL) + (1 if small else 0)
    shape = (S, panels * width // (2 * S), PANEL)

    def whole(x):
        return pl.BlockSpec(x.shape, lambda i: (0,) * x.ndim)

    out, token = pl.pallas_call(
        functools.partial(dense_kernel, S, N, bool(small)),
        grid=(1,),
        in_specs=[smem(), whole(left), whole(left_o)]
        + ([whole(x) for x in arrays] if isinstance(right, list) else specs)
        + [whole(x) for x in small]
        + [anywhere()] * len(tokens),
        out_specs=[pl.BlockSpec(shape, lambda i: (0, 0, 0)), token_spec()],
        out_shape=[jax.ShapeDtypeStruct(shape, bf16), TOKEN],
        compiler_params=params(60),
        cost_estimate=short(),
        name="dense",
    )(core, left, left_o, *arrays, *small, *tokens)
    return out, [token]


def wave_kernel(shapes_in, shapes_out, *refs):
    place_ref = refs[0]
    line, core = place_ref[0], place_ref[1]
    inner = (line == 1) | (line == 2)
    get = dict(zip(shapes_in, refs[1:]))
    put = dict(zip(shapes_out, refs[len(refs) - len(shapes_out) :]))
    give(put["token"])

    def add(a, b):
        return (get[a][...].astype(f32) + get[b][...].astype(f32)).astype(bf16)

    if "mid" in put:
        put["mid"][...] = add("s0", "got_pair")
    if "core" in put:
        put["core"][...] = jnp.where(inner, get["pair"][...], get["got_pair"][...])
    new = None
    if "keep" in get:
        new = add("keep", "recv") if "recv" in get else get["keep"][...]
    full = add("mid", "got_mid") if "mid" in get else None
    if new is not None:
        put["s0"][...] = new
    if "pair" in put:
        if new is None or full is None:
            put["pair"][...] = full if new is None else new
        else:
            put["pair"][...] = jnp.where(inner, full, new)
    if "final" in put:
        a, b = get["core"][...].astype(f32), get["got_core"][...].astype(f32)
        half = a.shape[1]
        put["final"][:, :half] = jnp.where(core == 0, a, b)
        put["final"][:, half:] = jnp.where(core == 0, b, a)


class Sums:
    def __init__(self, size, place):
        self.size, self.place = size, place
        self.line = size // 2 == 4
        self.queues = [[], []]
        self.state = [{}, {}]
        self.ids = [{}, {}]
        self.turn = 0
        self.added = 0
        self.dense = {}
        self.final = None
        self.targets = {}
        self.last = []

    def add(self, keep, k, recv, j, name, expert):
        if self.line:
            self.queues[self.added % 2].append((keep, k, recv, j, name, expert))
            self.added += 1
            return
        mine = line_sum((keep[k].astype(f32) + recv[j].astype(f32)).astype(bf16), self.size)
        other = swap_core(mine, self.size)
        first = self.place[1] == 0
        whole = jnp.concatenate([jnp.where(first, mine, other), jnp.where(first, other, mine)], 1)
        if name not in self.targets:
            self.targets[name] = jnp.zeros((EXPERTS,) + whole.shape, f32)
        self.targets[name] = self.targets[name].at[expert].set(whole.astype(f32))

    def busy(self):
        return any(self.queues) or any(self.state) or self.final is not None

    def begin(self):
        items = [queue.pop(0) for queue in self.queues]
        rows, cols = items[0][0].shape[1:]
        steps = max(g for g in (1, 2, 4) if rows % (16 * g) == 0)

        def block(k):
            return pl.BlockSpec((None, rows // steps, cols), lambda r: (k, r, 0))

        def kernel(*refs):
            give(refs[-1])
            outs = refs[-3:-1]
            for i in range(2):
                total = refs[2 * i][...].astype(f32) + refs[2 * i + 1][...].astype(f32)
                outs[i][...] = total.astype(bf16)

        spec = pl.BlockSpec((rows // steps, cols), lambda r: (r, 0))
        *sums, token = pl.pallas_call(
            kernel,
            grid=(steps,),
            in_specs=[block(k) for item in items for k in (item[1], item[3])]
            + [anywhere()] * len(self.last),
            out_specs=[spec, spec, token_spec()],
            out_shape=[pltpu.HBM((rows, cols), bf16)] * 2 + [TOKEN],
            compiler_params=params(60),
            cost_estimate=short(),
            name="begin",
        )(*[pin(x) for item in items for x in (item[0], item[2])], *self.last)
        self.last = [token]
        for i, item in enumerate(items):
            self.state[i] = {"s0": sums[i], "pair": sums[i]}
            self.ids[i] = {"in": (item[4], item[5])}

    def step(self, more=()):
        self.last = self.last + list(more)
        stream = self.turn
        self.turn = 1 - stream
        queue, state, ids = self.queues[stream], self.state[stream], self.ids[stream]
        rep_axis = "rep"
        ins, outs = {}, []
        if "s0" in state or "pair" in state:
            pairs = line_perm([(0, 1), (1, 0), (2, 3), (3, 2)])
            ins["got_pair"] = lax.ppermute(state["pair"], rep_axis, pairs)
        if "mid" in state:
            ins["mid"] = state["mid"]
            ins["got_mid"] = lax.ppermute(state["mid"], rep_axis, line_perm([(1, 2), (2, 1)]))
        new_ids = {}
        if "in" in ids:
            ins["s0"] = state["s0"]
            outs.append("mid")
            new_ids["mid"] = ids["in"]
        if "out" in ids:
            ins["pair"] = state["pair"]
            outs.append("core")
        if "mid" in ids:
            new_ids["out"] = ids["mid"]
        if queue:
            keep, k, recv, j, name, expert = queue.pop(0)
            ins["keep"] = (keep, k)
            if recv is not None:
                ins["recv"] = (recv, j)
            outs.append("s0")
            new_ids["in"] = (name, expert)
        if "in" in new_ids or "out" in new_ids:
            outs.append("pair")
        if self.final is not None:
            value, (name, expert) = self.final
            ins["core"] = value
            ins["got_core"] = swap_core(value, self.size)
            outs.append("final")
        if not outs:
            self.state[stream] = {}
            return
        result = self.kernel(ins, outs, self.final[1] if self.final is not None else None)
        if self.final is not None:
            self.targets[self.final[1][0]] = result["final"]
        self.final = None
        if "core" in outs:
            if ids["out"][1] is None:
                self.dense[ids["out"][0]] = result["core"]
            else:
                self.final = (result["core"], ids["out"])
        self.last = [result["token"]]
        self.state[stream] = {key: result[key] for key in ("s0", "mid", "pair") if key in outs}
        self.ids[stream] = new_ids

    def kernel(self, ins, outs, final):
        arrays, specs = [], []
        rows, cols = next(
            (x[0].shape[1:] if isinstance(x, tuple) else x.shape) for x in ins.values()
        )
        steps = max(g for g in (1, 2, 4) if rows % (16 * g) == 0)
        spec = pl.BlockSpec((rows // steps, cols), lambda r: (r, 0))
        for x in ins.values():
            if isinstance(x, tuple):
                arrays.append(pin(x[0]))
                specs.append(
                    pl.BlockSpec((None, rows // steps, cols), lambda r, k=x[1]: (k, r, 0))
                )
            else:
                arrays.append(x)
                specs.append(spec)
        shape = pltpu.HBM((rows, cols), bf16)
        out_specs, out_shapes, extra, aliases = [], [], [], {}
        for i, key in enumerate(outs):
            if key == "final":
                name, expert = final
                out_specs.append(
                    pl.BlockSpec((None, rows // steps, 2 * cols), lambda r: (expert, r, 0))
                )
                out_shapes.append(pltpu.HBM((EXPERTS, rows, 2 * cols), f32))
                if name in self.targets:
                    extra.append(pin(self.targets[name]))
                    aliases[1 + len(arrays)] = i
            else:
                out_specs.append(spec)
                out_shapes.append(shape)
        values = pl.pallas_call(
            functools.partial(wave_kernel, tuple(ins), tuple(outs) + ("token",)),
            grid=(steps,),
            in_specs=[smem()] + specs + [anywhere()] * (len(extra) + len(self.last)),
            out_specs=out_specs + [token_spec()],
            out_shape=out_shapes + [TOKEN],
            input_output_aliases=aliases,
            compiler_params=params(60),
            cost_estimate=short(),
            name="wave",
        )(self.place, *arrays, *extra, *self.last)
        return dict(zip(tuple(outs) + ("token",), values))


def assemble_kernel(half, many, place_ref, *refs):
    mine, other, outs = refs[:2], refs[2:4], refs[4:]
    core = place_ref[1]

    def rows(parts, first):
        cut = parts[0].shape[0]
        if first + half <= cut:
            return parts[0][first : first + half, :]
        if first >= cut:
            return parts[1][first - cut : first - cut + half, :]
        return jnp.concatenate([parts[0][first:, :], parts[1][: first + half - cut, :]], axis=0)

    def put(out, column, p, width):
        a = rows(mine, p * half)[:, :width].astype(f32)
        b = rows(other, p * half)[:, :width].astype(f32)
        out[:half, column : column + width] = jnp.where(core == 0, a, b)
        out[half:, column : column + width] = jnp.where(core == 0, b, a)

    for j in range(4):
        for q in range(many):
            put(outs[j], q * PANEL, j * many + q + (1 if j == 3 else 0), PANEL)
    put(outs[4], 0, 3 * many, LANES)


def assemble(place, half, width, mine, other):
    shapes = [jax.ShapeDtypeStruct((2 * half, width), f32)] * 4
    shapes.append(jax.ShapeDtypeStruct((2 * half, LANES), f32))
    return pl.pallas_call(
        functools.partial(assemble_kernel, half, width // PANEL),
        in_specs=[smem()] + [vmem()] * 4,
        out_specs=[vmem()] * 5,
        out_shape=shapes,
        compiler_params=params(60),
        cost_estimate=short(),
        name="assemble",
    )(place, *mine, *other)


def swap_core(x, size):
    return lax.ppermute(x, "rep", [(i, i ^ 1) for i in range(size)])


def swap_shard(x, size, mask):
    return lax.ppermute(x, "shard", [(i, i ^ mask) for i in range(size)])


def line_perm(pairs):
    return [(2 * a + c, 2 * b + c) for a, b in pairs for c in range(2)]


def after(x, *others):
    return lax.optimization_barrier((x,) + others)[0]


def relay_gather(x, S):
    if S != 4:
        return [[x]] + [[swap_shard(x, S, m)] for m in range(1, S)]
    cut = x.shape[0] // 2
    one, two = swap_shard(x, S, 1), swap_shard(x, S, 2)
    return [[x], [one], [two], [swap_shard(one[:cut], S, 2), swap_shard(two[cut:], S, 1)]]


def line_sum(x, size):
    n = size // 2
    h = n // 2
    line = lax.axis_index("rep") // 2
    for k in range(h - 1):
        x = x + lax.ppermute(x, "rep", line_perm([(k, k + 1), (n - 1 - k, n - 2 - k)]))
    x = x + lax.ppermute(x, "rep", line_perm([(h - 1, h), (h, h - 1)]))
    for k in reversed(range(h - 1)):
        got = lax.ppermute(x, "rep", line_perm([(k + 1, k), (n - 2 - k, n - 1 - k)]))
        x = jnp.where((line == k) | (line == n - 1 - k), got, x)
    return x


def deal_out(x):
    return lax.all_to_all(x, "shard", 0, 0, tiled=True)


def bucket_of(distance):
    bucket = jnp.minimum(distance, 16)
    for border in bucket_edges:
        bucket = bucket + (distance >= border).astype(jnp.int32)
    return bucket


def slot_positions(routes, order, lengths):
    n = order.shape[1]
    valid = jnp.arange(n, dtype=jnp.int32)[None, :] < lengths[:, None]
    experts = jnp.arange(EXPERTS, dtype=jnp.int32)
    hits = (routes[:, :, :, None] == experts) & valid[:, :, None, None]
    hits = hits.reshape(routes.shape[0], n, 2 * EXPERTS)
    before = (order[:, None, :] < order[:, :, None]).astype(bf16)
    count = jnp.einsum("stk,sut->sku", hits.astype(bf16), before, preferred_element_type=f32)
    total = jnp.sum(hits[:, :, :EXPERTS].astype(f32), axis=1)
    hits = jnp.swapaxes(hits, 1, 2)
    first, second = count[:, :EXPERTS], count[:, EXPERTS:] + total[:, :, None]
    slot = jnp.where(
        hits[:, :EXPERTS], first, jnp.where(hits[:, EXPERTS:], second, float(2 * CAP + n))
    )
    return jnp.where(slot < CAP, slot, -1.0).astype(jnp.int32)


def shards(
    R,
    S,
    tokens,
    cotangent,
    lengths,
    sequence_deal,
    routes,
    fill_order,
    norm_attn,
    w_query,
    w_key,
    w_value,
    w_out,
    rel_bias,
    norm_ffn,
    w_router,
    w_gate,
    w_up,
    w_down,
):
    me = lax.axis_index("shard")
    rep = lax.axis_index("rep")
    core = rep % 2
    line = rep // 2
    x_low, ct_low = tokens[0], cotangent[0]
    n, width = x_low.shape
    part = width // S
    half = part // 2
    group = jnp.arange(S, dtype=jnp.int32)

    dense = (w_query, w_key, w_value, w_out)
    stack = jnp.where(
        core == 0,
        jnp.concatenate([w[:half] for w in dense], axis=1),
        jnp.concatenate([w[half:] for w in dense], axis=1),
    )
    blocks = relay_gather(stack, S)
    count = len(blocks[-1])
    pieces, places = [], []
    for m in range(1, S):
        place = 2 * count * (me ^ m)
        each = count // len(blocks[m])
        pieces += blocks[m]
        places += [place + count * core + j * each for j in range(len(blocks[m]))]
        for j, block in enumerate(blocks[m]):
            pieces.append(swap_core(block, R))
            places.append(place + count * (1 - core) + j * each)
    offsets = jnp.stack(places + [2 * count * me]).astype(jnp.int32)
    ct_all = relay_gather(after(ct_low, *blocks[-1]), S)

    bias_flat = jnp.pad(rel_bias.reshape(-1), (0, part - rel_bias.size))
    small = jnp.concatenate(
        [norm_attn[:, None], norm_ffn[:, None], w_router, bias_flat[:, None]], axis=1
    )
    small = jnp.pad(small, ((0, n - part), (0, 0)))
    plan = jnp.concatenate([routes[0], fill_order[0][:, None]], axis=1).astype(bf16)
    small = jnp.concatenate([small, plan], axis=1)
    small = after(small, stack)
    small_all = deal_out(jnp.broadcast_to(small[None], (S,) + small.shape))
    plan_all = small_all[:, :, 3 + EXPERTS :]
    small_all = small_all[:, :part]
    gain_one = small_all[:, :, 0].reshape(-1).astype(f32)
    gain_two = small_all[:, :, 1].reshape(-1).astype(f32)
    router_w = small_all[:, :, 2 : 2 + EXPERTS].reshape(width, EXPERTS)
    bias_table = small_all[:, : rel_bias.size, 2 + EXPERTS].reshape(BUCKETS, HEADS)

    length = lax.dynamic_slice_in_dim(lengths[0], me, 1, 0)

    turned = jnp.arange(n, dtype=jnp.int32)
    hot = (bucket_of((n - turned) % n)[None, :] == jnp.arange(BUCKETS)[:, None]).astype(bf16)
    base = dot_tn(bias_table, hot)

    normed_low, qkv, context, middle, ffn_in, dense_w, bias = attn_fwd(
        offsets, length, x_low, gain_one[None], gain_two[None], base, dense, pieces
    )

    plan_all = after(plan_all, ffn_in).astype(jnp.int32)
    deal = sequence_deal[0]
    row_of = jnp.sum(group[:, None] * (deal[:, None] == group[None, :]).astype(jnp.int32), axis=0)
    homes = me ^ group
    plans = jnp.take(plan_all, jnp.take(row_of, homes), axis=0)
    pos = slot_positions(plans[:, :, :2], plans[:, :, 2], jnp.take(lengths[0], homes))

    h2_all = relay_gather(ffn_in, S)
    router_pad = jnp.pad(router_w, ((0, 0), (0, LANES - EXPERTS)))
    core_one = core.reshape(1).astype(jnp.int32)
    place = jnp.stack([line, core]).astype(jnp.int32)
    me_one = me.reshape(1).astype(jnp.int32)
    where = jnp.stack([me, core]).astype(jnp.int32)
    weights = [pin(w) for w in (jnp.swapaxes(w_gate, 1, 2), jnp.swapaxes(w_up, 1, 2), w_down)]
    sums = Sums(R, place)
    h1_other, context_other = swap_core(normed_low, R), swap_core(context, R)
    chain, aux = (), router_pad
    for experts, groups in (((0, 1), (2, 2, 2)), ((2, 3), (2, 2, 2))):
        first = sums.last if experts[0] == 0 else sums.last + [h1_other, context_other]
        got = ffn(experts, groups, where, pos, aux, h2_all, ct_all, weights, chain, first)
        M = 1 + len(groups)
        keep, sends, chain = got[0], got[1:M], got[M : M + 2]
        sums.last = [got[M + 2]]
        if experts[0] == 0:
            aux = got[-1]
        where_to = [(g, k) for g, size in enumerate(groups) for k in range(size)]
        recvs = [swap_core(x, R) for x in sends]
        for i, e in enumerate(experts):
            for j, name in enumerate(("down", "gate", "up")):
                g, k = where_to[3 * i + j]
                sums.add(keep, 3 * i + j, recvs[g], k, name, e)
        if experts[0] == 0 and sums.line:
            sums.begin()

    def run(steps, more=()):
        for _ in range(steps):
            if sums.line and sums.busy():
                sums.step(more)

    flat = jnp.arange(EXPERTS, dtype=jnp.int32) * CAP
    pos_col = jnp.swapaxes(jnp.where(pos < 0, -1, pos + flat[None, :, None]), 1, 2)
    pos_col = jnp.pad(pos_col, ((0, 0), (0, 0), (0, LANES - EXPERTS)))
    run(2)
    d_parts, sums.last = combine(me_one, pos_col, chain[1], sums.last)
    d_parts = deal_out(d_parts)
    run(1)
    run(1, recvs)

    dmid, dm, dc, extra, token = back_mid(
        S, middle, ct_low, gain_two[None], ffn_in, router_pad, dense_w, d_parts, sums.last
    )
    sums.last = [token]
    run(0)
    d3, diag, token = attn_bwd(qkv, bias, dc, sums.last)
    sums.last = [token]
    run(2)
    out_grads, sums.last = dense_grads_of(
        S, core_one, context, context_other, [dm], [swap_core(dm, R)], [], sums.last
    )
    out_grads = deal_out(out_grads)
    run(0)
    grad_x, extra, token = back_in(
        S, x_low, gain_one[None], d3, diag.reshape(HEADS, n), hot, extra, dmid, dense_w, sums.last
    )
    sums.last = [token]
    run(1)
    in_grads, sums.last = dense_grads_of(
        S, core_one, normed_low, h1_other, d3, swap_core(d3, R), [extra, swap_core(extra, R)], sums.last
    )
    in_grads = deal_out(in_grads)
    run(5)

    owned = [jnp.sum(x.astype(f32), axis=0).astype(bf16) for x in (in_grads, out_grads)]
    owned = jnp.concatenate(owned, axis=0)
    rows, cut = owned.shape[0], weights[0].shape[1]
    if sums.line and rows <= 2 * cut:
        owned = jnp.pad(owned, ((0, 2 * cut - rows), (0, 0)))[None]
        sums.add(owned[:, :cut], 0, None, 0, "top", None)
        sums.add(owned[:, cut:], 0, None, 0, "bottom", None)
        run(1)
    else:
        owned = line_sum(owned, R)
        sums.dense = {"top": owned[: rows // 2], "bottom": owned[rows // 2 :]}
    out_parts, sums.last = combine(me_one, pos_col, chain[0], sums.last)
    out_parts = deal_out(out_parts)
    run(4)
    result = (middle + jnp.sum(out_parts.astype(f32), axis=0)).astype(bf16)
    run(1, [result])
    run(100)
    mine = [sums.dense["top"], sums.dense["bottom"]]
    *dense_grads, small = assemble(place, half, width, mine, [swap_core(x, R) for x in mine])
    return (
        result[None],
        grad_x[None],
        small[:, 0],
        *dense_grads,
        small[: BUCKETS // S, 8 : 8 + HEADS],
        small[:, 1],
        small[:, 2 : 2 + EXPERTS],
        jnp.swapaxes(sums.targets["gate"], 1, 2),
        jnp.swapaxes(sums.targets["up"], 1, 2),
        sums.targets["down"],
    )


def solution(mesh):
    R, S = mesh.shape["rep"], mesh.shape["shard"]
    rows = P(("rep", "shard"), None, None)
    mat = P("shard", None)
    return jax.shard_map(
        functools.partial(shards, R, S),
        mesh=mesh,
        in_specs=(rows, rows, P("rep", None), P("rep", None), rows, P(("rep", "shard"), None))
        + (P("shard"), mat, mat, mat, mat, mat, P("shard"), mat)
        + (P(None, None, "shard"), P(None, None, "shard"), P(None, "shard", None)),
        out_specs=(rows, rows, P("shard"), mat, mat, mat, mat, mat, P("shard"), mat)
        + (P(None, None, "shard"), P(None, None, "shard"), P(None, "shard", None)),
        check_vma=False,
    )
```

```python
import functools
import math

import jax
import jax.numpy as jnp
from jax import lax
from jax.experimental import pallas as pl
from jax.experimental.pallas import tpu as pltpu
from jax.sharding import PartitionSpec as P

HEADS = 16
HEAD_DIM = 64
EXPERTS = 4
BUCKETS = 32
CAP = 144
LANES = 128

eps = 1e-06
bucket_edges = [int(math.ceil(16.0 * 8.0 ** (level / 16.0))) for level in range(1, 16)]
bf16 = jnp.bfloat16
f32 = jnp.float32


def dot_nn(a, b):
    return lax.dot_general(a, b, (((1,), (0,)), ((), ())), preferred_element_type=f32)


def dot_nt(a, b):
    return lax.dot_general(a, b, (((1,), (1,)), ((), ())), preferred_element_type=f32)


def dot_tn(a, b):
    return lax.dot_general(a, b, (((0,), (0,)), ((), ())), preferred_element_type=f32)


def params(mib):
    return pltpu.CompilerParams(vmem_limit_bytes=mib * 1024 * 1024)


def vmem():
    return pl.BlockSpec(memory_space=pltpu.VMEM)


def anywhere():
    return pl.BlockSpec(memory_space=pl.ANY)


TOKEN = jax.ShapeDtypeStruct((8, LANES), f32)


def token_spec():
    return pl.BlockSpec((8, LANES), lambda *i: (0, 0))


def give(token):
    token[...] = jnp.zeros(token.shape, token.dtype)


def short():
    return pl.CostEstimate(flops=1, bytes_accessed=1, transcendentals=0)


def hbm():
    return pl.BlockSpec(memory_space=pltpu.HBM)


def pin(x):
    return pltpu.with_memory_space_constraint(x, pltpu.HBM)


def smem():
    return pl.BlockSpec(memory_space=pltpu.SMEM)


def softmax_of(q, k, bias):
    s = dot_nt(q, k) * 0.125 + bias.astype(f32)
    e = jnp.exp(s - jnp.max(s, axis=-1, keepdims=True))
    return e * (1.0 / jnp.sum(e, axis=-1, keepdims=True))


def attn_fwd_kernel(N, *refs):
    off_ref, len_ref, x_ref, gain_ref, gain2_ref, base_ref = refs[:6]
    own, pieces = refs[6:10], refs[10 : 10 + N]
    h_ref, qkv_ref, c_ref, mid_ref, h2_ref, wout_ref, bias_hbm, w_s, bias_ref, sem, sems = refs[10 + N :]
    n, width = x_ref.shape
    unit = min(piece.shape[0] for piece in pieces)
    copies = []
    first = pl.multiple_of(off_ref[N] * unit, unit)
    for j in range(4):
        dest = w_s.at[pl.ds(first, own[j].shape[0]), pl.ds(j * width, width)]
        copies.append(pltpu.make_async_copy(own[j], dest, sems.at[N + j]))
    for p, piece in enumerate(pieces):
        start = pl.multiple_of(off_ref[p] * unit, unit)
        copies.append(
            pltpu.make_async_copy(piece, w_s.at[pl.ds(start, piece.shape[0])], sems.at[p])
        )
    for copy in copies:
        copy.start()
    x = x_ref[...].astype(f32)
    scale = lax.rsqrt(jnp.mean(x * x, axis=-1, keepdims=True) + eps)
    h_ref[...] = (x * scale * gain_ref[...]).astype(bf16)
    rows = lax.broadcasted_iota(jnp.int32, (n, n), 0)
    cols = lax.broadcasted_iota(jnp.int32, (n, n), 1)
    allowed = (cols <= rows) & (cols < len_ref[0])
    for h in range(HEADS):
        row = jnp.broadcast_to(base_ref[h : h + 1, :], (n, n))
        turned = pltpu.roll(row, 0, 1, stride=1, stride_axis=0)
        bias_ref[h] = jnp.where(allowed, turned, -1000000000.0).astype(bf16)
    outs = [pltpu.make_async_copy(bias_ref, bias_hbm, sem.at[0])]
    outs.append(pltpu.make_async_copy(w_s, wout_ref, sem.at[1]))
    outs[0].start()
    for copy in copies:
        copy.wait()
    outs[1].start()
    step = width // 2

    def project(i, carry):
        cut = pl.ds(pl.multiple_of(i * step, step), step)
        qkv_ref[:, cut] = dot_nn(h_ref[...], w_s[:, cut]).astype(bf16)
        return carry

    lax.fori_loop(0, 3 * width // step, project, 0)

    def some_heads(i, carry):
        def at(j):
            return pl.ds(pl.multiple_of(j * width + i * 2 * LANES, LANES), 2 * LANES)

        q, k, v = qkv_ref[:, at(0)], qkv_ref[:, at(1)], qkv_ref[:, at(2)]
        heads = []
        for h in range(4):
            cut = slice(h * HEAD_DIM, (h + 1) * HEAD_DIM)
            p = softmax_of(q[:, cut], k[:, cut], bias_ref[4 * i + h]).astype(bf16)
            heads.append(dot_nn(p, v[:, cut]).astype(bf16))
        c_ref[:, at(0)] = jnp.concatenate(heads, axis=1)
        return carry

    lax.fori_loop(0, HEADS // 4, some_heads, 0)
    mid = x_ref[...].astype(f32) + dot_nn(c_ref[...], w_s[:, 3 * width :])
    scale = lax.rsqrt(jnp.mean(mid * mid, axis=-1, keepdims=True) + eps)
    mid_ref[...] = mid
    h2_ref[...] = (mid * scale * gain2_ref[...]).astype(bf16)
    for copy in outs:
        copy.wait()


def attn_fwd(offsets, length, x, gain, gain_two, base, own, pieces):
    n, width = x.shape
    N = len(pieces)
    full = jax.ShapeDtypeStruct((n, width), bf16)
    return pl.pallas_call(
        functools.partial(attn_fwd_kernel, N),
        in_specs=[smem(), smem(), vmem(), vmem(), vmem(), vmem()] + [anywhere()] * (4 + N),
        out_specs=[vmem()] * 5 + [hbm()] * 2,
        out_shape=[
            full,
            jax.ShapeDtypeStruct((n, 3 * width), bf16),
            full,
            jax.ShapeDtypeStruct((n, width), f32),
            full,
            pltpu.HBM((width, 4 * width), bf16),
            pltpu.HBM((HEADS, n, n), bf16),
        ],
        scratch_shapes=[
            pltpu.VMEM((width, 4 * width), bf16),
            pltpu.VMEM((HEADS, n, n), bf16),
            pltpu.SemaphoreType.DMA((2,)),
            pltpu.SemaphoreType.DMA((N + 4,)),
        ],
        compiler_params=params(60),
        cost_estimate=short(),
        name="attn_fwd",
    )(offsets, length, x, gain, gain_two, base, *own, *pieces)


def attn_bwd_kernel(q_ref, k_ref, v_ref, bias_ref, dc_ref, *refs):
    d_ref, diag_ref, token = refs[-3:]
    give(token)
    n = q_ref.shape[0]
    rows = lax.broadcasted_iota(jnp.int32, (n, n), 0)
    cols = lax.broadcasted_iota(jnp.int32, (n, n), 1)
    reverse = (rows + cols == n - 1).astype(bf16)
    for h in range(4):
        cut = slice(h * HEAD_DIM, (h + 1) * HEAD_DIM)
        q, k, v, dc = q_ref[:, cut], k_ref[:, cut], v_ref[:, cut], dc_ref[:, cut]
        p = softmax_of(q, k, bias_ref[h])
        dp = dot_nt(dc, v)
        ds = p * (dp - jnp.sum(p * dp, axis=-1, keepdims=True))
        low = ds.astype(bf16)
        d_ref[0, :, cut] = (dot_nn(low, k) * 0.125).astype(bf16)
        d_ref[1, :, cut] = (dot_tn(low, q) * 0.125).astype(bf16)
        d_ref[2, :, cut] = dot_tn(p.astype(bf16), dc).astype(bf16)
        turned = pltpu.roll(dot_nn(reverse, low), 1, 1, stride=1, stride_axis=0)
        diag_ref[0, h : h + 1, :] = jnp.sum(turned, axis=0, keepdims=True)


def attn_bwd(qkv, bias, dc, tokens):
    n = qkv.shape[0]
    steps = HEADS // 4
    blk = pl.BlockSpec((n, 2 * LANES), lambda i: (0, i))
    row = pl.BlockSpec((1, 4, n), lambda i: (i, 0, 0))
    return pl.pallas_call(
        attn_bwd_kernel,
        grid=(steps,),
        in_specs=[
            blk,
            pl.BlockSpec((n, 2 * LANES), lambda i: (0, steps + i)),
            pl.BlockSpec((n, 2 * LANES), lambda i: (0, 2 * steps + i)),
            pl.BlockSpec((4, n, n), lambda i: (i, 0, 0)),
            blk,
        ]
        + [anywhere()] * len(tokens),
        out_specs=[pl.BlockSpec((3, n, 2 * LANES), lambda i: (0, 0, i)), row, token_spec()],
        out_shape=[
            jax.ShapeDtypeStruct((3, n, HEADS * HEAD_DIM), bf16),
            jax.ShapeDtypeStruct((steps, 4, n), f32),
            TOKEN,
        ],
        compiler_params=params(60),
        cost_estimate=short(),
        name="attn_bwd",
    )(qkv, qkv, qkv, bias, dc, *tokens)


def rows_of(refs):
    return refs[0][...] if len(refs) == 1 else jnp.concatenate([r[...] for r in refs], axis=0)


def ffn_kernel(shape, experts, groups, n_after, *refs):
    S, n_seq, first = len(shape), sum(shape), experts[0] == 0
    where_ref, pos_ref, aux_ref = refs[:3]
    refs = refs[3:]

    def sequences(parts):
        out, at = [], 0
        for count in shape:
            out.append(parts[at : at + count])
            at += count
        return out

    h2, ct = sequences(refs[:n_seq]), sequences(refs[n_seq : 2 * n_seq])
    refs = refs[2 * n_seq :]
    w_hbm = refs[:3]
    refs = refs[3 + n_after + (0 if first else 2) :]
    keeps, sends, (e_all, d_all, token) = refs[0], refs[1 : 1 + len(groups)], refs[1 + len(groups) : 4 + len(groups)]
    give(token)
    refs = refs[4 + len(groups) :]
    where_to = [(g, k) for g, size in enumerate(groups) for k in range(size)]
    if first:
        prob_ref, refs = refs[0], refs[1:]
    else:
        prob_ref = aux_ref
    w_v, x_s, c_s, gate_s, hid_s, da_s, du_s, o_s, eo_s, dx_s, sem_l, sem_s = refs
    n, width = pos_ref.shape[2], x_s.shape[1]
    loads = [[] for _ in experts]
    for i, e in enumerate(experts):
        for j in range(3):
            copy = pltpu.make_async_copy(w_hbm[j].at[e], w_v.at[i, j], sem_l.at[i, j])
            copy.start()
            loads[i].append(copy)
    lanes = lax.broadcasted_iota(jnp.int32, (n, LANES), 1)
    slot_lanes = lax.broadcasted_iota(jnp.int32, (S * CAP, LANES), 1)
    slots = lax.broadcasted_iota(jnp.int32, (CAP, n), 0)
    if first:
        for s in range(S):
            logits = jnp.where(lanes < EXPERTS, dot_nn(rows_of(h2[s]), aux_ref[...]), -1e30)
            ex = jnp.exp(logits - jnp.max(logits, axis=-1, keepdims=True))
            prob = ex / jnp.sum(ex, axis=-1, keepdims=True)
            high = prob.astype(bf16).astype(f32)
            rest = pltpu.roll(prob - high, EXPERTS, 1)
            prob_ref[s] = jnp.where(lanes < EXPERTS, high, rest).astype(bf16)
    half_w = width // 2
    core = where_ref[1]
    mine = pl.ds(pl.multiple_of(core * half_w, half_w), half_w)
    other = pl.ds(pl.multiple_of((1 - core) * half_w, half_w), half_w)
    const = math.sqrt(2.0 / math.pi)
    pending = {}

    def store(key, i, j, src, dst):
        copy = pltpu.make_async_copy(src, dst, sem_s.at[i, j])
        copy.start()
        pending.setdefault(key, []).append(copy)

    def settle(key):
        for copy in pending.pop(key, []):
            copy.wait()

    for i, e in enumerate(experts):
        wg, wu, wd = w_v.at[i, 0], w_v.at[i, 1], w_v.at[i, 2]
        for s in range(S):
            rows = slice(s * CAP, (s + 1) * CAP)
            hot = (slots == pos_ref[s, e : e + 1, :]).astype(bf16)
            x_s[rows, :] = dot_nn(hot, rows_of(h2[s])).astype(bf16)
            c_s[rows, :] = dot_nn(hot, rows_of(ct[s])).astype(bf16)
            picked = dot_nn(hot, prob_ref[s])
            gate_s[rows, :] = jnp.broadcast_to(
                picked[:, e : e + 1] + picked[:, EXPERTS + e : EXPERTS + e + 1], (CAP, LANES)
            )
        for copy in loads[i]:
            copy.wait()
        settle("dx")
        cols, gate = hid_s.shape[1], gate_s[:, 0:1]
        dg = jnp.zeros(gate.shape, f32)
        for f in range(0, cols, 256):
            cut = slice(f, min(f + 256, cols))
            a = dot_nt(x_s[...], wg[cut, :])
            u = dot_nt(x_s[...], wu[cut, :])
            d0 = dot_nt(c_s[...], wd[cut, :])
            t = jnp.tanh(const * (a + 0.044715 * a * a * a))
            half = 0.5 * (1.0 + t)
            act = a * half
            slope = half + 0.5 * a * (1.0 - t * t) * (const * (1.0 + 3 * 0.044715 * a * a))
            hid = act * u
            dg = dg + jnp.sum(hid * d0, axis=-1, keepdims=True)
            hid_s[:, cut] = (gate * hid).astype(bf16)
            dh = gate * d0
            da_s[:, cut] = (dh * u * slope).astype(bf16)
            du_s[:, cut] = (dh * act).astype(bf16)
        dx_s[:, width:] = jnp.where(slot_lanes == e, dg, 0.0).astype(bf16)
        for j, (left, right) in enumerate(((hid_s, c_s), (da_s, x_s), (du_s, x_s))):
            settle(j)
            o_s[j] = dot_tn(left[...], right[...]).astype(bf16)
            g, k = where_to[3 * i + j]
            store(j, i, 2 * j, o_s.at[j, :, other], sends[g].at[k])
            store(j, i, 2 * j + 1, o_s.at[j, :, mine], keeps.at[3 * i + j])
        settle("eo")
        eo_s[...] = dot_nn(hid_s[...], wd[...]).astype(bf16)
        for s in range(S):
            rows = pl.ds(s * CAP, CAP)
            store("eo", i, 6 + s, eo_s.at[rows], e_all.at[s, pl.ds(e * CAP, CAP)])
        dx_s[:, :width] = (dot_nn(da_s[...], wg[...]) + dot_nn(du_s[...], wu[...])).astype(bf16)
        for s in range(S):
            rows = pl.ds(s * CAP, CAP)
            store("dx", i, 6 + S + s, dx_s.at[rows], d_all.at[s, pl.ds(e * CAP, CAP)])
    for key in list(pending):
        settle(key)


def ffn(experts, groups, core, pos, aux, h2, ct, weights, chain, after):
    shape = tuple(len(blocks) for blocks in h2)
    S, n_seq, N = len(shape), sum(shape), len(experts)
    n = pos.shape[2]
    cols, width = weights[0].shape[1:]
    rows = S * CAP
    first = experts[0] == 0
    shapes = [pltpu.HBM((k, cols, width // 2), bf16) for k in (3 * N,) + groups] + [
        pltpu.HBM((S, EXPERTS * CAP, width), bf16),
        pltpu.HBM((S, EXPERTS * CAP, width + LANES), bf16),
        TOKEN,
    ]
    M = 1 + len(groups)
    specs = [hbm()] * (M + 2) + [vmem()]
    if first:
        shapes.append(jax.ShapeDtypeStruct((S, n, LANES), bf16))
        specs.append(vmem())
    at = 6 + 2 * n_seq + len(after)
    return pl.pallas_call(
        functools.partial(ffn_kernel, shape, experts, groups, len(after)),
        in_specs=[smem()]
        + [vmem()] * (2 + 2 * n_seq)
        + [hbm()] * 3
        + [anywhere()] * len(after)
        + [hbm()] * (0 if first else 2),
        out_specs=specs,
        out_shape=shapes,
        input_output_aliases={} if first else {at: M, at + 1: M + 1},
        scratch_shapes=[pltpu.VMEM((N, 3, cols, width), bf16)]
        + [pltpu.VMEM((rows, width), bf16)] * 2
        + [pltpu.VMEM((rows, LANES), f32)]
        + [pltpu.VMEM((rows, cols), bf16)] * 3
        + [pltpu.VMEM((3, cols, width), bf16)]
        + [pltpu.VMEM((rows, width), bf16), pltpu.VMEM((rows, width + LANES), bf16)]
        + [pltpu.SemaphoreType.DMA((N, 3)), pltpu.SemaphoreType.DMA((N, 6 + 2 * S))],
        compiler_params=params(60),
        cost_estimate=short(),
        name=f"ffn{experts[0]}",
    )(
        core,
        pos,
        aux,
        *[b for blocks in h2 for b in blocks],
        *[b for blocks in ct for b in blocks],
        *weights,
        *after,
        *([] if first else [pin(x) for x in chain]),
    )


def combine_kernel(me_ref, pos_ref, src_ref, *refs):
    out, token = refs[-2:]
    give(token)
    n = pos_ref.shape[0]
    lanes = lax.broadcasted_iota(jnp.int32, (n, EXPERTS * CAP), 1)
    hot = lanes == pos_ref[:, 0:1]
    for e in range(1, EXPERTS):
        hot = hot | (lanes == pos_ref[:, e : e + 1])
    out[...] = dot_nn(hot.astype(bf16), src_ref[...]).astype(bf16)


def combine(me, pos_col, src, tokens):
    S, n = pos_col.shape[:2]
    width = src.shape[2]
    out, token = pl.pallas_call(
        combine_kernel,
        grid_spec=pltpu.PrefetchScalarGridSpec(
            num_scalar_prefetch=1,
            grid=(S,),
            in_specs=[
                pl.BlockSpec((None, n, LANES), lambda s, me: (s, 0, 0)),
                pl.BlockSpec((None, EXPERTS * CAP, width), lambda s, me: (s, 0, 0)),
            ]
            + [anywhere()] * len(tokens),
            out_specs=[
                pl.BlockSpec((None, n, width), lambda s, me: (jnp.bitwise_xor(me[0], s), 0, 0)),
                token_spec(),
            ],
        ),
        out_shape=[jax.ShapeDtypeStruct((S, n, width), bf16), TOKEN],
        compiler_params=params(60),
        cost_estimate=short(),
        name="combine",
    )(me, pos_col, src, *tokens)
    return out, [token]


PANEL = 512


def core_columns(ref, core, s, half):
    low = ref[:, 2 * s * half : (2 * s + 1) * half]
    return jnp.where(core == 0, low, ref[:, (2 * s + 1) * half : (2 * s + 2) * half])


def hi_lo(x):
    high = x.astype(bf16)
    return high, (x - high.astype(f32)).astype(bf16)


def sum_columns(x):
    ones = jnp.ones((x.shape[0], LANES), bf16)
    high, rest = hi_lo(x)
    return dot_tn(high, ones) + dot_tn(rest, ones)


def back_mid_kernel(S, *refs):
    mid_ref, ct_ref, gain_ref, h2_ref, wr_ref, wo_hbm = refs[:6]
    parts_ref = refs[6]
    dmid_ref, low_ref, dc_ref, extra_ref, token, wo, sem_w = refs[-7:]
    give(token)
    n, width = mid_ref.shape
    load = pltpu.make_async_copy(wo_hbm.at[:, pl.ds(3 * width, width)], wo, sem_w)
    load.start()

    dh = parts_ref[0].astype(f32)
    for m in range(1, S):
        dh = dh + parts_ref[m].astype(f32)
    lanes = lax.broadcasted_iota(jnp.int32, (n, LANES), 1)
    logits = jnp.where(lanes < EXPERTS, dot_nn(h2_ref[...], wr_ref[...]), -1e30)
    ex = jnp.exp(logits - jnp.max(logits, axis=-1, keepdims=True))
    prob = ex / jnp.sum(ex, axis=-1, keepdims=True)
    drouter = dh[:, width:]
    dlogit = prob * (drouter - jnp.sum(prob * drouter, axis=-1, keepdims=True))
    high, rest = hi_lo(dlogit)
    dh2 = dh[:, :width] + dot_nt(high, wr_ref[...]) + dot_nt(rest, wr_ref[...])
    grad_router = dot_tn(h2_ref[...], high) + dot_tn(h2_ref[...], rest)
    mid = mid_ref[...]
    scale = lax.rsqrt(jnp.mean(mid * mid, axis=-1, keepdims=True) + eps)
    weighted = dh2 * gain_ref[...]
    dz = scale * weighted - mid * (scale * scale * scale) * jnp.mean(
        mid * weighted, axis=-1, keepdims=True
    )
    dmid = ct_ref[...].astype(f32) + dz
    dmid_ref[...] = dmid
    low = dmid.astype(bf16)
    low_ref[...] = low
    load.wait()
    dc_ref[...] = dot_nt(low, wo[...]).astype(bf16)
    wide = lax.broadcasted_iota(jnp.int32, (width, LANES), 1)
    gain_column = sum_columns(dh2 * mid * scale)
    extra_ref[...] = jnp.where(wide == 1, gain_column, pltpu.roll(grad_router, 2, 1))


def back_mid(S, mid, ct, gain, h2, router_w, dense_w, parts, tokens):
    n, width = mid.shape
    low = jax.ShapeDtypeStruct((n, width), bf16)
    return pl.pallas_call(
        functools.partial(back_mid_kernel, S),
        in_specs=[vmem()] * 5 + [hbm(), vmem()] + [anywhere()] * len(tokens),
        out_specs=[vmem()] * 5,
        out_shape=[
            jax.ShapeDtypeStruct((n, width), f32),
            low,
            low,
            jax.ShapeDtypeStruct((width, LANES), f32),
            TOKEN,
        ],
        scratch_shapes=[pltpu.VMEM((width, width), bf16), pltpu.SemaphoreType.DMA],
        compiler_params=params(60),
        cost_estimate=short(),
        name="back_mid",
    )(mid, ct, gain, h2, router_w, dense_w, parts, *tokens)


def back_in_kernel(S, x_ref, gain_ref, d_ref, diag_ref, hot_ref, extra_ref, dmid_ref, w_hbm, *refs):
    dx_ref, small_ref, token, w_s, sem = refs[-5:]
    give(token)
    n, width = x_ref.shape
    load = pltpu.make_async_copy(w_hbm.at[:, pl.ds(0, 3 * width)], w_s, sem)
    load.start()
    diag = jnp.concatenate(
        [jnp.zeros((8, n), f32), diag_ref[...], jnp.zeros((LANES - 8 - HEADS, n), f32)], axis=0
    )
    high, rest = hi_lo(diag)
    table = dot_nt(hot_ref[...], high) + dot_nt(hot_ref[...], rest)
    part, count = width // S, BUCKETS // S
    places = lax.broadcasted_iota(jnp.int32, (16, BUCKETS), 0)
    buckets = lax.broadcasted_iota(jnp.int32, (16, BUCKETS), 1)
    high, rest = hi_lo(table)
    x = x_ref[...].astype(f32)
    scale = lax.rsqrt(jnp.mean(x * x, axis=-1, keepdims=True) + eps)
    load.wait()
    dh = dot_nt(d_ref[0], w_s[:, :width])
    dh = dh + dot_nt(d_ref[1], w_s[:, width : 2 * width])
    dh = dh + dot_nt(d_ref[2], w_s[:, 2 * width :])
    wide = lax.broadcasted_iota(jnp.int32, (width, LANES), 1)
    extra = jnp.where(wide == 0, sum_columns(dh * x * scale), extra_ref[...])
    small_ref[...] = jnp.where(wide < 2 + EXPERTS, extra, 0.0).astype(bf16)
    for s in range(S):
        pick = ((places < count) & (buckets == places + s * count)).astype(bf16)
        cut = slice(s * part, s * part + 16)
        rows = dot_nn(pick, high) + dot_nn(pick, rest) + small_ref[cut, :].astype(f32)
        small_ref[cut, :] = rows.astype(bf16)
    weighted = dh * gain_ref[...]
    dz = scale * weighted - x * (scale * scale * scale) * jnp.mean(
        x * weighted, axis=-1, keepdims=True
    )
    dx_ref[...] = (dz + dmid_ref[...]).astype(bf16)


def back_in(S, x, gain, d3, diag, hot, extra, dmid, dense_w, tokens):
    n, width = x.shape
    return pl.pallas_call(
        functools.partial(back_in_kernel, S),
        in_specs=[vmem()] * 7 + [hbm()] + [anywhere()] * len(tokens),
        out_specs=[vmem()] * 3,
        out_shape=[
            jax.ShapeDtypeStruct((n, width), bf16),
            jax.ShapeDtypeStruct((width, LANES), bf16),
            TOKEN,
        ],
        scratch_shapes=[pltpu.VMEM((width, 3 * width), bf16), pltpu.SemaphoreType.DMA],
        compiler_params=params(60),
        cost_estimate=short(),
        name="back_in",
    )(x, gain, d3, diag, hot, extra, dmid, dense_w, *tokens)


def dense_kernel(S, N, with_small, core_ref, *refs):
    left, left_o, *refs = refs
    right, refs = refs[: 2 * N], refs[2 * N :]
    out, token = refs[-2:]
    give(token)
    core = core_ref[0]
    width = left.shape[1]
    half, many = width // (2 * S), width // PANEL
    for s in range(S):
        a, b = core_columns(left, core, s, half), core_columns(left_o, core, s, half)
        for j in range(N):
            total = (dot_tn(a, right[j][...]) + dot_tn(b, right[N + j][...])).astype(bf16)
            for p in range(many):
                rows = slice((j * many + p) * half, (j * many + p + 1) * half)
                out[s, rows, :] = total[:, p * PANEL : (p + 1) * PANEL]
        if with_small:
            low, high = slice(2 * s * half, (2 * s + 1) * half), slice((2 * s + 1) * half, (2 * s + 2) * half)
            total = [
                jnp.where(core == 0, r[low, :], r[high, :]).astype(f32) for r in refs[:2]
            ]
            rows = slice(N * many * half, (N * many + 1) * half)
            out[s, rows, :LANES] = (total[0] + total[1]).astype(bf16)
            out[s, rows, LANES:] = jnp.zeros((half, PANEL - LANES), bf16)


def dense_grads_of(S, core, left, left_o, right, right_o, small, tokens):
    n, width = left.shape
    if isinstance(right, list):
        N, arrays = len(right), right + right_o
        specs = [vmem()] * (2 * N)
    else:
        N, arrays = 3, [right] * 3 + [right_o] * 3
        specs = [pl.BlockSpec((None, n, width), lambda i, j=j: (j, 0, 0)) for j in range(3)] * 2
    panels = N * (width // PANEL) + (1 if small else 0)
    shape = (S, panels * width // (2 * S), PANEL)

    def whole(x):
        return pl.BlockSpec(x.shape, lambda i: (0,) * x.ndim)

    out, token = pl.pallas_call(
        functools.partial(dense_kernel, S, N, bool(small)),
        grid=(1,),
        in_specs=[smem(), whole(left), whole(left_o)]
        + ([whole(x) for x in arrays] if isinstance(right, list) else specs)
        + [whole(x) for x in small]
        + [anywhere()] * len(tokens),
        out_specs=[pl.BlockSpec(shape, lambda i: (0, 0, 0)), token_spec()],
        out_shape=[jax.ShapeDtypeStruct(shape, bf16), TOKEN],
        compiler_params=params(60),
        cost_estimate=short(),
        name="dense",
    )(core, left, left_o, *arrays, *small, *tokens)
    return out, [token]


def wave_kernel(shapes_in, shapes_out, *refs):
    place_ref = refs[0]
    line, core = place_ref[0], place_ref[1]
    inner = (line == 1) | (line == 2)
    get = dict(zip(shapes_in, refs[1:]))
    put = dict(zip(shapes_out, refs[len(refs) - len(shapes_out) :]))
    give(put["token"])

    def add(a, b):
        return (get[a][...].astype(f32) + get[b][...].astype(f32)).astype(bf16)

    if "mid" in put:
        put["mid"][...] = add("s0", "got_pair")
    if "core" in put:
        put["core"][...] = jnp.where(inner, get["pair"][...], get["got_pair"][...])
    new = None
    if "keep" in get:
        new = add("keep", "recv") if "recv" in get else get["keep"][...]
    full = add("mid", "got_mid") if "mid" in get else None
    if new is not None:
        put["s0"][...] = new
    if "pair" in put:
        if new is None or full is None:
            put["pair"][...] = full if new is None else new
        else:
            put["pair"][...] = jnp.where(inner, full, new)
    if "final" in put:
        a, b = get["core"][...].astype(f32), get["got_core"][...].astype(f32)
        half = a.shape[1]
        put["final"][:, :half] = jnp.where(core == 0, a, b)
        put["final"][:, half:] = jnp.where(core == 0, b, a)


class Sums:
    def __init__(self, size, place):
        self.size, self.place = size, place
        self.line = size // 2 == 4
        self.queues = [[], []]
        self.state = [{}, {}]
        self.ids = [{}, {}]
        self.turn = 0
        self.added = 0
        self.dense = {}
        self.final = None
        self.targets = {}
        self.last = []

    def add(self, keep, k, recv, j, name, expert):
        if self.line:
            self.queues[self.added % 2].append((keep, k, recv, j, name, expert))
            self.added += 1
            return
        mine = line_sum((keep[k].astype(f32) + recv[j].astype(f32)).astype(bf16), self.size)
        other = swap_core(mine, self.size)
        first = self.place[1] == 0
        whole = jnp.concatenate([jnp.where(first, mine, other), jnp.where(first, other, mine)], 1)
        if name not in self.targets:
            self.targets[name] = jnp.zeros((EXPERTS,) + whole.shape, f32)
        self.targets[name] = self.targets[name].at[expert].set(whole.astype(f32))

    def busy(self):
        return any(self.queues) or any(self.state) or self.final is not None

    def begin(self):
        items = [queue.pop(0) for queue in self.queues]
        rows, cols = items[0][0].shape[1:]
        steps = max(g for g in (1, 2, 4) if rows % (16 * g) == 0)

        def block(k):
            return pl.BlockSpec((None, rows // steps, cols), lambda r: (k, r, 0))

        def kernel(*refs):
            give(refs[-1])
            outs = refs[-3:-1]
            for i in range(2):
                total = refs[2 * i][...].astype(f32) + refs[2 * i + 1][...].astype(f32)
                outs[i][...] = total.astype(bf16)

        spec = pl.BlockSpec((rows // steps, cols), lambda r: (r, 0))
        *sums, token = pl.pallas_call(
            kernel,
            grid=(steps,),
            in_specs=[block(k) for item in items for k in (item[1], item[3])]
            + [anywhere()] * len(self.last),
            out_specs=[spec, spec, token_spec()],
            out_shape=[pltpu.HBM((rows, cols), bf16)] * 2 + [TOKEN],
            compiler_params=params(60),
            cost_estimate=short(),
            name="begin",
        )(*[pin(x) for item in items for x in (item[0], item[2])], *self.last)
        self.last = [token]
        for i, item in enumerate(items):
            self.state[i] = {"s0": sums[i], "pair": sums[i]}
            self.ids[i] = {"in": (item[4], item[5])}

    def step(self, more=()):
        self.last = self.last + list(more)
        stream = self.turn
        self.turn = 1 - stream
        queue, state, ids = self.queues[stream], self.state[stream], self.ids[stream]
        rep_axis = "rep"
        ins, outs = {}, []
        if "s0" in state or "pair" in state:
            pairs = line_perm([(0, 1), (1, 0), (2, 3), (3, 2)])
            ins["got_pair"] = lax.ppermute(state["pair"], rep_axis, pairs)
        if "mid" in state:
            ins["mid"] = state["mid"]
            ins["got_mid"] = lax.ppermute(state["mid"], rep_axis, line_perm([(1, 2), (2, 1)]))
        new_ids = {}
        if "in" in ids:
            ins["s0"] = state["s0"]
            outs.append("mid")
            new_ids["mid"] = ids["in"]
        if "out" in ids:
            ins["pair"] = state["pair"]
            outs.append("core")
        if "mid" in ids:
            new_ids["out"] = ids["mid"]
        if queue:
            keep, k, recv, j, name, expert = queue.pop(0)
            ins["keep"] = (keep, k)
            if recv is not None:
                ins["recv"] = (recv, j)
            outs.append("s0")
            new_ids["in"] = (name, expert)
        if "in" in new_ids or "out" in new_ids:
            outs.append("pair")
        if self.final is not None:
            value, (name, expert) = self.final
            ins["core"] = value
            ins["got_core"] = swap_core(value, self.size)
            outs.append("final")
        if not outs:
            self.state[stream] = {}
            return
        result = self.kernel(ins, outs, self.final[1] if self.final is not None else None)
        if self.final is not None:
            self.targets[self.final[1][0]] = result["final"]
        self.final = None
        if "core" in outs:
            if ids["out"][1] is None:
                self.dense[ids["out"][0]] = result["core"]
            else:
                self.final = (result["core"], ids["out"])
        self.last = [result["token"]]
        self.state[stream] = {key: result[key] for key in ("s0", "mid", "pair") if key in outs}
        self.ids[stream] = new_ids

    def kernel(self, ins, outs, final):
        arrays, specs = [], []
        rows, cols = next(
            (x[0].shape[1:] if isinstance(x, tuple) else x.shape) for x in ins.values()
        )
        steps = max(g for g in (1, 2, 4) if rows % (16 * g) == 0)
        spec = pl.BlockSpec((rows // steps, cols), lambda r: (r, 0))
        for x in ins.values():
            if isinstance(x, tuple):
                arrays.append(pin(x[0]))
                specs.append(
                    pl.BlockSpec((None, rows // steps, cols), lambda r, k=x[1]: (k, r, 0))
                )
            else:
                arrays.append(x)
                specs.append(spec)
        shape = pltpu.HBM((rows, cols), bf16)
        out_specs, out_shapes, extra, aliases = [], [], [], {}
        for i, key in enumerate(outs):
            if key == "final":
                name, expert = final
                out_specs.append(
                    pl.BlockSpec((None, rows // steps, 2 * cols), lambda r: (expert, r, 0))
                )
                out_shapes.append(pltpu.HBM((EXPERTS, rows, 2 * cols), f32))
                if name in self.targets:
                    extra.append(pin(self.targets[name]))
                    aliases[1 + len(arrays)] = i
            else:
                out_specs.append(spec)
                out_shapes.append(shape)
        values = pl.pallas_call(
            functools.partial(wave_kernel, tuple(ins), tuple(outs) + ("token",)),
            grid=(steps,),
            in_specs=[smem()] + specs + [anywhere()] * (len(extra) + len(self.last)),
            out_specs=out_specs + [token_spec()],
            out_shape=out_shapes + [TOKEN],
            input_output_aliases=aliases,
            compiler_params=params(60),
            cost_estimate=short(),
            name="wave",
        )(self.place, *arrays, *extra, *self.last)
        return dict(zip(tuple(outs) + ("token",), values))


def assemble_kernel(half, many, place_ref, *refs):
    mine, other, outs = refs[:2], refs[2:4], refs[4:]
    core = place_ref[1]

    def rows(parts, first):
        cut = parts[0].shape[0]
        if first + half <= cut:
            return parts[0][first : first + half, :]
        if first >= cut:
            return parts[1][first - cut : first - cut + half, :]
        return jnp.concatenate([parts[0][first:, :], parts[1][: first + half - cut, :]], axis=0)

    def put(out, column, p, width):
        a = rows(mine, p * half)[:, :width].astype(f32)
        b = rows(other, p * half)[:, :width].astype(f32)
        out[:half, column : column + width] = jnp.where(core == 0, a, b)
        out[half:, column : column + width] = jnp.where(core == 0, b, a)

    for j in range(4):
        for q in range(many):
            put(outs[j], q * PANEL, j * many + q + (1 if j == 3 else 0), PANEL)
    small = outs[6]
    put(small, 0, 3 * many, LANES)
    outs[4][...] = small[:, 2 : 2 + EXPERTS]
    outs[5][...] = small[: outs[5].shape[0], 8 : 8 + HEADS]


def assemble(place, half, width, mine, other):
    shapes = [jax.ShapeDtypeStruct((2 * half, width), f32)] * 4
    shapes.append(jax.ShapeDtypeStruct((2 * half, EXPERTS), f32))
    shapes.append(jax.ShapeDtypeStruct((BUCKETS * 2 * half // width, HEADS), f32))
    shapes.append(jax.ShapeDtypeStruct((2 * half, LANES), f32))
    return pl.pallas_call(
        functools.partial(assemble_kernel, half, width // PANEL),
        in_specs=[smem()] + [vmem()] * 4,
        out_specs=[vmem()] * 7,
        out_shape=shapes,
        compiler_params=params(60),
        cost_estimate=short(),
        name="assemble",
    )(place, *mine, *other)


def swap_core(x, size):
    return lax.ppermute(x, "rep", [(i, i ^ 1) for i in range(size)])


def swap_shard(x, size, mask):
    return lax.ppermute(x, "shard", [(i, i ^ mask) for i in range(size)])


def line_perm(pairs):
    return [(2 * a + c, 2 * b + c) for a, b in pairs for c in range(2)]


def after(x, *others):
    return lax.optimization_barrier((x,) + others)[0]


def relay_gather(top, bottom, S):
    if S != 4:
        x = jnp.concatenate([top, bottom], axis=0)
        return [[x]] + [[swap_shard(x, S, m)] for m in range(1, S)]
    one_top, two_bottom = swap_shard(top, S, 1), swap_shard(bottom, S, 2)
    one = [one_top, swap_shard(bottom, S, 1)]
    two = [swap_shard(top, S, 2), two_bottom]
    return [[top, bottom], one, two, [swap_shard(one_top, S, 2), swap_shard(two_bottom, S, 1)]]


def relay_whole(x, S):
    if S != 4:
        return [[x]] + [[swap_shard(x, S, m)] for m in range(1, S)]
    cut = x.shape[0] // 2
    one, two = swap_shard(x, S, 1), swap_shard(x, S, 2)
    return [[x], [one], [two], [swap_shard(one[:cut], S, 2), swap_shard(two[cut:], S, 1)]]


def line_sum(x, size):
    n = size // 2
    h = n // 2
    line = lax.axis_index("rep") // 2
    for k in range(h - 1):
        x = x + lax.ppermute(x, "rep", line_perm([(k, k + 1), (n - 1 - k, n - 2 - k)]))
    x = x + lax.ppermute(x, "rep", line_perm([(h - 1, h), (h, h - 1)]))
    for k in reversed(range(h - 1)):
        got = lax.ppermute(x, "rep", line_perm([(k + 1, k), (n - 2 - k, n - 1 - k)]))
        x = jnp.where((line == k) | (line == n - 1 - k), got, x)
    return x


def deal_out(x):
    return lax.all_to_all(x, "shard", 0, 0, tiled=True)


def bucket_of(distance):
    bucket = jnp.minimum(distance, 16)
    for border in bucket_edges:
        bucket = bucket + (distance >= border).astype(jnp.int32)
    return bucket


def slot_positions(routes, order, lengths):
    n = order.shape[1]
    valid = jnp.arange(n, dtype=jnp.int32)[None, :] < lengths[:, None]
    experts = jnp.arange(EXPERTS, dtype=jnp.int32)
    hits = (routes[:, :, :, None] == experts) & valid[:, :, None, None]
    hits = hits.reshape(routes.shape[0], n, 2 * EXPERTS)
    before = (order[:, None, :] < order[:, :, None]).astype(bf16)
    count = jnp.einsum("stk,sut->sku", hits.astype(bf16), before, preferred_element_type=f32)
    total = jnp.sum(hits[:, :, :EXPERTS].astype(f32), axis=1)
    hits = jnp.swapaxes(hits, 1, 2)
    first, second = count[:, :EXPERTS], count[:, EXPERTS:] + total[:, :, None]
    slot = jnp.where(
        hits[:, :EXPERTS], first, jnp.where(hits[:, EXPERTS:], second, float(2 * CAP + n))
    )
    return jnp.where(slot < CAP, slot, -1.0).astype(jnp.int32)


def shards(
    R,
    S,
    tokens,
    cotangent,
    lengths,
    sequence_deal,
    routes,
    fill_order,
    norm_attn,
    w_query,
    w_key,
    w_value,
    w_out,
    rel_bias,
    norm_ffn,
    w_router,
    w_gate,
    w_up,
    w_down,
):
    me = lax.axis_index("shard")
    rep = lax.axis_index("rep")
    core = rep % 2
    line = rep // 2
    x_low, ct_low = tokens[0], cotangent[0]
    n, width = x_low.shape
    part = width // S
    half = part // 2
    group = jnp.arange(S, dtype=jnp.int32)

    dense = (w_query, w_key, w_value, w_out)
    cut = half // 2

    def rows_for_core(first):
        return jnp.where(
            core == 0,
            jnp.concatenate([w[first : first + cut] for w in dense], axis=1),
            jnp.concatenate([w[half + first : half + first + cut] for w in dense], axis=1),
        )

    stack = rows_for_core(0)
    blocks = relay_gather(stack, rows_for_core(cut), S)
    count = len(blocks[-1])
    pieces, places = [], []
    for m in range(1, S):
        place = 2 * count * (me ^ m)
        each = count // len(blocks[m])
        pieces += blocks[m]
        places += [place + count * core + j * each for j in range(len(blocks[m]))]
        for j, block in enumerate(blocks[m]):
            pieces.append(swap_core(block, R))
            places.append(place + count * (1 - core) + j * each)
    offsets = jnp.stack(places + [2 * count * me]).astype(jnp.int32)
    ct_all = relay_whole(after(ct_low, *blocks[-1]), S)

    bias_flat = jnp.pad(rel_bias.reshape(-1), (0, part - rel_bias.size))
    small = jnp.concatenate(
        [norm_attn[:, None], norm_ffn[:, None], w_router, bias_flat[:, None]], axis=1
    )
    small = jnp.pad(small, ((0, n - part), (0, 0)))
    plan = jnp.concatenate([routes[0], fill_order[0][:, None]], axis=1).astype(bf16)
    small = jnp.concatenate([small, plan], axis=1)
    small = after(small, stack)
    small_all = deal_out(jnp.broadcast_to(small[None], (S,) + small.shape))
    plan_all = small_all[:, :, 3 + EXPERTS :]
    small_all = small_all[:, :part]
    gain_one = small_all[:, :, 0].reshape(-1).astype(f32)
    gain_two = small_all[:, :, 1].reshape(-1).astype(f32)
    router_w = small_all[:, :, 2 : 2 + EXPERTS].reshape(width, EXPERTS)
    bias_table = small_all[:, : rel_bias.size, 2 + EXPERTS].reshape(BUCKETS, HEADS)

    length = lax.dynamic_slice_in_dim(lengths[0], me, 1, 0)

    turned = jnp.arange(n, dtype=jnp.int32)
    hot = (bucket_of((n - turned) % n)[None, :] == jnp.arange(BUCKETS)[:, None]).astype(bf16)
    base = dot_tn(bias_table, hot)

    normed_low, qkv, context, middle, ffn_in, dense_w, bias = attn_fwd(
        offsets, length, x_low, gain_one[None], gain_two[None], base, dense, pieces
    )

    plan_all = after(plan_all, ffn_in).astype(jnp.int32)
    deal = sequence_deal[0]
    row_of = jnp.sum(group[:, None] * (deal[:, None] == group[None, :]).astype(jnp.int32), axis=0)
    homes = me ^ group
    plans = jnp.take(plan_all, jnp.take(row_of, homes), axis=0)
    pos = slot_positions(plans[:, :, :2], plans[:, :, 2], jnp.take(lengths[0], homes))

    h2_all = relay_whole(ffn_in, S)
    router_pad = jnp.pad(router_w, ((0, 0), (0, LANES - EXPERTS)))
    core_one = core.reshape(1).astype(jnp.int32)
    place = jnp.stack([line, core]).astype(jnp.int32)
    me_one = me.reshape(1).astype(jnp.int32)
    where = jnp.stack([me, core]).astype(jnp.int32)
    weights = [pin(w) for w in (jnp.swapaxes(w_gate, 1, 2), jnp.swapaxes(w_up, 1, 2), w_down)]
    sums = Sums(R, place)
    h1_other, context_other = swap_core(normed_low, R), swap_core(context, R)
    chain, aux = (), router_pad
    for experts, groups in (((0, 1), (2, 2, 2)), ((2, 3), (2, 2, 2))):
        first = sums.last if experts[0] == 0 else sums.last + [h1_other, context_other]
        got = ffn(experts, groups, where, pos, aux, h2_all, ct_all, weights, chain, first)
        M = 1 + len(groups)
        keep, sends, chain = got[0], got[1:M], got[M : M + 2]
        sums.last = [got[M + 2]]
        if experts[0] == 0:
            aux = got[-1]
        where_to = [(g, k) for g, size in enumerate(groups) for k in range(size)]
        recvs = [swap_core(x, R) for x in sends]
        for i, e in enumerate(experts):
            for j, name in enumerate(("down", "gate", "up")):
                g, k = where_to[3 * i + j]
                sums.add(keep, 3 * i + j, recvs[g], k, name, e)
        if experts[0] == 0 and sums.line:
            sums.begin()

    def run(steps, more=()):
        for _ in range(steps):
            if sums.line and sums.busy():
                sums.step(more)

    flat = jnp.arange(EXPERTS, dtype=jnp.int32) * CAP
    pos_col = jnp.swapaxes(jnp.where(pos < 0, -1, pos + flat[None, :, None]), 1, 2)
    pos_col = jnp.pad(pos_col, ((0, 0), (0, 0), (0, LANES - EXPERTS)))
    run(2)
    d_parts, sums.last = combine(me_one, pos_col, chain[1], sums.last)
    d_parts = deal_out(d_parts)
    run(1)
    run(1, recvs)

    dmid, dm, dc, extra, token = back_mid(
        S, middle, ct_low, gain_two[None], ffn_in, router_pad, dense_w, d_parts, sums.last
    )
    sums.last = [token]
    run(0)
    d3, diag, token = attn_bwd(qkv, bias, dc, sums.last)
    sums.last = [token]
    run(2)
    out_grads, sums.last = dense_grads_of(
        S, core_one, context, context_other, [dm], [swap_core(dm, R)], [], sums.last
    )
    out_grads = deal_out(out_grads)
    run(0)
    grad_x, extra, token = back_in(
        S, x_low, gain_one[None], d3, diag.reshape(HEADS, n), hot, extra, dmid, dense_w, sums.last
    )
    sums.last = [token]
    run(1)
    in_grads, sums.last = dense_grads_of(
        S, core_one, normed_low, h1_other, d3, swap_core(d3, R), [extra, swap_core(extra, R)], sums.last
    )
    in_grads = deal_out(in_grads)
    run(5)

    owned = [jnp.sum(x.astype(f32), axis=0).astype(bf16) for x in (in_grads, out_grads)]
    owned = jnp.concatenate(owned, axis=0)
    rows, cut = owned.shape[0], weights[0].shape[1]
    if sums.line and rows <= 2 * cut:
        owned = jnp.pad(owned, ((0, 2 * cut - rows), (0, 0)))[None]
        sums.add(owned[:, :cut], 0, None, 0, "top", None)
        sums.add(owned[:, cut:], 0, None, 0, "bottom", None)
        run(1)
    else:
        owned = line_sum(owned, R)
        sums.dense = {"top": owned[: rows // 2], "bottom": owned[rows // 2 :]}
    out_parts, sums.last = combine(me_one, pos_col, chain[0], sums.last)
    out_parts = deal_out(out_parts)
    run(4)
    result = (middle + jnp.sum(out_parts.astype(f32), axis=0)).astype(bf16)
    run(1, [result])
    run(100)
    mine = [sums.dense["top"], sums.dense["bottom"]]
    *dense_grads, grad_router_w, grad_table, small = assemble(place, half, width, mine, [swap_core(x, R) for x in mine])
    return (
        result[None],
        grad_x[None],
        small[:, 0],
        *dense_grads,
        grad_table,
        small[:, 1],
        grad_router_w,
        jnp.swapaxes(sums.targets["gate"], 1, 2),
        jnp.swapaxes(sums.targets["up"], 1, 2),
        sums.targets["down"],
    )


def solution(mesh):
    R, S = mesh.shape["rep"], mesh.shape["shard"]
    rows = P(("rep", "shard"), None, None)
    mat = P("shard", None)
    return jax.shard_map(
        functools.partial(shards, R, S),
        mesh=mesh,
        in_specs=(rows, rows, P("rep", None), P("rep", None), rows, P(("rep", "shard"), None))
        + (P("shard"), mat, mat, mat, mat, mat, P("shard"), mat)
        + (P(None, None, "shard"), P(None, None, "shard"), P(None, "shard", None)),
        out_specs=(rows, rows, P("shard"), mat, mat, mat, mat, mat, P("shard"), mat)
        + (P(None, None, "shard"), P(None, None, "shard"), P(None, "shard", None)),
        check_vma=False,
    )
```

```python
import functools
import math

import jax
import jax.numpy as jnp
from jax import lax
from jax.experimental import pallas as pl
from jax.experimental.pallas import tpu as pltpu
from jax.sharding import PartitionSpec as P

HEADS = 16
HEAD_DIM = 64
EXPERTS = 4
BUCKETS = 32
CAP = 144
LANES = 128

eps = 1e-06
bucket_edges = [int(math.ceil(16.0 * 8.0 ** (level / 16.0))) for level in range(1, 16)]
bf16 = jnp.bfloat16
f32 = jnp.float32


def dot_nn(a, b):
    return lax.dot_general(a, b, (((1,), (0,)), ((), ())), preferred_element_type=f32)


def dot_nt(a, b):
    return lax.dot_general(a, b, (((1,), (1,)), ((), ())), preferred_element_type=f32)


def dot_tn(a, b):
    return lax.dot_general(a, b, (((0,), (0,)), ((), ())), preferred_element_type=f32)


def params(mib):
    return pltpu.CompilerParams(vmem_limit_bytes=mib * 1024 * 1024)


def vmem():
    return pl.BlockSpec(memory_space=pltpu.VMEM)


def anywhere():
    return pl.BlockSpec(memory_space=pl.ANY)


TOKEN = jax.ShapeDtypeStruct((8, LANES), f32)


def token_spec():
    return pl.BlockSpec((8, LANES), lambda *i: (0, 0))


def give(token):
    token[...] = jnp.zeros(token.shape, token.dtype)


def short():
    return pl.CostEstimate(flops=1, bytes_accessed=1, transcendentals=0)


def hbm():
    return pl.BlockSpec(memory_space=pltpu.HBM)


def pin(x):
    return pltpu.with_memory_space_constraint(x, pltpu.HBM)


def smem():
    return pl.BlockSpec(memory_space=pltpu.SMEM)


def softmax_of(q, k, bias):
    s = dot_nt(q, k) * 0.125 + bias.astype(f32)
    e = jnp.exp(s - jnp.max(s, axis=-1, keepdims=True))
    return e * (1.0 / jnp.sum(e, axis=-1, keepdims=True))


def attn_fwd_kernel(N, *refs):
    off_ref, len_ref, x_ref, gain_ref, gain2_ref, base_ref = refs[:6]
    own, pieces = refs[6:10], refs[10 : 10 + N]
    h_ref, qkv_ref, c_ref, mid_ref, h2_ref, wout_ref, bias_hbm, w_s, bias_ref, sem, sems = refs[10 + N :]
    n, width = x_ref.shape
    unit = min(piece.shape[0] for piece in pieces)
    copies = []
    first = pl.multiple_of(off_ref[N] * unit, unit)
    for j in range(4):
        dest = w_s.at[pl.ds(first, own[j].shape[0]), pl.ds(j * width, width)]
        copies.append(pltpu.make_async_copy(own[j], dest, sems.at[N + j]))
    for p, piece in enumerate(pieces):
        start = pl.multiple_of(off_ref[p] * unit, unit)
        copies.append(
            pltpu.make_async_copy(piece, w_s.at[pl.ds(start, piece.shape[0])], sems.at[p])
        )
    for copy in copies:
        copy.start()
    x = x_ref[...].astype(f32)
    scale = lax.rsqrt(jnp.mean(x * x, axis=-1, keepdims=True) + eps)
    h_ref[...] = (x * scale * gain_ref[...]).astype(bf16)
    rows = lax.broadcasted_iota(jnp.int32, (n, n), 0)
    cols = lax.broadcasted_iota(jnp.int32, (n, n), 1)
    allowed = (cols <= rows) & (cols < len_ref[0])
    for h in range(HEADS):
        row = jnp.broadcast_to(base_ref[h : h + 1, :], (n, n))
        turned = pltpu.roll(row, 0, 1, stride=1, stride_axis=0)
        bias_ref[h] = jnp.where(allowed, turned, -1000000000.0).astype(bf16)
    outs = [pltpu.make_async_copy(bias_ref, bias_hbm, sem.at[0])]
    outs.append(pltpu.make_async_copy(w_s, wout_ref, sem.at[1]))
    outs[0].start()
    for copy in copies:
        copy.wait()
    outs[1].start()
    step = width // 2

    def project(i, carry):
        cut = pl.ds(pl.multiple_of(i * step, step), step)
        qkv_ref[:, cut] = dot_nn(h_ref[...], w_s[:, cut]).astype(bf16)
        return carry

    lax.fori_loop(0, 3 * width // step, project, 0)

    def some_heads(i, carry):
        def at(j):
            return pl.ds(pl.multiple_of(j * width + i * 2 * LANES, LANES), 2 * LANES)

        q, k, v = qkv_ref[:, at(0)], qkv_ref[:, at(1)], qkv_ref[:, at(2)]
        heads = []
        for h in range(4):
            cut = slice(h * HEAD_DIM, (h + 1) * HEAD_DIM)
            p = softmax_of(q[:, cut], k[:, cut], bias_ref[4 * i + h]).astype(bf16)
            heads.append(dot_nn(p, v[:, cut]).astype(bf16))
        c_ref[:, at(0)] = jnp.concatenate(heads, axis=1)
        return carry

    lax.fori_loop(0, HEADS // 4, some_heads, 0)
    mid = x_ref[...].astype(f32) + dot_nn(c_ref[...], w_s[:, 3 * width :])
    scale = lax.rsqrt(jnp.mean(mid * mid, axis=-1, keepdims=True) + eps)
    mid_ref[...] = mid
    h2_ref[...] = (mid * scale * gain2_ref[...]).astype(bf16)
    for copy in outs:
        copy.wait()


def attn_fwd(offsets, length, x, gain, gain_two, base, own, pieces):
    n, width = x.shape
    N = len(pieces)
    full = jax.ShapeDtypeStruct((n, width), bf16)
    return pl.pallas_call(
        functools.partial(attn_fwd_kernel, N),
        in_specs=[smem(), smem(), vmem(), vmem(), vmem(), vmem()] + [anywhere()] * (4 + N),
        out_specs=[vmem()] * 5 + [hbm()] * 2,
        out_shape=[
            full,
            jax.ShapeDtypeStruct((n, 3 * width), bf16),
            full,
            jax.ShapeDtypeStruct((n, width), f32),
            full,
            pltpu.HBM((width, 4 * width), bf16),
            pltpu.HBM((HEADS, n, n), bf16),
        ],
        scratch_shapes=[
            pltpu.VMEM((width, 4 * width), bf16),
            pltpu.VMEM((HEADS, n, n), bf16),
            pltpu.SemaphoreType.DMA((2,)),
            pltpu.SemaphoreType.DMA((N + 4,)),
        ],
        compiler_params=params(60),
        cost_estimate=short(),
        name="attn_fwd",
    )(offsets, length, x, gain, gain_two, base, *own, *pieces)


def attn_bwd_kernel(q_ref, k_ref, v_ref, bias_ref, dc_ref, *refs):
    d_ref, diag_ref, token = refs[-3:]
    give(token)
    n = q_ref.shape[0]
    rows = lax.broadcasted_iota(jnp.int32, (n, n), 0)
    cols = lax.broadcasted_iota(jnp.int32, (n, n), 1)
    reverse = (rows + cols == n - 1).astype(bf16)
    for h in range(4):
        cut = slice(h * HEAD_DIM, (h + 1) * HEAD_DIM)
        q, k, v, dc = q_ref[:, cut], k_ref[:, cut], v_ref[:, cut], dc_ref[:, cut]
        p = softmax_of(q, k, bias_ref[h])
        dp = dot_nt(dc, v)
        ds = p * (dp - jnp.sum(p * dp, axis=-1, keepdims=True))
        low = ds.astype(bf16)
        d_ref[0, :, cut] = (dot_nn(low, k) * 0.125).astype(bf16)
        d_ref[1, :, cut] = (dot_tn(low, q) * 0.125).astype(bf16)
        d_ref[2, :, cut] = dot_tn(p.astype(bf16), dc).astype(bf16)
        turned = pltpu.roll(dot_nn(reverse, low), 1, 1, stride=1, stride_axis=0)
        diag_ref[0, h : h + 1, :] = jnp.sum(turned, axis=0, keepdims=True)


def attn_bwd(qkv, bias, dc, tokens):
    n = qkv.shape[0]
    steps = HEADS // 4
    blk = pl.BlockSpec((n, 2 * LANES), lambda i: (0, i))
    row = pl.BlockSpec((1, 4, n), lambda i: (i, 0, 0))
    return pl.pallas_call(
        attn_bwd_kernel,
        grid=(steps,),
        in_specs=[
            blk,
            pl.BlockSpec((n, 2 * LANES), lambda i: (0, steps + i)),
            pl.BlockSpec((n, 2 * LANES), lambda i: (0, 2 * steps + i)),
            pl.BlockSpec((4, n, n), lambda i: (i, 0, 0)),
            blk,
        ]
        + [anywhere()] * len(tokens),
        out_specs=[pl.BlockSpec((3, n, 2 * LANES), lambda i: (0, 0, i)), row, token_spec()],
        out_shape=[
            jax.ShapeDtypeStruct((3, n, HEADS * HEAD_DIM), bf16),
            jax.ShapeDtypeStruct((steps, 4, n), f32),
            TOKEN,
        ],
        compiler_params=params(60),
        cost_estimate=short(),
        name="attn_bwd",
    )(qkv, qkv, qkv, bias, dc, *tokens)


def rows_of(refs):
    return refs[0][...] if len(refs) == 1 else jnp.concatenate([r[...] for r in refs], axis=0)


def ffn_kernel(shape, experts, groups, n_after, *refs):
    S, n_seq, first = len(shape), sum(shape), experts[0] == 0
    where_ref, pos_ref, aux_ref = refs[:3]
    refs = refs[3:]

    def sequences(parts):
        out, at = [], 0
        for count in shape:
            out.append(parts[at : at + count])
            at += count
        return out

    h2, ct = sequences(refs[:n_seq]), sequences(refs[n_seq : 2 * n_seq])
    refs = refs[2 * n_seq :]
    w_hbm = refs[:3]
    refs = refs[3 + n_after + (0 if first else 2) :]
    keeps, sends, (e_all, d_all, token) = refs[0], refs[1 : 1 + len(groups)], refs[1 + len(groups) : 4 + len(groups)]
    give(token)
    refs = refs[4 + len(groups) :]
    where_to = [(g, k) for g, size in enumerate(groups) for k in range(size)]
    if first:
        prob_ref, refs = refs[0], refs[1:]
    else:
        prob_ref = aux_ref
    w_v, x_s, c_s, gate_s, hid_s, da_s, du_s, o_s, eo_s, dx_s, sem_l, sem_s = refs
    n, width = pos_ref.shape[2], x_s.shape[1]
    loads = [[] for _ in experts]
    for i, e in enumerate(experts):
        for j in range(3):
            copy = pltpu.make_async_copy(w_hbm[j].at[e], w_v.at[i, j], sem_l.at[i, j])
            copy.start()
            loads[i].append(copy)
    lanes = lax.broadcasted_iota(jnp.int32, (n, LANES), 1)
    slot_lanes = lax.broadcasted_iota(jnp.int32, (S * CAP, LANES), 1)
    slots = lax.broadcasted_iota(jnp.int32, (CAP, n), 0)
    if first:
        for s in range(S):
            logits = jnp.where(lanes < EXPERTS, dot_nn(rows_of(h2[s]), aux_ref[...]), -1e30)
            ex = jnp.exp(logits - jnp.max(logits, axis=-1, keepdims=True))
            prob = ex / jnp.sum(ex, axis=-1, keepdims=True)
            high = prob.astype(bf16).astype(f32)
            rest = pltpu.roll(prob - high, EXPERTS, 1)
            prob_ref[s] = jnp.where(lanes < EXPERTS, high, rest).astype(bf16)
    half_w = width // 2
    core = where_ref[1]
    mine = pl.ds(pl.multiple_of(core * half_w, half_w), half_w)
    other = pl.ds(pl.multiple_of((1 - core) * half_w, half_w), half_w)
    const = math.sqrt(2.0 / math.pi)
    pending = {}

    def store(key, i, j, src, dst):
        copy = pltpu.make_async_copy(src, dst, sem_s.at[i, j])
        copy.start()
        pending.setdefault(key, []).append(copy)

    def settle(key):
        for copy in pending.pop(key, []):
            copy.wait()

    for i, e in enumerate(experts):
        wg, wu, wd = w_v.at[i, 0], w_v.at[i, 1], w_v.at[i, 2]
        for s in range(S):
            rows = slice(s * CAP, (s + 1) * CAP)
            hot = (slots == pos_ref[s, e : e + 1, :]).astype(bf16)
            x_s[rows, :] = dot_nn(hot, rows_of(h2[s])).astype(bf16)
            c_s[rows, :] = dot_nn(hot, rows_of(ct[s])).astype(bf16)
            picked = dot_nn(hot, prob_ref[s])
            gate_s[rows, :] = jnp.broadcast_to(
                picked[:, e : e + 1] + picked[:, EXPERTS + e : EXPERTS + e + 1], (CAP, LANES)
            )
        for copy in loads[i]:
            copy.wait()
        settle("dx")
        cols, gate = hid_s.shape[1], gate_s[:, 0:1]
        dg = jnp.zeros(gate.shape, f32)
        for f in range(0, cols, 256):
            cut = slice(f, min(f + 256, cols))
            a = dot_nt(x_s[...], wg[cut, :])
            u = dot_nt(x_s[...], wu[cut, :])
            d0 = dot_nt(c_s[...], wd[cut, :])
            t = jnp.tanh(const * (a + 0.044715 * a * a * a))
            half = 0.5 * (1.0 + t)
            act = a * half
            slope = half + 0.5 * a * (1.0 - t * t) * (const * (1.0 + 3 * 0.044715 * a * a))
            hid = act * u
            dg = dg + jnp.sum(hid * d0, axis=-1, keepdims=True)
            hid_s[:, cut] = (gate * hid).astype(bf16)
            dh = gate * d0
            da_s[:, cut] = (dh * u * slope).astype(bf16)
            du_s[:, cut] = (dh * act).astype(bf16)
        dx_s[:, width:] = jnp.where(slot_lanes == e, dg, 0.0).astype(bf16)
        for j, (left, right) in enumerate(((hid_s, c_s), (da_s, x_s), (du_s, x_s))):
            settle(j)
            o_s[j] = dot_tn(left[...], right[...]).astype(bf16)
            g, k = where_to[3 * i + j]
            store(j, i, 2 * j, o_s.at[j, :, other], sends[g].at[k])
            store(j, i, 2 * j + 1, o_s.at[j, :, mine], keeps.at[3 * i + j])
        settle("eo")
        eo_s[...] = dot_nn(hid_s[...], wd[...]).astype(bf16)
        for s in range(S):
            rows = pl.ds(s * CAP, CAP)
            store("eo", i, 6 + s, eo_s.at[rows], e_all.at[s, pl.ds(e * CAP, CAP)])
        dx_s[:, :width] = (dot_nn(da_s[...], wg[...]) + dot_nn(du_s[...], wu[...])).astype(bf16)
        for s in range(S):
            rows = pl.ds(s * CAP, CAP)
            store("dx", i, 6 + S + s, dx_s.at[rows], d_all.at[s, pl.ds(e * CAP, CAP)])
    for key in list(pending):
        settle(key)


def ffn(experts, groups, core, pos, aux, h2, ct, weights, chain, after):
    shape = tuple(len(blocks) for blocks in h2)
    S, n_seq, N = len(shape), sum(shape), len(experts)
    n = pos.shape[2]
    cols, width = weights[0].shape[1:]
    rows = S * CAP
    first = experts[0] == 0
    shapes = [pltpu.HBM((k, cols, width // 2), bf16) for k in (3 * N,) + groups] + [
        pltpu.HBM((S, EXPERTS * CAP, width), bf16),
        pltpu.HBM((S, EXPERTS * CAP, width + LANES), bf16),
        TOKEN,
    ]
    M = 1 + len(groups)
    specs = [hbm()] * (M + 2) + [vmem()]
    if first:
        shapes.append(jax.ShapeDtypeStruct((S, n, LANES), bf16))
        specs.append(vmem())
    at = 6 + 2 * n_seq + len(after)
    return pl.pallas_call(
        functools.partial(ffn_kernel, shape, experts, groups, len(after)),
        in_specs=[smem()]
        + [vmem()] * (2 + 2 * n_seq)
        + [hbm()] * 3
        + [anywhere()] * len(after)
        + [hbm()] * (0 if first else 2),
        out_specs=specs,
        out_shape=shapes,
        input_output_aliases={} if first else {at: M, at + 1: M + 1},
        scratch_shapes=[pltpu.VMEM((N, 3, cols, width), bf16)]
        + [pltpu.VMEM((rows, width), bf16)] * 2
        + [pltpu.VMEM((rows, LANES), f32)]
        + [pltpu.VMEM((rows, cols), bf16)] * 3
        + [pltpu.VMEM((3, cols, width), bf16)]
        + [pltpu.VMEM((rows, width), bf16), pltpu.VMEM((rows, width + LANES), bf16)]
        + [pltpu.SemaphoreType.DMA((N, 3)), pltpu.SemaphoreType.DMA((N, 6 + 2 * S))],
        compiler_params=params(60),
        cost_estimate=short(),
        name=f"ffn{experts[0]}",
    )(
        core,
        pos,
        aux,
        *[b for blocks in h2 for b in blocks],
        *[b for blocks in ct for b in blocks],
        *weights,
        *after,
        *([] if first else [pin(x) for x in chain]),
    )


def combine_kernel(me_ref, pos_ref, src_ref, *refs):
    out, token = refs[-2:]
    give(token)
    n = pos_ref.shape[0]
    lanes = lax.broadcasted_iota(jnp.int32, (n, EXPERTS * CAP), 1)
    hot = lanes == pos_ref[:, 0:1]
    for e in range(1, EXPERTS):
        hot = hot | (lanes == pos_ref[:, e : e + 1])
    out[...] = dot_nn(hot.astype(bf16), src_ref[...]).astype(bf16)


def combine(me, pos_col, src, tokens):
    S, n = pos_col.shape[:2]
    width = src.shape[2]
    out, token = pl.pallas_call(
        combine_kernel,
        grid_spec=pltpu.PrefetchScalarGridSpec(
            num_scalar_prefetch=1,
            grid=(S,),
            in_specs=[
                pl.BlockSpec((None, n, LANES), lambda s, me: (s, 0, 0)),
                pl.BlockSpec((None, EXPERTS * CAP, width), lambda s, me: (s, 0, 0)),
            ]
            + [anywhere()] * len(tokens),
            out_specs=[
                pl.BlockSpec((None, n, width), lambda s, me: (jnp.bitwise_xor(me[0], s), 0, 0)),
                token_spec(),
            ],
        ),
        out_shape=[jax.ShapeDtypeStruct((S, n, width), bf16), TOKEN],
        compiler_params=params(60),
        cost_estimate=short(),
        name="combine",
    )(me, pos_col, src, *tokens)
    return out, [token]


PANEL = 512


def core_columns(ref, core, s, half):
    low = ref[:, 2 * s * half : (2 * s + 1) * half]
    return jnp.where(core == 0, low, ref[:, (2 * s + 1) * half : (2 * s + 2) * half])


def hi_lo(x):
    high = x.astype(bf16)
    return high, (x - high.astype(f32)).astype(bf16)


def sum_columns(x):
    ones = jnp.ones((x.shape[0], LANES), bf16)
    high, rest = hi_lo(x)
    return dot_tn(high, ones) + dot_tn(rest, ones)


def back_mid_kernel(S, *refs):
    mid_ref, ct_ref, gain_ref, h2_ref, wr_ref, wo_hbm = refs[:6]
    parts_ref = refs[6]
    dmid_ref, low_ref, dc_ref, extra_ref, token, wo, sem_w = refs[-7:]
    give(token)
    n, width = mid_ref.shape
    load = pltpu.make_async_copy(wo_hbm.at[:, pl.ds(3 * width, width)], wo, sem_w)
    load.start()

    dh = parts_ref[0].astype(f32)
    for m in range(1, S):
        dh = dh + parts_ref[m].astype(f32)
    lanes = lax.broadcasted_iota(jnp.int32, (n, LANES), 1)
    logits = jnp.where(lanes < EXPERTS, dot_nn(h2_ref[...], wr_ref[...]), -1e30)
    ex = jnp.exp(logits - jnp.max(logits, axis=-1, keepdims=True))
    prob = ex / jnp.sum(ex, axis=-1, keepdims=True)
    drouter = dh[:, width:]
    dlogit = prob * (drouter - jnp.sum(prob * drouter, axis=-1, keepdims=True))
    high, rest = hi_lo(dlogit)
    dh2 = dh[:, :width] + dot_nt(high, wr_ref[...]) + dot_nt(rest, wr_ref[...])
    grad_router = dot_tn(h2_ref[...], high) + dot_tn(h2_ref[...], rest)
    mid = mid_ref[...]
    scale = lax.rsqrt(jnp.mean(mid * mid, axis=-1, keepdims=True) + eps)
    weighted = dh2 * gain_ref[...]
    dz = scale * weighted - mid * (scale * scale * scale) * jnp.mean(
        mid * weighted, axis=-1, keepdims=True
    )
    dmid = ct_ref[...].astype(f32) + dz
    dmid_ref[...] = dmid
    low = dmid.astype(bf16)
    low_ref[...] = low
    load.wait()
    dc_ref[...] = dot_nt(low, wo[...]).astype(bf16)
    wide = lax.broadcasted_iota(jnp.int32, (width, LANES), 1)
    gain_column = sum_columns(dh2 * mid * scale)
    extra_ref[...] = jnp.where(wide == 1, gain_column, pltpu.roll(grad_router, 2, 1))


def back_mid(S, mid, ct, gain, h2, router_w, dense_w, parts, tokens):
    n, width = mid.shape
    low = jax.ShapeDtypeStruct((n, width), bf16)
    return pl.pallas_call(
        functools.partial(back_mid_kernel, S),
        in_specs=[vmem()] * 5 + [hbm(), vmem()] + [anywhere()] * len(tokens),
        out_specs=[vmem()] * 5,
        out_shape=[
            jax.ShapeDtypeStruct((n, width), f32),
            low,
            low,
            jax.ShapeDtypeStruct((width, LANES), f32),
            TOKEN,
        ],
        scratch_shapes=[pltpu.VMEM((width, width), bf16), pltpu.SemaphoreType.DMA],
        compiler_params=params(60),
        cost_estimate=short(),
        name="back_mid",
    )(mid, ct, gain, h2, router_w, dense_w, parts, *tokens)


def back_in_kernel(S, x_ref, gain_ref, d_ref, diag_ref, hot_ref, extra_ref, dmid_ref, w_hbm, *refs):
    dx_ref, small_ref, token, w_s, sem = refs[-5:]
    give(token)
    n, width = x_ref.shape
    load = pltpu.make_async_copy(w_hbm.at[:, pl.ds(0, 3 * width)], w_s, sem)
    load.start()
    diag = jnp.concatenate(
        [jnp.zeros((8, n), f32), diag_ref[...], jnp.zeros((LANES - 8 - HEADS, n), f32)], axis=0
    )
    high, rest = hi_lo(diag)
    table = dot_nt(hot_ref[...], high) + dot_nt(hot_ref[...], rest)
    part, count = width // S, BUCKETS // S
    places = lax.broadcasted_iota(jnp.int32, (16, BUCKETS), 0)
    buckets = lax.broadcasted_iota(jnp.int32, (16, BUCKETS), 1)
    high, rest = hi_lo(table)
    x = x_ref[...].astype(f32)
    scale = lax.rsqrt(jnp.mean(x * x, axis=-1, keepdims=True) + eps)
    load.wait()
    dh = dot_nt(d_ref[0], w_s[:, :width])
    dh = dh + dot_nt(d_ref[1], w_s[:, width : 2 * width])
    dh = dh + dot_nt(d_ref[2], w_s[:, 2 * width :])
    wide = lax.broadcasted_iota(jnp.int32, (width, LANES), 1)
    extra = jnp.where(wide == 0, sum_columns(dh * x * scale), extra_ref[...])
    small_ref[...] = jnp.where(wide < 2 + EXPERTS, extra, 0.0).astype(bf16)
    for s in range(S):
        pick = ((places < count) & (buckets == places + s * count)).astype(bf16)
        cut = slice(s * part, s * part + 16)
        rows = dot_nn(pick, high) + dot_nn(pick, rest) + small_ref[cut, :].astype(f32)
        small_ref[cut, :] = rows.astype(bf16)
    weighted = dh * gain_ref[...]
    dz = scale * weighted - x * (scale * scale * scale) * jnp.mean(
        x * weighted, axis=-1, keepdims=True
    )
    dx_ref[...] = (dz + dmid_ref[...]).astype(bf16)


def back_in(S, x, gain, d3, diag, hot, extra, dmid, dense_w, tokens):
    n, width = x.shape
    return pl.pallas_call(
        functools.partial(back_in_kernel, S),
        in_specs=[vmem()] * 7 + [hbm()] + [anywhere()] * len(tokens),
        out_specs=[vmem()] * 3,
        out_shape=[
            jax.ShapeDtypeStruct((n, width), bf16),
            jax.ShapeDtypeStruct((width, LANES), bf16),
            TOKEN,
        ],
        scratch_shapes=[pltpu.VMEM((width, 3 * width), bf16), pltpu.SemaphoreType.DMA],
        compiler_params=params(60),
        cost_estimate=short(),
        name="back_in",
    )(x, gain, d3, diag, hot, extra, dmid, dense_w, *tokens)


def dense_kernel(S, N, with_small, core_ref, *refs):
    left, left_o, *refs = refs
    right, refs = refs[: 2 * N], refs[2 * N :]
    out, token = refs[-2:]
    give(token)
    core = core_ref[0]
    width = left.shape[1]
    half, many = width // (2 * S), width // PANEL
    for s in range(S):
        a, b = core_columns(left, core, s, half), core_columns(left_o, core, s, half)
        for j in range(N):
            total = (dot_tn(a, right[j][...]) + dot_tn(b, right[N + j][...])).astype(bf16)
            for p in range(many):
                rows = slice((j * many + p) * half, (j * many + p + 1) * half)
                out[s, rows, :] = total[:, p * PANEL : (p + 1) * PANEL]
        if with_small:
            low, high = slice(2 * s * half, (2 * s + 1) * half), slice((2 * s + 1) * half, (2 * s + 2) * half)
            total = [
                jnp.where(core == 0, r[low, :], r[high, :]).astype(f32) for r in refs[:2]
            ]
            rows = slice(N * many * half, (N * many + 1) * half)
            out[s, rows, :LANES] = (total[0] + total[1]).astype(bf16)
            out[s, rows, LANES:] = jnp.zeros((half, PANEL - LANES), bf16)


def dense_grads_of(S, core, left, left_o, right, right_o, small, tokens):
    n, width = left.shape
    if isinstance(right, list):
        N, arrays = len(right), right + right_o
        specs = [vmem()] * (2 * N)
    else:
        N, arrays = 3, [right] * 3 + [right_o] * 3
        specs = [pl.BlockSpec((None, n, width), lambda i, j=j: (j, 0, 0)) for j in range(3)] * 2
    panels = N * (width // PANEL) + (1 if small else 0)
    shape = (S, panels * width // (2 * S), PANEL)

    def whole(x):
        return pl.BlockSpec(x.shape, lambda i: (0,) * x.ndim)

    out, token = pl.pallas_call(
        functools.partial(dense_kernel, S, N, bool(small)),
        grid=(1,),
        in_specs=[smem(), whole(left), whole(left_o)]
        + ([whole(x) for x in arrays] if isinstance(right, list) else specs)
        + [whole(x) for x in small]
        + [anywhere()] * len(tokens),
        out_specs=[pl.BlockSpec(shape, lambda i: (0, 0, 0)), token_spec()],
        out_shape=[jax.ShapeDtypeStruct(shape, bf16), TOKEN],
        compiler_params=params(60),
        cost_estimate=short(),
        name="dense",
    )(core, left, left_o, *arrays, *small, *tokens)
    return out, [token]


def wave_kernel(shapes_in, shapes_out, *refs):
    place_ref = refs[0]
    line, core = place_ref[0], place_ref[1]
    inner = (line == 1) | (line == 2)
    get = dict(zip(shapes_in, refs[1:]))
    put = dict(zip(shapes_out, refs[len(refs) - len(shapes_out) :]))
    give(put["token"])

    def add(a, b):
        return (get[a][...].astype(f32) + get[b][...].astype(f32)).astype(bf16)

    if "mid" in put:
        put["mid"][...] = add("s0", "got_pair")
    if "core" in put:
        put["core"][...] = jnp.where(inner, get["pair"][...], get["got_pair"][...])
    new = None
    if "keep" in get:
        new = add("keep", "recv") if "recv" in get else get["keep"][...]
    full = add("mid", "got_mid") if "mid" in get else None
    if new is not None:
        put["s0"][...] = new
    if "pair" in put:
        if new is None or full is None:
            put["pair"][...] = full if new is None else new
        else:
            put["pair"][...] = jnp.where(inner, full, new)
    if "final" in put:
        a, b = get["core"][...].astype(f32), get["got_core"][...].astype(f32)
        half = a.shape[1]
        put["final"][:, :half] = jnp.where(core == 0, a, b)
        put["final"][:, half:] = jnp.where(core == 0, b, a)


class Sums:
    def __init__(self, size, place):
        self.size, self.place = size, place
        self.line = size // 2 == 4
        self.queues = [[], []]
        self.state = [{}, {}]
        self.ids = [{}, {}]
        self.turn = 0
        self.added = 0
        self.dense = {}
        self.final = None
        self.targets = {}
        self.last = []

    def add(self, keep, k, recv, j, name, expert):
        if self.line:
            self.queues[self.added % 2].append((keep, k, recv, j, name, expert))
            self.added += 1
            return
        mine = line_sum((keep[k].astype(f32) + recv[j].astype(f32)).astype(bf16), self.size)
        other = swap_core(mine, self.size)
        first = self.place[1] == 0
        whole = jnp.concatenate([jnp.where(first, mine, other), jnp.where(first, other, mine)], 1)
        if name not in self.targets:
            self.targets[name] = jnp.zeros((EXPERTS,) + whole.shape, f32)
        self.targets[name] = self.targets[name].at[expert].set(whole.astype(f32))

    def busy(self):
        return any(self.queues) or any(self.state) or self.final is not None

    def begin(self):
        items = [queue.pop(0) for queue in self.queues]
        rows, cols = items[0][0].shape[1:]
        steps = max(g for g in (1, 2, 4) if rows % (16 * g) == 0)

        def block(k):
            return pl.BlockSpec((None, rows // steps, cols), lambda r: (k, r, 0))

        def kernel(*refs):
            give(refs[-1])
            outs = refs[-3:-1]
            for i in range(2):
                total = refs[2 * i][...].astype(f32) + refs[2 * i + 1][...].astype(f32)
                outs[i][...] = total.astype(bf16)

        spec = pl.BlockSpec((rows // steps, cols), lambda r: (r, 0))
        *sums, token = pl.pallas_call(
            kernel,
            grid=(steps,),
            in_specs=[block(k) for item in items for k in (item[1], item[3])]
            + [anywhere()] * len(self.last),
            out_specs=[spec, spec, token_spec()],
            out_shape=[pltpu.HBM((rows, cols), bf16)] * 2 + [TOKEN],
            compiler_params=params(60),
            cost_estimate=short(),
            name="begin",
        )(*[pin(x) for item in items for x in (item[0], item[2])], *self.last)
        self.last = [token]
        for i, item in enumerate(items):
            self.state[i] = {"s0": sums[i], "pair": sums[i]}
            self.ids[i] = {"in": (item[4], item[5])}

    def step(self, more=()):
        self.last = self.last + list(more)
        stream = self.turn
        self.turn = 1 - stream
        queue, state, ids = self.queues[stream], self.state[stream], self.ids[stream]
        rep_axis = "rep"
        ins, outs = {}, []
        if "s0" in state or "pair" in state:
            pairs = line_perm([(0, 1), (1, 0), (2, 3), (3, 2)])
            ins["got_pair"] = lax.ppermute(state["pair"], rep_axis, pairs)
        if "mid" in state:
            ins["mid"] = state["mid"]
            ins["got_mid"] = lax.ppermute(state["mid"], rep_axis, line_perm([(1, 2), (2, 1)]))
        new_ids = {}
        if "in" in ids:
            ins["s0"] = state["s0"]
            outs.append("mid")
            new_ids["mid"] = ids["in"]
        if "out" in ids:
            ins["pair"] = state["pair"]
            outs.append("core")
        if "mid" in ids:
            new_ids["out"] = ids["mid"]
        if queue:
            keep, k, recv, j, name, expert = queue.pop(0)
            ins["keep"] = (keep, k)
            if recv is not None:
                ins["recv"] = (recv, j)
            outs.append("s0")
            new_ids["in"] = (name, expert)
        if "in" in new_ids or "out" in new_ids:
            outs.append("pair")
        if self.final is not None:
            value, (name, expert) = self.final
            ins["core"] = value
            ins["got_core"] = swap_core(value, self.size)
            outs.append("final")
        if not outs:
            self.state[stream] = {}
            return
        result = self.kernel(ins, outs, self.final[1] if self.final is not None else None)
        if self.final is not None:
            self.targets[self.final[1][0]] = result["final"]
        self.final = None
        if "core" in outs:
            if ids["out"][1] is None:
                self.dense[ids["out"][0]] = result["core"]
            else:
                self.final = (result["core"], ids["out"])
        self.last = [result["token"]]
        self.state[stream] = {key: result[key] for key in ("s0", "mid", "pair") if key in outs}
        self.ids[stream] = new_ids

    def kernel(self, ins, outs, final):
        arrays, specs = [], []
        rows, cols = next(
            (x[0].shape[1:] if isinstance(x, tuple) else x.shape) for x in ins.values()
        )
        steps = max(g for g in (1, 2, 4) if rows % (16 * g) == 0)
        spec = pl.BlockSpec((rows // steps, cols), lambda r: (r, 0))
        for x in ins.values():
            if isinstance(x, tuple):
                arrays.append(pin(x[0]))
                specs.append(
                    pl.BlockSpec((None, rows // steps, cols), lambda r, k=x[1]: (k, r, 0))
                )
            else:
                arrays.append(x)
                specs.append(spec)
        shape = pltpu.HBM((rows, cols), bf16)
        out_specs, out_shapes, extra, aliases = [], [], [], {}
        for i, key in enumerate(outs):
            if key == "final":
                name, expert = final
                out_specs.append(
                    pl.BlockSpec((None, rows // steps, 2 * cols), lambda r: (expert, r, 0))
                )
                out_shapes.append(pltpu.HBM((EXPERTS, rows, 2 * cols), f32))
                if name in self.targets:
                    extra.append(pin(self.targets[name]))
                    aliases[1 + len(arrays)] = i
            else:
                out_specs.append(spec)
                out_shapes.append(shape)
        values = pl.pallas_call(
            functools.partial(wave_kernel, tuple(ins), tuple(outs) + ("token",)),
            grid=(steps,),
            in_specs=[smem()] + specs + [anywhere()] * (len(extra) + len(self.last)),
            out_specs=out_specs + [token_spec()],
            out_shape=out_shapes + [TOKEN],
            input_output_aliases=aliases,
            compiler_params=params(60),
            cost_estimate=short(),
            name="wave",
        )(self.place, *arrays, *extra, *self.last)
        return dict(zip(tuple(outs) + ("token",), values))


def assemble_kernel(half, many, place_ref, *refs):
    mine, other, outs = refs[:2], refs[2:4], refs[4:]
    core = place_ref[1]

    def rows(parts, first):
        cut = parts[0].shape[0]
        if first + half <= cut:
            return parts[0][first : first + half, :]
        if first >= cut:
            return parts[1][first - cut : first - cut + half, :]
        return jnp.concatenate([parts[0][first:, :], parts[1][: first + half - cut, :]], axis=0)

    def put(out, column, p, width):
        a = rows(mine, p * half)[:, :width].astype(f32)
        b = rows(other, p * half)[:, :width].astype(f32)
        out[:half, column : column + width] = jnp.where(core == 0, a, b)
        out[half:, column : column + width] = jnp.where(core == 0, b, a)

    for j in range(4):
        for q in range(many):
            put(outs[j], q * PANEL, j * many + q + (1 if j == 3 else 0), PANEL)
    small = outs[6]
    put(small, 0, 3 * many, LANES)
    outs[4][...] = small[:, 2 : 2 + EXPERTS]
    outs[5][...] = small[: outs[5].shape[0], 8 : 8 + HEADS]


def assemble(place, half, width, mine, other):
    shapes = [jax.ShapeDtypeStruct((2 * half, width), f32)] * 4
    shapes.append(jax.ShapeDtypeStruct((2 * half, EXPERTS), f32))
    shapes.append(jax.ShapeDtypeStruct((BUCKETS * 2 * half // width, HEADS), f32))
    shapes.append(jax.ShapeDtypeStruct((2 * half, LANES), f32))
    return pl.pallas_call(
        functools.partial(assemble_kernel, half, width // PANEL),
        in_specs=[smem()] + [vmem()] * 4,
        out_specs=[vmem()] * 7,
        out_shape=shapes,
        compiler_params=params(60),
        cost_estimate=short(),
        name="assemble",
    )(place, *mine, *other)


def swap_core(x, size):
    return lax.ppermute(x, "rep", [(i, i ^ 1) for i in range(size)])


def swap_shard(x, size, mask):
    return lax.ppermute(x, "shard", [(i, i ^ mask) for i in range(size)])


def line_perm(pairs):
    return [(2 * a + c, 2 * b + c) for a, b in pairs for c in range(2)]


def after(x, *others):
    return lax.optimization_barrier((x,) + others)[0]


def relay_gather(top, bottom, S):
    if S != 4:
        x = jnp.concatenate([top, bottom], axis=0)
        return [[x]] + [[swap_shard(x, S, m)] for m in range(1, S)]
    one_top, two_bottom = swap_shard(top, S, 1), swap_shard(bottom, S, 2)
    one = [one_top, swap_shard(bottom, S, 1)]
    two = [swap_shard(top, S, 2), two_bottom]
    return [[top, bottom], one, two, [swap_shard(one_top, S, 2), swap_shard(two_bottom, S, 1)]]


def relay_whole(x, S):
    if S != 4:
        return [[x]] + [[swap_shard(x, S, m)] for m in range(1, S)]
    cut = x.shape[0] // 2
    one, two = swap_shard(x, S, 1), swap_shard(x, S, 2)
    return [[x], [one], [two], [swap_shard(one[:cut], S, 2), swap_shard(two[cut:], S, 1)]]


def line_sum(x, size):
    n = size // 2
    h = n // 2
    line = lax.axis_index("rep") // 2
    for k in range(h - 1):
        x = x + lax.ppermute(x, "rep", line_perm([(k, k + 1), (n - 1 - k, n - 2 - k)]))
    x = x + lax.ppermute(x, "rep", line_perm([(h - 1, h), (h, h - 1)]))
    for k in reversed(range(h - 1)):
        got = lax.ppermute(x, "rep", line_perm([(k + 1, k), (n - 2 - k, n - 1 - k)]))
        x = jnp.where((line == k) | (line == n - 1 - k), got, x)
    return x


def deal_out(x):
    return lax.all_to_all(x, "shard", 0, 0, tiled=True)


def bucket_of(distance):
    bucket = jnp.minimum(distance, 16)
    for border in bucket_edges:
        bucket = bucket + (distance >= border).astype(jnp.int32)
    return bucket


def slot_positions(routes, order, lengths):
    n = order.shape[1]
    valid = jnp.arange(n, dtype=jnp.int32)[None, :] < lengths[:, None]
    experts = jnp.arange(EXPERTS, dtype=jnp.int32)
    hits = (routes[:, :, :, None] == experts) & valid[:, :, None, None]
    hits = hits.reshape(routes.shape[0], n, 2 * EXPERTS)
    before = (order[:, None, :] < order[:, :, None]).astype(bf16)
    count = jnp.einsum("stk,sut->sku", hits.astype(bf16), before, preferred_element_type=f32)
    total = jnp.sum(hits[:, :, :EXPERTS].astype(f32), axis=1)
    hits = jnp.swapaxes(hits, 1, 2)
    first, second = count[:, :EXPERTS], count[:, EXPERTS:] + total[:, :, None]
    slot = jnp.where(
        hits[:, :EXPERTS], first, jnp.where(hits[:, EXPERTS:], second, float(2 * CAP + n))
    )
    return jnp.where(slot < CAP, slot, -1.0).astype(jnp.int32)


def shards(
    R,
    S,
    tokens,
    cotangent,
    lengths,
    sequence_deal,
    routes,
    fill_order,
    norm_attn,
    w_query,
    w_key,
    w_value,
    w_out,
    rel_bias,
    norm_ffn,
    w_router,
    w_gate,
    w_up,
    w_down,
):
    me = lax.axis_index("shard")
    rep = lax.axis_index("rep")
    core = rep % 2
    line = rep // 2
    x_low, ct_low = tokens[0], cotangent[0]
    n, width = x_low.shape
    part = width // S
    half = part // 2
    group = jnp.arange(S, dtype=jnp.int32)

    dense = (w_query, w_key, w_value, w_out)
    cut = half // 2

    def rows_for_core(first):
        return jnp.where(
            core == 0,
            jnp.concatenate([w[first : first + cut] for w in dense], axis=1),
            jnp.concatenate([w[half + first : half + first + cut] for w in dense], axis=1),
        )

    stack = rows_for_core(0)
    blocks = relay_gather(stack, rows_for_core(cut), S)
    count = len(blocks[-1])
    pieces, places = [], []
    for m in range(1, S):
        place = 2 * count * (me ^ m)
        each = count // len(blocks[m])
        pieces += blocks[m]
        places += [place + count * core + j * each for j in range(len(blocks[m]))]
        for j, block in enumerate(blocks[m]):
            pieces.append(swap_core(block, R))
            places.append(place + count * (1 - core) + j * each)
    offsets = jnp.stack(places + [2 * count * me]).astype(jnp.int32)
    ct_all = relay_whole(after(ct_low, *blocks[-1]), S)

    bias_flat = jnp.pad(rel_bias.reshape(-1), (0, part - rel_bias.size))
    small = jnp.concatenate(
        [norm_attn[:, None], norm_ffn[:, None], w_router, bias_flat[:, None]], axis=1
    )
    small = jnp.pad(small, ((0, n - part), (0, 0)))
    plan = jnp.concatenate([routes[0], fill_order[0][:, None]], axis=1).astype(bf16)
    small = jnp.concatenate([small, plan], axis=1)
    small = after(small, stack)
    small_all = deal_out(jnp.broadcast_to(small[None], (S,) + small.shape))
    plan_all = small_all[:, :, 3 + EXPERTS :]
    small_all = small_all[:, :part]
    gain_one = small_all[:, :, 0].reshape(-1).astype(f32)
    gain_two = small_all[:, :, 1].reshape(-1).astype(f32)
    router_w = small_all[:, :, 2 : 2 + EXPERTS].reshape(width, EXPERTS)
    bias_table = small_all[:, : rel_bias.size, 2 + EXPERTS].reshape(BUCKETS, HEADS)

    length = lax.dynamic_slice_in_dim(lengths[0], me, 1, 0)

    turned = jnp.arange(n, dtype=jnp.int32)
    hot = (bucket_of((n - turned) % n)[None, :] == jnp.arange(BUCKETS)[:, None]).astype(bf16)
    base = dot_tn(bias_table, hot)

    normed_low, qkv, context, middle, ffn_in, dense_w, bias = attn_fwd(
        offsets, length, x_low, gain_one[None], gain_two[None], base, dense, pieces
    )

    plan_all = after(plan_all, ffn_in).astype(jnp.int32)
    deal = sequence_deal[0]
    row_of = jnp.sum(group[:, None] * (deal[:, None] == group[None, :]).astype(jnp.int32), axis=0)
    homes = me ^ group
    plans = jnp.take(plan_all, jnp.take(row_of, homes), axis=0)
    pos = slot_positions(plans[:, :, :2], plans[:, :, 2], jnp.take(lengths[0], homes))

    h2_all = relay_whole(ffn_in, S)
    router_pad = jnp.pad(router_w, ((0, 0), (0, LANES - EXPERTS)))
    core_one = core.reshape(1).astype(jnp.int32)
    place = jnp.stack([line, core]).astype(jnp.int32)
    me_one = me.reshape(1).astype(jnp.int32)
    where = jnp.stack([me, core]).astype(jnp.int32)
    weights = [pin(w) for w in (jnp.swapaxes(w_gate, 1, 2), jnp.swapaxes(w_up, 1, 2), w_down)]
    sums = Sums(R, place)
    h1_other, context_other = swap_core(normed_low, R), swap_core(context, R)
    chain, aux = (), router_pad
    for experts, groups in (((0, 1), (2, 2, 2)), ((2, 3), (2, 2, 2))):
        first = sums.last if experts[0] == 0 else sums.last + [h1_other, context_other]
        got = ffn(experts, groups, where, pos, aux, h2_all, ct_all, weights, chain, first)
        M = 1 + len(groups)
        keep, sends, chain = got[0], got[1:M], got[M : M + 2]
        sums.last = [got[M + 2]]
        if experts[0] == 0:
            aux = got[-1]
        where_to = [(g, k) for g, size in enumerate(groups) for k in range(size)]
        recvs = [swap_core(x, R) for x in sends]
        for i, e in enumerate(experts):
            for j, name in enumerate(("down", "gate", "up")):
                g, k = where_to[3 * i + j]
                sums.add(keep, 3 * i + j, recvs[g], k, name, e)
        if experts[0] == 0 and sums.line:
            sums.begin()

    def run(steps, more=()):
        for _ in range(steps):
            if sums.line and sums.busy():
                sums.step(more)

    flat = jnp.arange(EXPERTS, dtype=jnp.int32) * CAP
    pos_col = jnp.swapaxes(jnp.where(pos < 0, -1, pos + flat[None, :, None]), 1, 2)
    pos_col = jnp.pad(pos_col, ((0, 0), (0, 0), (0, LANES - EXPERTS)))
    run(2)
    d_parts, sums.last = combine(me_one, pos_col, chain[1], sums.last)
    d_parts = deal_out(d_parts)
    run(1)
    run(1, recvs)

    dmid, dm, dc, extra, token = back_mid(
        S, middle, ct_low, gain_two[None], ffn_in, router_pad, dense_w, d_parts, sums.last
    )
    sums.last = [token]
    run(0)
    d3, diag, token = attn_bwd(qkv, bias, dc, sums.last)
    sums.last = [token]
    run(2)
    out_grads, sums.last = dense_grads_of(
        S, core_one, context, context_other, [dm], [swap_core(dm, R)], [], sums.last
    )
    out_grads = deal_out(out_grads)
    run(0)
    grad_x, extra, token = back_in(
        S, x_low, gain_one[None], d3, diag.reshape(HEADS, n), hot, extra, dmid, dense_w, sums.last
    )
    sums.last = [token]
    run(1)
    in_grads, sums.last = dense_grads_of(
        S, core_one, normed_low, h1_other, d3, swap_core(d3, R), [extra, swap_core(extra, R)], sums.last
    )
    in_grads = deal_out(in_grads)
    run(3)
    out_parts, sums.last = combine(me_one, pos_col, chain[0], sums.last)
    out_parts = deal_out(out_parts)
    run(2)

    owned = [jnp.sum(x.astype(f32), axis=0).astype(bf16) for x in (in_grads, out_grads)]
    owned = jnp.concatenate(owned, axis=0)
    rows, cut = owned.shape[0], weights[0].shape[1]
    if sums.line and rows <= 2 * cut:
        owned = jnp.pad(owned, ((0, 2 * cut - rows), (0, 0)))[None]
        sums.add(owned[:, :cut], 0, None, 0, "top", None)
        sums.add(owned[:, cut:], 0, None, 0, "bottom", None)
        run(1)
    else:
        owned = line_sum(owned, R)
        sums.dense = {"top": owned[: rows // 2], "bottom": owned[rows // 2 :]}
    run(4)
    result = (middle + jnp.sum(out_parts.astype(f32), axis=0)).astype(bf16)
    run(1, [result])
    run(100)
    mine = [sums.dense["top"], sums.dense["bottom"]]
    *dense_grads, grad_router_w, grad_table, small = assemble(place, half, width, mine, [swap_core(x, R) for x in mine])
    return (
        result[None],
        grad_x[None],
        small[:, 0],
        *dense_grads,
        grad_table,
        small[:, 1],
        grad_router_w,
        jnp.swapaxes(sums.targets["gate"], 1, 2),
        jnp.swapaxes(sums.targets["up"], 1, 2),
        sums.targets["down"],
    )


def solution(mesh):
    R, S = mesh.shape["rep"], mesh.shape["shard"]
    rows = P(("rep", "shard"), None, None)
    mat = P("shard", None)
    return jax.shard_map(
        functools.partial(shards, R, S),
        mesh=mesh,
        in_specs=(rows, rows, P("rep", None), P("rep", None), rows, P(("rep", "shard"), None))
        + (P("shard"), mat, mat, mat, mat, mat, P("shard"), mat)
        + (P(None, None, "shard"), P(None, None, "shard"), P(None, "shard", None)),
        out_specs=(rows, rows, P("shard"), mat, mat, mat, mat, mat, P("shard"), mat)
        + (P(None, None, "shard"), P(None, None, "shard"), P(None, "shard", None)),
        check_vma=False,
    )
```

```python
import functools
import math

import jax
import jax.numpy as jnp
from jax import lax
from jax.experimental import pallas as pl
from jax.experimental.pallas import tpu as pltpu
from jax.sharding import PartitionSpec as P

HEADS = 16
HEAD_DIM = 64
EXPERTS = 4
BUCKETS = 32
CAP = 144
LANES = 128

eps = 1e-06
bucket_edges = [int(math.ceil(16.0 * 8.0 ** (level / 16.0))) for level in range(1, 16)]
bf16 = jnp.bfloat16
f32 = jnp.float32


def dot_nn(a, b):
    return lax.dot_general(a, b, (((1,), (0,)), ((), ())), preferred_element_type=f32)


def dot_nt(a, b):
    return lax.dot_general(a, b, (((1,), (1,)), ((), ())), preferred_element_type=f32)


def dot_tn(a, b):
    return lax.dot_general(a, b, (((0,), (0,)), ((), ())), preferred_element_type=f32)


def params(mib):
    return pltpu.CompilerParams(vmem_limit_bytes=mib * 1024 * 1024)


def vmem():
    return pl.BlockSpec(memory_space=pltpu.VMEM)


def anywhere():
    return pl.BlockSpec(memory_space=pl.ANY)


TOKEN = jax.ShapeDtypeStruct((8, LANES), f32)


def token_spec():
    return pl.BlockSpec((8, LANES), lambda *i: (0, 0))


def give(token):
    token[...] = jnp.zeros(token.shape, token.dtype)


def short():
    return pl.CostEstimate(flops=1, bytes_accessed=1, transcendentals=0)


def hbm():
    return pl.BlockSpec(memory_space=pltpu.HBM)


def pin(x):
    return pltpu.with_memory_space_constraint(x, pltpu.HBM)


def smem():
    return pl.BlockSpec(memory_space=pltpu.SMEM)


def softmax_of(q, k, bias):
    s = dot_nt(q, k) * 0.125 + bias.astype(f32)
    e = jnp.exp(s - jnp.max(s, axis=-1, keepdims=True))
    return e * (1.0 / jnp.sum(e, axis=-1, keepdims=True))


def attn_fwd_kernel(N, *refs):
    off_ref, len_ref, x_ref, gain_ref, gain2_ref, base_ref = refs[:6]
    own, pieces = refs[6:10], refs[10 : 10 + N]
    h_ref, qkv_ref, c_ref, mid_ref, h2_ref, wout_ref, bias_hbm, w_s, bias_ref, sem, sems = refs[10 + N :]
    n, width = x_ref.shape
    unit = min(piece.shape[0] for piece in pieces)
    copies = []
    first = pl.multiple_of(off_ref[N] * unit, unit)
    for j in range(4):
        dest = w_s.at[pl.ds(first, own[j].shape[0]), pl.ds(j * width, width)]
        copies.append(pltpu.make_async_copy(own[j], dest, sems.at[N + j]))
    for p, piece in enumerate(pieces):
        start = pl.multiple_of(off_ref[p] * unit, unit)
        copies.append(
            pltpu.make_async_copy(piece, w_s.at[pl.ds(start, piece.shape[0])], sems.at[p])
        )
    for copy in copies:
        copy.start()
    x = x_ref[...].astype(f32)
    scale = lax.rsqrt(jnp.mean(x * x, axis=-1, keepdims=True) + eps)
    h_ref[...] = (x * scale * gain_ref[...]).astype(bf16)
    rows = lax.broadcasted_iota(jnp.int32, (n, n), 0)
    cols = lax.broadcasted_iota(jnp.int32, (n, n), 1)
    allowed = (cols <= rows) & (cols < len_ref[0])
    for h in range(HEADS):
        row = jnp.broadcast_to(base_ref[h : h + 1, :], (n, n))
        turned = pltpu.roll(row, 0, 1, stride=1, stride_axis=0)
        bias_ref[h] = jnp.where(allowed, turned, -1000000000.0).astype(bf16)
    outs = [pltpu.make_async_copy(bias_ref, bias_hbm, sem.at[0])]
    outs.append(pltpu.make_async_copy(w_s, wout_ref, sem.at[1]))
    outs[0].start()
    for copy in copies:
        copy.wait()
    outs[1].start()
    step = width // 2

    def project(i, carry):
        cut = pl.ds(pl.multiple_of(i * step, step), step)
        qkv_ref[:, cut] = dot_nn(h_ref[...], w_s[:, cut]).astype(bf16)
        return carry

    lax.fori_loop(0, 3 * width // step, project, 0)

    def some_heads(i, carry):
        def at(j):
            return pl.ds(pl.multiple_of(j * width + i * 2 * LANES, LANES), 2 * LANES)

        q, k, v = qkv_ref[:, at(0)], qkv_ref[:, at(1)], qkv_ref[:, at(2)]
        heads = []
        for h in range(4):
            cut = slice(h * HEAD_DIM, (h + 1) * HEAD_DIM)
            p = softmax_of(q[:, cut], k[:, cut], bias_ref[4 * i + h]).astype(bf16)
            heads.append(dot_nn(p, v[:, cut]).astype(bf16))
        c_ref[:, at(0)] = jnp.concatenate(heads, axis=1)
        return carry

    lax.fori_loop(0, HEADS // 4, some_heads, 0)
    mid = x_ref[...].astype(f32) + dot_nn(c_ref[...], w_s[:, 3 * width :])
    scale = lax.rsqrt(jnp.mean(mid * mid, axis=-1, keepdims=True) + eps)
    mid_ref[...] = mid
    h2_ref[...] = (mid * scale * gain2_ref[...]).astype(bf16)
    for copy in outs:
        copy.wait()


def attn_fwd(offsets, length, x, gain, gain_two, base, own, pieces):
    n, width = x.shape
    N = len(pieces)
    full = jax.ShapeDtypeStruct((n, width), bf16)
    return pl.pallas_call(
        functools.partial(attn_fwd_kernel, N),
        in_specs=[smem(), smem(), vmem(), vmem(), vmem(), vmem()] + [anywhere()] * (4 + N),
        out_specs=[vmem()] * 5 + [hbm()] * 2,
        out_shape=[
            full,
            jax.ShapeDtypeStruct((n, 3 * width), bf16),
            full,
            jax.ShapeDtypeStruct((n, width), f32),
            full,
            pltpu.HBM((width, 4 * width), bf16),
            pltpu.HBM((HEADS, n, n), bf16),
        ],
        scratch_shapes=[
            pltpu.VMEM((width, 4 * width), bf16),
            pltpu.VMEM((HEADS, n, n), bf16),
            pltpu.SemaphoreType.DMA((2,)),
            pltpu.SemaphoreType.DMA((N + 4,)),
        ],
        compiler_params=params(60),
        cost_estimate=short(),
        name="attn_fwd",
    )(offsets, length, x, gain, gain_two, base, *own, *pieces)


def attn_bwd_kernel(q_ref, k_ref, v_ref, bias_ref, dc_ref, *refs):
    d_ref, diag_ref, token = refs[-3:]
    give(token)
    n = q_ref.shape[0]
    rows = lax.broadcasted_iota(jnp.int32, (n, n), 0)
    cols = lax.broadcasted_iota(jnp.int32, (n, n), 1)
    reverse = (rows + cols == n - 1).astype(bf16)
    for h in range(4):
        cut = slice(h * HEAD_DIM, (h + 1) * HEAD_DIM)
        q, k, v, dc = q_ref[:, cut], k_ref[:, cut], v_ref[:, cut], dc_ref[:, cut]
        p = softmax_of(q, k, bias_ref[h])
        dp = dot_nt(dc, v)
        ds = p * (dp - jnp.sum(p * dp, axis=-1, keepdims=True))
        low = ds.astype(bf16)
        d_ref[0, :, cut] = (dot_nn(low, k) * 0.125).astype(bf16)
        d_ref[1, :, cut] = (dot_tn(low, q) * 0.125).astype(bf16)
        d_ref[2, :, cut] = dot_tn(p.astype(bf16), dc).astype(bf16)
        turned = pltpu.roll(dot_nn(reverse, low), 1, 1, stride=1, stride_axis=0)
        diag_ref[0, h : h + 1, :] = jnp.sum(turned, axis=0, keepdims=True)


def attn_bwd(qkv, bias, dc, tokens):
    n = qkv.shape[0]
    steps = HEADS // 4
    blk = pl.BlockSpec((n, 2 * LANES), lambda i: (0, i))
    row = pl.BlockSpec((1, 4, n), lambda i: (i, 0, 0))
    return pl.pallas_call(
        attn_bwd_kernel,
        grid=(steps,),
        in_specs=[
            blk,
            pl.BlockSpec((n, 2 * LANES), lambda i: (0, steps + i)),
            pl.BlockSpec((n, 2 * LANES), lambda i: (0, 2 * steps + i)),
            pl.BlockSpec((4, n, n), lambda i: (i, 0, 0)),
            blk,
        ]
        + [anywhere()] * len(tokens),
        out_specs=[pl.BlockSpec((3, n, 2 * LANES), lambda i: (0, 0, i)), row, token_spec()],
        out_shape=[
            jax.ShapeDtypeStruct((3, n, HEADS * HEAD_DIM), bf16),
            jax.ShapeDtypeStruct((steps, 4, n), f32),
            TOKEN,
        ],
        compiler_params=params(60),
        cost_estimate=short(),
        name="attn_bwd",
    )(qkv, qkv, qkv, bias, dc, *tokens)


def rows_of(refs):
    return refs[0][...] if len(refs) == 1 else jnp.concatenate([r[...] for r in refs], axis=0)


def ffn_kernel(shape, experts, groups, n_after, *refs):
    S, n_seq, first = len(shape), sum(shape), experts[0] == 0
    where_ref, pos_ref, aux_ref = refs[:3]
    refs = refs[3:]

    def sequences(parts):
        out, at = [], 0
        for count in shape:
            out.append(parts[at : at + count])
            at += count
        return out

    h2, ct = sequences(refs[:n_seq]), sequences(refs[n_seq : 2 * n_seq])
    refs = refs[2 * n_seq :]
    w_hbm = refs[:3]
    refs = refs[3 + n_after + (0 if first else 2) :]
    keeps, sends, (e_all, d_all, token) = refs[0], refs[1 : 1 + len(groups)], refs[1 + len(groups) : 4 + len(groups)]
    give(token)
    refs = refs[4 + len(groups) :]
    where_to = [(g, k) for g, size in enumerate(groups) for k in range(size)]
    if first:
        prob_ref, refs = refs[0], refs[1:]
    else:
        prob_ref = aux_ref
    w_v, x_s, c_s, gate_s, hid_s, da_s, du_s, o_s, eo_s, dx_s, sem_l, sem_s = refs
    n, width = pos_ref.shape[2], x_s.shape[1]
    loads = [[] for _ in experts]
    for i, e in enumerate(experts):
        for j in range(3):
            copy = pltpu.make_async_copy(w_hbm[j].at[e], w_v.at[i, j], sem_l.at[i, j])
            copy.start()
            loads[i].append(copy)
    lanes = lax.broadcasted_iota(jnp.int32, (n, LANES), 1)
    slot_lanes = lax.broadcasted_iota(jnp.int32, (S * CAP, LANES), 1)
    slots = lax.broadcasted_iota(jnp.int32, (CAP, n), 0)
    if first:
        for s in range(S):
            logits = jnp.where(lanes < EXPERTS, dot_nn(rows_of(h2[s]), aux_ref[...]), -1e30)
            ex = jnp.exp(logits - jnp.max(logits, axis=-1, keepdims=True))
            prob = ex / jnp.sum(ex, axis=-1, keepdims=True)
            high = prob.astype(bf16).astype(f32)
            rest = pltpu.roll(prob - high, EXPERTS, 1)
            prob_ref[s] = jnp.where(lanes < EXPERTS, high, rest).astype(bf16)
    half_w = width // 2
    core = where_ref[1]
    mine = pl.ds(pl.multiple_of(core * half_w, half_w), half_w)
    other = pl.ds(pl.multiple_of((1 - core) * half_w, half_w), half_w)
    const = math.sqrt(2.0 / math.pi)
    pending = {}

    def store(key, i, j, src, dst):
        copy = pltpu.make_async_copy(src, dst, sem_s.at[i, j])
        copy.start()
        pending.setdefault(key, []).append(copy)

    def settle(key):
        for copy in pending.pop(key, []):
            copy.wait()

    for i, e in enumerate(experts):
        wg, wu, wd = w_v.at[i, 0], w_v.at[i, 1], w_v.at[i, 2]
        for s in range(S):
            rows = slice(s * CAP, (s + 1) * CAP)
            hot = (slots == pos_ref[s, e : e + 1, :]).astype(bf16)
            x_s[rows, :] = dot_nn(hot, rows_of(h2[s])).astype(bf16)
            c_s[rows, :] = dot_nn(hot, rows_of(ct[s])).astype(bf16)
            picked = dot_nn(hot, prob_ref[s])
            gate_s[rows, :] = jnp.broadcast_to(
                picked[:, e : e + 1] + picked[:, EXPERTS + e : EXPERTS + e + 1], (CAP, LANES)
            )
        for copy in loads[i]:
            copy.wait()
        settle("dx")
        cols, gate = hid_s.shape[1], gate_s[:, 0:1]
        dg = jnp.zeros(gate.shape, f32)
        for f in range(0, cols, 256):
            cut = slice(f, min(f + 256, cols))
            a = dot_nt(x_s[...], wg[cut, :])
            u = dot_nt(x_s[...], wu[cut, :])
            d0 = dot_nt(c_s[...], wd[cut, :])
            t = jnp.tanh(const * (a + 0.044715 * a * a * a))
            half = 0.5 * (1.0 + t)
            act = a * half
            slope = half + 0.5 * a * (1.0 - t * t) * (const * (1.0 + 3 * 0.044715 * a * a))
            hid = act * u
            dg = dg + jnp.sum(hid * d0, axis=-1, keepdims=True)
            hid_s[:, cut] = (gate * hid).astype(bf16)
            dh = gate * d0
            da_s[:, cut] = (dh * u * slope).astype(bf16)
            du_s[:, cut] = (dh * act).astype(bf16)
        dx_s[:, width:] = jnp.where(slot_lanes == e, dg, 0.0).astype(bf16)
        for j, (left, right) in enumerate(((hid_s, c_s), (da_s, x_s), (du_s, x_s))):
            settle(j)
            o_s[j] = dot_tn(left[...], right[...]).astype(bf16)
            g, k = where_to[3 * i + j]
            store(j, i, 2 * j, o_s.at[j, :, other], sends[g].at[k])
            store(j, i, 2 * j + 1, o_s.at[j, :, mine], keeps.at[3 * i + j])
        settle("eo")
        eo_s[...] = dot_nn(hid_s[...], wd[...]).astype(bf16)
        for s in range(S):
            rows = pl.ds(s * CAP, CAP)
            store("eo", i, 6 + s, eo_s.at[rows], e_all.at[s, pl.ds(e * CAP, CAP)])
        dx_s[:, :width] = (dot_nn(da_s[...], wg[...]) + dot_nn(du_s[...], wu[...])).astype(bf16)
        for s in range(S):
            rows = pl.ds(s * CAP, CAP)
            store("dx", i, 6 + S + s, dx_s.at[rows], d_all.at[s, pl.ds(e * CAP, CAP)])
    for key in list(pending):
        settle(key)


def ffn(experts, groups, core, pos, aux, h2, ct, weights, chain, after):
    shape = tuple(len(blocks) for blocks in h2)
    S, n_seq, N = len(shape), sum(shape), len(experts)
    n = pos.shape[2]
    cols, width = weights[0].shape[1:]
    rows = S * CAP
    first = experts[0] == 0
    shapes = [pltpu.HBM((k, cols, width // 2), bf16) for k in (3 * N,) + groups] + [
        pltpu.HBM((S, EXPERTS * CAP, width), bf16),
        pltpu.HBM((S, EXPERTS * CAP, width + LANES), bf16),
        TOKEN,
    ]
    M = 1 + len(groups)
    specs = [hbm()] * (M + 2) + [vmem()]
    if first:
        shapes.append(jax.ShapeDtypeStruct((S, n, LANES), bf16))
        specs.append(vmem())
    at = 6 + 2 * n_seq + len(after)
    return pl.pallas_call(
        functools.partial(ffn_kernel, shape, experts, groups, len(after)),
        in_specs=[smem()]
        + [vmem()] * (2 + 2 * n_seq)
        + [hbm()] * 3
        + [anywhere()] * len(after)
        + [hbm()] * (0 if first else 2),
        out_specs=specs,
        out_shape=shapes,
        input_output_aliases={} if first else {at: M, at + 1: M + 1},
        scratch_shapes=[pltpu.VMEM((N, 3, cols, width), bf16)]
        + [pltpu.VMEM((rows, width), bf16)] * 2
        + [pltpu.VMEM((rows, LANES), f32)]
        + [pltpu.VMEM((rows, cols), bf16)] * 3
        + [pltpu.VMEM((3, cols, width), bf16)]
        + [pltpu.VMEM((rows, width), bf16), pltpu.VMEM((rows, width + LANES), bf16)]
        + [pltpu.SemaphoreType.DMA((N, 3)), pltpu.SemaphoreType.DMA((N, 6 + 2 * S))],
        compiler_params=params(60),
        cost_estimate=short(),
        name=f"ffn{experts[0]}",
    )(
        core,
        pos,
        aux,
        *[b for blocks in h2 for b in blocks],
        *[b for blocks in ct for b in blocks],
        *weights,
        *after,
        *([] if first else [pin(x) for x in chain]),
    )


def combine_kernel(me_ref, pos_ref, src_ref, *refs):
    out, token = refs[-2:]
    give(token)
    n = pos_ref.shape[0]
    lanes = lax.broadcasted_iota(jnp.int32, (n, EXPERTS * CAP), 1)
    hot = lanes == pos_ref[:, 0:1]
    for e in range(1, EXPERTS):
        hot = hot | (lanes == pos_ref[:, e : e + 1])
    out[...] = dot_nn(hot.astype(bf16), src_ref[...]).astype(bf16)


def combine(me, pos_col, src, tokens):
    S, n = pos_col.shape[:2]
    width = src.shape[2]
    out, token = pl.pallas_call(
        combine_kernel,
        grid_spec=pltpu.PrefetchScalarGridSpec(
            num_scalar_prefetch=1,
            grid=(S,),
            in_specs=[
                pl.BlockSpec((None, n, LANES), lambda s, me: (s, 0, 0)),
                pl.BlockSpec((None, EXPERTS * CAP, width), lambda s, me: (s, 0, 0)),
            ]
            + [anywhere()] * len(tokens),
            out_specs=[
                pl.BlockSpec((None, n, width), lambda s, me: (jnp.bitwise_xor(me[0], s), 0, 0)),
                token_spec(),
            ],
        ),
        out_shape=[jax.ShapeDtypeStruct((S, n, width), bf16), TOKEN],
        compiler_params=params(60),
        cost_estimate=short(),
        name="combine",
    )(me, pos_col, src, *tokens)
    return out, [token]


PANEL = 512


def core_columns(ref, core, s, half):
    low = ref[:, 2 * s * half : (2 * s + 1) * half]
    return jnp.where(core == 0, low, ref[:, (2 * s + 1) * half : (2 * s + 2) * half])


def hi_lo(x):
    high = x.astype(bf16)
    return high, (x - high.astype(f32)).astype(bf16)


def sum_columns(x):
    ones = jnp.ones((x.shape[0], LANES), bf16)
    high, rest = hi_lo(x)
    return dot_tn(high, ones) + dot_tn(rest, ones)


def back_mid_kernel(S, *refs):
    mid_ref, ct_ref, gain_ref, h2_ref, wr_ref, wo_hbm = refs[:6]
    parts_ref = refs[6]
    dmid_ref, low_ref, dc_ref, extra_ref, token, wo, sem_w = refs[-7:]
    give(token)
    n, width = mid_ref.shape
    load = pltpu.make_async_copy(wo_hbm.at[:, pl.ds(3 * width, width)], wo, sem_w)
    load.start()

    dh = parts_ref[0].astype(f32)
    for m in range(1, S):
        dh = dh + parts_ref[m].astype(f32)
    lanes = lax.broadcasted_iota(jnp.int32, (n, LANES), 1)
    logits = jnp.where(lanes < EXPERTS, dot_nn(h2_ref[...], wr_ref[...]), -1e30)
    ex = jnp.exp(logits - jnp.max(logits, axis=-1, keepdims=True))
    prob = ex / jnp.sum(ex, axis=-1, keepdims=True)
    drouter = dh[:, width:]
    dlogit = prob * (drouter - jnp.sum(prob * drouter, axis=-1, keepdims=True))
    high, rest = hi_lo(dlogit)
    dh2 = dh[:, :width] + dot_nt(high, wr_ref[...]) + dot_nt(rest, wr_ref[...])
    grad_router = dot_tn(h2_ref[...], high) + dot_tn(h2_ref[...], rest)
    mid = mid_ref[...]
    scale = lax.rsqrt(jnp.mean(mid * mid, axis=-1, keepdims=True) + eps)
    weighted = dh2 * gain_ref[...]
    dz = scale * weighted - mid * (scale * scale * scale) * jnp.mean(
        mid * weighted, axis=-1, keepdims=True
    )
    dmid = ct_ref[...].astype(f32) + dz
    dmid_ref[...] = dmid
    low = dmid.astype(bf16)
    low_ref[...] = low
    load.wait()
    dc_ref[...] = dot_nt(low, wo[...]).astype(bf16)
    wide = lax.broadcasted_iota(jnp.int32, (width, LANES), 1)
    gain_column = sum_columns(dh2 * mid * scale)
    extra_ref[...] = jnp.where(wide == 1, gain_column, pltpu.roll(grad_router, 2, 1))


def back_mid(S, mid, ct, gain, h2, router_w, dense_w, parts, tokens):
    n, width = mid.shape
    low = jax.ShapeDtypeStruct((n, width), bf16)
    return pl.pallas_call(
        functools.partial(back_mid_kernel, S),
        in_specs=[vmem()] * 5 + [hbm(), vmem()] + [anywhere()] * len(tokens),
        out_specs=[vmem()] * 5,
        out_shape=[
            jax.ShapeDtypeStruct((n, width), f32),
            low,
            low,
            jax.ShapeDtypeStruct((width, LANES), f32),
            TOKEN,
        ],
        scratch_shapes=[pltpu.VMEM((width, width), bf16), pltpu.SemaphoreType.DMA],
        compiler_params=params(60),
        cost_estimate=short(),
        name="back_mid",
    )(mid, ct, gain, h2, router_w, dense_w, parts, *tokens)


def back_in_kernel(S, x_ref, gain_ref, d_ref, diag_ref, hot_ref, extra_ref, dmid_ref, w_hbm, *refs):
    dx_ref, small_ref, token, w_s, sem = refs[-5:]
    give(token)
    n, width = x_ref.shape
    load = pltpu.make_async_copy(w_hbm.at[:, pl.ds(0, 3 * width)], w_s, sem)
    load.start()
    diag = jnp.concatenate(
        [jnp.zeros((8, n), f32), diag_ref[...], jnp.zeros((LANES - 8 - HEADS, n), f32)], axis=0
    )
    high, rest = hi_lo(diag)
    table = dot_nt(hot_ref[...], high) + dot_nt(hot_ref[...], rest)
    part, count = width // S, BUCKETS // S
    places = lax.broadcasted_iota(jnp.int32, (16, BUCKETS), 0)
    buckets = lax.broadcasted_iota(jnp.int32, (16, BUCKETS), 1)
    high, rest = hi_lo(table)
    x = x_ref[...].astype(f32)
    scale = lax.rsqrt(jnp.mean(x * x, axis=-1, keepdims=True) + eps)
    load.wait()
    dh = dot_nt(d_ref[0], w_s[:, :width])
    dh = dh + dot_nt(d_ref[1], w_s[:, width : 2 * width])
    dh = dh + dot_nt(d_ref[2], w_s[:, 2 * width :])
    wide = lax.broadcasted_iota(jnp.int32, (width, LANES), 1)
    extra = jnp.where(wide == 0, sum_columns(dh * x * scale), extra_ref[...])
    small_ref[...] = jnp.where(wide < 2 + EXPERTS, extra, 0.0).astype(bf16)
    for s in range(S):
        pick = ((places < count) & (buckets == places + s * count)).astype(bf16)
        cut = slice(s * part, s * part + 16)
        rows = dot_nn(pick, high) + dot_nn(pick, rest) + small_ref[cut, :].astype(f32)
        small_ref[cut, :] = rows.astype(bf16)
    weighted = dh * gain_ref[...]
    dz = scale * weighted - x * (scale * scale * scale) * jnp.mean(
        x * weighted, axis=-1, keepdims=True
    )
    dx_ref[...] = (dz + dmid_ref[...]).astype(bf16)


def back_in(S, x, gain, d3, diag, hot, extra, dmid, dense_w, tokens):
    n, width = x.shape
    return pl.pallas_call(
        functools.partial(back_in_kernel, S),
        in_specs=[vmem()] * 7 + [hbm()] + [anywhere()] * len(tokens),
        out_specs=[vmem()] * 3,
        out_shape=[
            jax.ShapeDtypeStruct((n, width), bf16),
            jax.ShapeDtypeStruct((width, LANES), bf16),
            TOKEN,
        ],
        scratch_shapes=[pltpu.VMEM((width, 3 * width), bf16), pltpu.SemaphoreType.DMA],
        compiler_params=params(60),
        cost_estimate=short(),
        name="back_in",
    )(x, gain, d3, diag, hot, extra, dmid, dense_w, *tokens)


def dense_kernel(S, N, with_small, core_ref, *refs):
    left, left_o, *refs = refs
    right, refs = refs[: 2 * N], refs[2 * N :]
    out, token = refs[-2:]
    give(token)
    core = core_ref[0]
    width = left.shape[1]
    half, many = width // (2 * S), width // PANEL
    for s in range(S):
        a, b = core_columns(left, core, s, half), core_columns(left_o, core, s, half)
        for j in range(N):
            total = (dot_tn(a, right[j][...]) + dot_tn(b, right[N + j][...])).astype(bf16)
            for p in range(many):
                rows = slice((j * many + p) * half, (j * many + p + 1) * half)
                out[s, rows, :] = total[:, p * PANEL : (p + 1) * PANEL]
        if with_small:
            low, high = slice(2 * s * half, (2 * s + 1) * half), slice((2 * s + 1) * half, (2 * s + 2) * half)
            total = [
                jnp.where(core == 0, r[low, :], r[high, :]).astype(f32) for r in refs[:2]
            ]
            rows = slice(N * many * half, (N * many + 1) * half)
            out[s, rows, :LANES] = (total[0] + total[1]).astype(bf16)
            out[s, rows, LANES:] = jnp.zeros((half, PANEL - LANES), bf16)


def dense_grads_of(S, core, left, left_o, right, right_o, small, tokens):
    n, width = left.shape
    if isinstance(right, list):
        N, arrays = len(right), right + right_o
        specs = [vmem()] * (2 * N)
    else:
        N, arrays = 3, [right] * 3 + [right_o] * 3
        specs = [pl.BlockSpec((None, n, width), lambda i, j=j: (j, 0, 0)) for j in range(3)] * 2
    panels = N * (width // PANEL) + (1 if small else 0)
    shape = (S, panels * width // (2 * S), PANEL)

    def whole(x):
        return pl.BlockSpec(x.shape, lambda i: (0,) * x.ndim)

    out, token = pl.pallas_call(
        functools.partial(dense_kernel, S, N, bool(small)),
        grid=(1,),
        in_specs=[smem(), whole(left), whole(left_o)]
        + ([whole(x) for x in arrays] if isinstance(right, list) else specs)
        + [whole(x) for x in small]
        + [anywhere()] * len(tokens),
        out_specs=[pl.BlockSpec(shape, lambda i: (0, 0, 0)), token_spec()],
        out_shape=[jax.ShapeDtypeStruct(shape, bf16), TOKEN],
        compiler_params=params(60),
        cost_estimate=short(),
        name="dense",
    )(core, left, left_o, *arrays, *small, *tokens)
    return out, [token]


def wave_kernel(shapes_in, shapes_out, *refs):
    place_ref = refs[0]
    line, core = place_ref[0], place_ref[1]
    inner = (line == 1) | (line == 2)
    get = dict(zip(shapes_in, refs[1:]))
    put = dict(zip(shapes_out, refs[len(refs) - len(shapes_out) :]))
    give(put["token"])

    def add(a, b):
        return (get[a][...].astype(f32) + get[b][...].astype(f32)).astype(bf16)

    if "mid" in put:
        put["mid"][...] = add("s0", "got_pair")
    if "core" in put:
        put["core"][...] = jnp.where(inner, get["pair"][...], get["got_pair"][...])
    new = None
    if "keep" in get:
        new = add("keep", "recv") if "recv" in get else get["keep"][...]
    full = add("mid", "got_mid") if "mid" in get else None
    if new is not None:
        put["s0"][...] = new
    if "pair" in put:
        if new is None or full is None:
            put["pair"][...] = full if new is None else new
        else:
            put["pair"][...] = jnp.where(inner, full, new)
    if "final" in put:
        a, b = get["core"][...].astype(f32), get["got_core"][...].astype(f32)
        half = a.shape[1]
        put["final"][:, :half] = jnp.where(core == 0, a, b)
        put["final"][:, half:] = jnp.where(core == 0, b, a)


class Sums:
    def __init__(self, size, place):
        self.size, self.place = size, place
        self.line = size // 2 == 4
        self.queues = [[], []]
        self.state = [{}, {}]
        self.ids = [{}, {}]
        self.turn = 0
        self.added = 0
        self.dense = {}
        self.final = None
        self.targets = {}
        self.last = []

    def add(self, keep, k, recv, j, name, expert):
        if self.line:
            self.queues[self.added % 2].append((keep, k, recv, j, name, expert))
            self.added += 1
            return
        mine = line_sum((keep[k].astype(f32) + recv[j].astype(f32)).astype(bf16), self.size)
        other = swap_core(mine, self.size)
        first = self.place[1] == 0
        whole = jnp.concatenate([jnp.where(first, mine, other), jnp.where(first, other, mine)], 1)
        if name not in self.targets:
            self.targets[name] = jnp.zeros((EXPERTS,) + whole.shape, f32)
        self.targets[name] = self.targets[name].at[expert].set(whole.astype(f32))

    def busy(self):
        return any(self.queues) or any(self.state) or self.final is not None

    def begin(self):
        items = [queue.pop(0) for queue in self.queues]
        rows, cols = items[0][0].shape[1:]
        steps = max(g for g in (1, 2, 4) if rows % (16 * g) == 0)

        def block(k):
            return pl.BlockSpec((None, rows // steps, cols), lambda r: (k, r, 0))

        def kernel(*refs):
            give(refs[-1])
            outs = refs[-3:-1]
            for i in range(2):
                total = refs[2 * i][...].astype(f32) + refs[2 * i + 1][...].astype(f32)
                outs[i][...] = total.astype(bf16)

        spec = pl.BlockSpec((rows // steps, cols), lambda r: (r, 0))
        *sums, token = pl.pallas_call(
            kernel,
            grid=(steps,),
            in_specs=[block(k) for item in items for k in (item[1], item[3])]
            + [anywhere()] * len(self.last),
            out_specs=[spec, spec, token_spec()],
            out_shape=[pltpu.HBM((rows, cols), bf16)] * 2 + [TOKEN],
            compiler_params=params(60),
            cost_estimate=short(),
            name="begin",
        )(*[pin(x) for item in items for x in (item[0], item[2])], *self.last)
        self.last = [token]
        for i, item in enumerate(items):
            self.state[i] = {"s0": sums[i], "pair": sums[i]}
            self.ids[i] = {"in": (item[4], item[5])}

    def step(self, more=()):
        self.last = self.last + list(more)
        stream = self.turn
        self.turn = 1 - stream
        queue, state, ids = self.queues[stream], self.state[stream], self.ids[stream]
        rep_axis = "rep"
        ins, outs = {}, []
        if "s0" in state or "pair" in state:
            pairs = line_perm([(0, 1), (1, 0), (2, 3), (3, 2)])
            ins["got_pair"] = lax.ppermute(state["pair"], rep_axis, pairs)
        if "mid" in state:
            ins["mid"] = state["mid"]
            ins["got_mid"] = lax.ppermute(state["mid"], rep_axis, line_perm([(1, 2), (2, 1)]))
        new_ids = {}
        if "in" in ids:
            ins["s0"] = state["s0"]
            outs.append("mid")
            new_ids["mid"] = ids["in"]
        if "out" in ids:
            ins["pair"] = state["pair"]
            outs.append("core")
        if "mid" in ids:
            new_ids["out"] = ids["mid"]
        if queue:
            keep, k, recv, j, name, expert = queue.pop(0)
            ins["keep"] = (keep, k)
            if recv is not None:
                ins["recv"] = (recv, j)
            outs.append("s0")
            new_ids["in"] = (name, expert)
        if "in" in new_ids or "out" in new_ids:
            outs.append("pair")
        if self.final is not None:
            value, (name, expert) = self.final
            ins["core"] = value
            ins["got_core"] = swap_core(value, self.size)
            outs.append("final")
        if not outs:
            self.state[stream] = {}
            return
        result = self.kernel(ins, outs, self.final[1] if self.final is not None else None)
        if self.final is not None:
            self.targets[self.final[1][0]] = result["final"]
        self.final = None
        if "core" in outs:
            if ids["out"][1] is None:
                self.dense[ids["out"][0]] = result["core"]
            else:
                self.final = (result["core"], ids["out"])
        self.last = [result["token"]]
        self.state[stream] = {key: result[key] for key in ("s0", "mid", "pair") if key in outs}
        self.ids[stream] = new_ids

    def kernel(self, ins, outs, final):
        arrays, specs = [], []
        rows, cols = next(
            (x[0].shape[1:] if isinstance(x, tuple) else x.shape) for x in ins.values()
        )
        steps = max(g for g in (1, 2, 4) if rows % (16 * g) == 0)
        spec = pl.BlockSpec((rows // steps, cols), lambda r: (r, 0))
        for x in ins.values():
            if isinstance(x, tuple):
                arrays.append(pin(x[0]))
                specs.append(
                    pl.BlockSpec((None, rows // steps, cols), lambda r, k=x[1]: (k, r, 0))
                )
            else:
                arrays.append(x)
                specs.append(spec)
        shape = pltpu.HBM((rows, cols), bf16)
        out_specs, out_shapes, extra, aliases = [], [], [], {}
        for i, key in enumerate(outs):
            if key == "final":
                name, expert = final
                out_specs.append(
                    pl.BlockSpec((None, rows // steps, 2 * cols), lambda r: (expert, r, 0))
                )
                out_shapes.append(pltpu.HBM((EXPERTS, rows, 2 * cols), f32))
                if name in self.targets:
                    extra.append(pin(self.targets[name]))
                    aliases[1 + len(arrays)] = i
            else:
                out_specs.append(spec)
                out_shapes.append(shape)
        values = pl.pallas_call(
            functools.partial(wave_kernel, tuple(ins), tuple(outs) + ("token",)),
            grid=(steps,),
            in_specs=[smem()] + specs + [anywhere()] * (len(extra) + len(self.last)),
            out_specs=out_specs + [token_spec()],
            out_shape=out_shapes + [TOKEN],
            input_output_aliases=aliases,
            compiler_params=params(60),
            cost_estimate=short(),
            name="wave",
        )(self.place, *arrays, *extra, *self.last)
        return dict(zip(tuple(outs) + ("token",), values))


def assemble_kernel(half, many, place_ref, *refs):
    mine, other, outs = refs[:2], refs[2:4], refs[4:]
    core = place_ref[1]

    def rows(parts, first):
        cut = parts[0].shape[0]
        if first + half <= cut:
            return parts[0][first : first + half, :]
        if first >= cut:
            return parts[1][first - cut : first - cut + half, :]
        return jnp.concatenate([parts[0][first:, :], parts[1][: first + half - cut, :]], axis=0)

    def put(out, column, p, width):
        a = rows(mine, p * half)[:, :width].astype(f32)
        b = rows(other, p * half)[:, :width].astype(f32)
        out[:half, column : column + width] = jnp.where(core == 0, a, b)
        out[half:, column : column + width] = jnp.where(core == 0, b, a)

    for j in range(4):
        for q in range(many):
            put(outs[j], q * PANEL, j * many + q + (1 if j == 3 else 0), PANEL)
    small = outs[6]
    put(small, 0, 3 * many, LANES)
    outs[4][...] = small[:, 2 : 2 + EXPERTS]
    outs[5][...] = small[: outs[5].shape[0], 8 : 8 + HEADS]


def assemble(place, half, width, mine, other):
    shapes = [jax.ShapeDtypeStruct((2 * half, width), f32)] * 4
    shapes.append(jax.ShapeDtypeStruct((2 * half, EXPERTS), f32))
    shapes.append(jax.ShapeDtypeStruct((BUCKETS * 2 * half // width, HEADS), f32))
    shapes.append(jax.ShapeDtypeStruct((2 * half, LANES), f32))
    return pl.pallas_call(
        functools.partial(assemble_kernel, half, width // PANEL),
        in_specs=[smem()] + [vmem()] * 4,
        out_specs=[vmem()] * 7,
        out_shape=shapes,
        compiler_params=params(60),
        cost_estimate=short(),
        name="assemble",
    )(place, *mine, *other)


def swap_core(x, size):
    return lax.ppermute(x, "rep", [(i, i ^ 1) for i in range(size)])


def swap_shard(x, size, mask):
    return lax.ppermute(x, "shard", [(i, i ^ mask) for i in range(size)])


def line_perm(pairs):
    return [(2 * a + c, 2 * b + c) for a, b in pairs for c in range(2)]


def after(x, *others):
    return lax.optimization_barrier((x,) + others)[0]


def relay_gather(top, bottom, S):
    if S != 4:
        x = jnp.concatenate([top, bottom], axis=0)
        return [[x]] + [[swap_shard(x, S, m)] for m in range(1, S)]
    one_top, two_bottom = swap_shard(top, S, 1), swap_shard(bottom, S, 2)
    one = [one_top, swap_shard(bottom, S, 1)]
    two = [swap_shard(top, S, 2), two_bottom]
    return [[top, bottom], one, two, [swap_shard(one_top, S, 2), swap_shard(two_bottom, S, 1)]]


def relay_whole(x, S):
    if S != 4:
        return [[x]] + [[swap_shard(x, S, m)] for m in range(1, S)]
    cut = x.shape[0] // 2
    one, two = swap_shard(x, S, 1), swap_shard(x, S, 2)
    return [[x], [one], [two], [swap_shard(one[:cut], S, 2), swap_shard(two[cut:], S, 1)]]


def line_sum(x, size):
    n = size // 2
    h = n // 2
    line = lax.axis_index("rep") // 2
    for k in range(h - 1):
        x = x + lax.ppermute(x, "rep", line_perm([(k, k + 1), (n - 1 - k, n - 2 - k)]))
    x = x + lax.ppermute(x, "rep", line_perm([(h - 1, h), (h, h - 1)]))
    for k in reversed(range(h - 1)):
        got = lax.ppermute(x, "rep", line_perm([(k + 1, k), (n - 2 - k, n - 1 - k)]))
        x = jnp.where((line == k) | (line == n - 1 - k), got, x)
    return x


def deal_out(x):
    return lax.all_to_all(x, "shard", 0, 0, tiled=True)


def bucket_of(distance):
    bucket = jnp.minimum(distance, 16)
    for border in bucket_edges:
        bucket = bucket + (distance >= border).astype(jnp.int32)
    return bucket


def slot_positions(routes, order, lengths):
    n = order.shape[1]
    valid = jnp.arange(n, dtype=jnp.int32)[None, :] < lengths[:, None]
    experts = jnp.arange(EXPERTS, dtype=jnp.int32)
    hits = (routes[:, :, :, None] == experts) & valid[:, :, None, None]
    hits = hits.reshape(routes.shape[0], n, 2 * EXPERTS)
    before = (order[:, None, :] < order[:, :, None]).astype(bf16)
    count = jnp.einsum("stk,sut->sku", hits.astype(bf16), before, preferred_element_type=f32)
    total = jnp.sum(hits[:, :, :EXPERTS].astype(f32), axis=1)
    hits = jnp.swapaxes(hits, 1, 2)
    first, second = count[:, :EXPERTS], count[:, EXPERTS:] + total[:, :, None]
    slot = jnp.where(
        hits[:, :EXPERTS], first, jnp.where(hits[:, EXPERTS:], second, float(2 * CAP + n))
    )
    return jnp.where(slot < CAP, slot, -1.0).astype(jnp.int32)


def shards(
    R,
    S,
    tokens,
    cotangent,
    lengths,
    sequence_deal,
    routes,
    fill_order,
    norm_attn,
    w_query,
    w_key,
    w_value,
    w_out,
    rel_bias,
    norm_ffn,
    w_router,
    w_gate,
    w_up,
    w_down,
):
    me = lax.axis_index("shard")
    rep = lax.axis_index("rep")
    core = rep % 2
    line = rep // 2
    x_low, ct_low = tokens[0], cotangent[0]
    n, width = x_low.shape
    part = width // S
    half = part // 2
    group = jnp.arange(S, dtype=jnp.int32)

    dense = (w_query, w_key, w_value, w_out)
    cut = half // 2

    def rows_for_core(first):
        return jnp.where(
            core == 0,
            jnp.concatenate([w[first : first + cut] for w in dense], axis=1),
            jnp.concatenate([w[half + first : half + first + cut] for w in dense], axis=1),
        )

    stack = rows_for_core(0)
    blocks = relay_gather(stack, rows_for_core(cut), S)
    count = len(blocks[-1])
    pieces, places, late = [], [], []
    for m in range(1, S):
        place = 2 * count * (me ^ m)
        each = count // len(blocks[m])
        pieces += blocks[m]
        places += [place + count * core + j * each for j in range(len(blocks[m]))]
        for j, block in enumerate(blocks[m]):
            if m == S - 1:
                late.append(len(pieces))
            pieces.append(block if m == S - 1 else swap_core(block, R))
            places.append(place + count * (1 - core) + j * each)
    offsets = jnp.stack(places + [2 * count * me]).astype(jnp.int32)
    ct_all = relay_whole(after(ct_low, *blocks[-1]), S)

    bias_flat = jnp.pad(rel_bias.reshape(-1), (0, part - rel_bias.size))
    small = jnp.concatenate(
        [norm_attn[:, None], norm_ffn[:, None], w_router, bias_flat[:, None]], axis=1
    )
    small = jnp.pad(small, ((0, n - part), (0, 0)))
    plan = jnp.concatenate([routes[0], fill_order[0][:, None]], axis=1).astype(bf16)
    small = jnp.concatenate([small, plan], axis=1)
    small = after(small, stack)
    small_all = deal_out(jnp.broadcast_to(small[None], (S,) + small.shape))
    plan_all = small_all[:, :, 3 + EXPERTS :]
    small_all = small_all[:, :part]
    gain_one = small_all[:, :, 0].reshape(-1).astype(f32)
    gain_two = small_all[:, :, 1].reshape(-1).astype(f32)
    router_w = small_all[:, :, 2 : 2 + EXPERTS].reshape(width, EXPERTS)
    bias_table = small_all[:, : rel_bias.size, 2 + EXPERTS].reshape(BUCKETS, HEADS)

    length = lax.dynamic_slice_in_dim(lengths[0], me, 1, 0)

    turned = jnp.arange(n, dtype=jnp.int32)
    hot = (bucket_of((n - turned) % n)[None, :] == jnp.arange(BUCKETS)[:, None]).astype(bf16)
    base = dot_tn(bias_table, hot)
    for i in late:
        pieces[i] = swap_core(after(pieces[i], base, gain_one, gain_two), R)

    normed_low, qkv, context, middle, ffn_in, dense_w, bias = attn_fwd(
        offsets, length, x_low, gain_one[None], gain_two[None], base, dense, pieces
    )

    plan_all = after(plan_all, ffn_in).astype(jnp.int32)
    deal = sequence_deal[0]
    row_of = jnp.sum(group[:, None] * (deal[:, None] == group[None, :]).astype(jnp.int32), axis=0)
    homes = me ^ group
    plans = jnp.take(plan_all, jnp.take(row_of, homes), axis=0)
    pos = slot_positions(plans[:, :, :2], plans[:, :, 2], jnp.take(lengths[0], homes))

    h2_all = relay_whole(ffn_in, S)
    router_pad = jnp.pad(router_w, ((0, 0), (0, LANES - EXPERTS)))
    core_one = core.reshape(1).astype(jnp.int32)
    place = jnp.stack([line, core]).astype(jnp.int32)
    me_one = me.reshape(1).astype(jnp.int32)
    where = jnp.stack([me, core]).astype(jnp.int32)
    weights = [pin(w) for w in (jnp.swapaxes(w_gate, 1, 2), jnp.swapaxes(w_up, 1, 2), w_down)]
    sums = Sums(R, place)
    h1_other, context_other = swap_core(normed_low, R), swap_core(context, R)
    chain, aux = (), router_pad
    for experts, groups in (((0, 1), (2, 2, 2)), ((2, 3), (2, 2, 2))):
        first = sums.last if experts[0] == 0 else sums.last + [h1_other, context_other]
        got = ffn(experts, groups, where, pos, aux, h2_all, ct_all, weights, chain, first)
        M = 1 + len(groups)
        keep, sends, chain = got[0], got[1:M], got[M : M + 2]
        sums.last = [got[M + 2]]
        if experts[0] == 0:
            aux = got[-1]
        where_to = [(g, k) for g, size in enumerate(groups) for k in range(size)]
        recvs = [swap_core(x, R) for x in sends]
        for i, e in enumerate(experts):
            for j, name in enumerate(("down", "gate", "up")):
                g, k = where_to[3 * i + j]
                sums.add(keep, 3 * i + j, recvs[g], k, name, e)
        if experts[0] == 0 and sums.line:
            sums.begin()

    def run(steps, more=()):
        for _ in range(steps):
            if sums.line and sums.busy():
                sums.step(more)

    flat = jnp.arange(EXPERTS, dtype=jnp.int32) * CAP
    pos_col = jnp.swapaxes(jnp.where(pos < 0, -1, pos + flat[None, :, None]), 1, 2)
    pos_col = jnp.pad(pos_col, ((0, 0), (0, 0), (0, LANES - EXPERTS)))
    run(2)
    d_parts, sums.last = combine(me_one, pos_col, chain[1], sums.last)
    d_parts = deal_out(d_parts)
    run(1)
    run(1, recvs)

    dmid, dm, dc, extra, token = back_mid(
        S, middle, ct_low, gain_two[None], ffn_in, router_pad, dense_w, d_parts, sums.last
    )
    sums.last = [token]
    run(0)
    d3, diag, token = attn_bwd(qkv, bias, dc, sums.last)
    sums.last = [token]
    run(2)
    out_grads, sums.last = dense_grads_of(
        S, core_one, context, context_other, [dm], [swap_core(dm, R)], [], sums.last
    )
    out_grads = deal_out(out_grads)
    run(0)
    grad_x, extra, token = back_in(
        S, x_low, gain_one[None], d3, diag.reshape(HEADS, n), hot, extra, dmid, dense_w, sums.last
    )
    sums.last = [token]
    run(1)
    in_grads, sums.last = dense_grads_of(
        S, core_one, normed_low, h1_other, d3, swap_core(d3, R), [extra, swap_core(extra, R)], sums.last
    )
    in_grads = deal_out(in_grads)
    run(3)
    out_parts, sums.last = combine(me_one, pos_col, chain[0], sums.last)
    out_parts = deal_out(out_parts)
    run(2)

    owned = [jnp.sum(x.astype(f32), axis=0).astype(bf16) for x in (in_grads, out_grads)]
    owned = jnp.concatenate(owned, axis=0)
    rows, cut = owned.shape[0], weights[0].shape[1]
    if sums.line and rows <= 2 * cut:
        owned = jnp.pad(owned, ((0, 2 * cut - rows), (0, 0)))[None]
        sums.add(owned[:, :cut], 0, None, 0, "top", None)
        sums.add(owned[:, cut:], 0, None, 0, "bottom", None)
        run(1)
    else:
        owned = line_sum(owned, R)
        sums.dense = {"top": owned[: rows // 2], "bottom": owned[rows // 2 :]}
    run(4)
    result = (middle + jnp.sum(out_parts.astype(f32), axis=0)).astype(bf16)
    run(1, [result])
    run(100)
    mine = [sums.dense["top"], sums.dense["bottom"]]
    *dense_grads, grad_router_w, grad_table, small = assemble(place, half, width, mine, [swap_core(x, R) for x in mine])
    return (
        result[None],
        grad_x[None],
        small[:, 0],
        *dense_grads,
        grad_table,
        small[:, 1],
        grad_router_w,
        jnp.swapaxes(sums.targets["gate"], 1, 2),
        jnp.swapaxes(sums.targets["up"], 1, 2),
        sums.targets["down"],
    )


def solution(mesh):
    R, S = mesh.shape["rep"], mesh.shape["shard"]
    rows = P(("rep", "shard"), None, None)
    mat = P("shard", None)
    return jax.shard_map(
        functools.partial(shards, R, S),
        mesh=mesh,
        in_specs=(rows, rows, P("rep", None), P("rep", None), rows, P(("rep", "shard"), None))
        + (P("shard"), mat, mat, mat, mat, mat, P("shard"), mat)
        + (P(None, None, "shard"), P(None, None, "shard"), P(None, "shard", None)),
        out_specs=(rows, rows, P("shard"), mat, mat, mat, mat, mat, P("shard"), mat)
        + (P(None, None, "shard"), P(None, None, "shard"), P(None, "shard", None)),
        check_vma=False,
    )
```
